32 devices in a mesh: dp: 4 (over y, x), fsdp: 8 (over z, core).
Axes of the slice: x: 2, y: 2, z: 4, core: 2. Of those that a mesh axis runs over, the one named last changes fastest.
Arguments:
- tokens: bfloat16 [32, 128, 2048], P(('dp', 'fsdp')), may hold values from -6 to 6
- cotangent: bfloat16 [32, 128, 2048], P(('dp', 'fsdp')), may hold values from -6 to 6
- lengths: int32 [32, 4], P(('dp', 'fsdp')), may hold values from 0 to 128, as said below
- prefix: int32 [32, 4], P(('dp', 'fsdp')), may hold values from 0 to 128, as said below
- qkv_weight: bfloat16 [2048, 6144], P(('dp', 'fsdp')), may hold values from -0.125 to 0.125
- dense_weight: bfloat16 [2048, 2048], P(('dp', 'fsdp')), may hold values from -2 to 2
- ffin_weight: bfloat16 [2048, 10922], P(('dp', 'fsdp')), may hold values from -0.125 to 0.125
- ffout_weight: bfloat16 [2048, 5461], P(('dp', 'fsdp')), may hold values from -0.4375 to 0.4375
- biases: bfloat16 [2048, 7], P(('dp', 'fsdp')), may hold values from -3 to 3
- norm_gains: bfloat16 [2048, 2], P(('dp', 'fsdp')), may hold values from 0.099609375 to 1.8984375
Outputs:
- output: bfloat16 [32, 128, 2048], P(('dp', 'fsdp'))
- grad_tokens: float32 [32, 128, 2048], P(('dp', 'fsdp'))
- grad_qkv: float32 [2048, 6144], P(('dp', 'fsdp'))
- grad_dense: float32 [2048, 2048], P(('dp', 'fsdp'))
- grad_ffin: float32 [2048, 10922], P(('dp', 'fsdp'))
- grad_ffout: float32 [2048, 5461], P(('dp', 'fsdp'))
- grad_biases: float32 [2048, 7], P(('dp', 'fsdp'))
- grad_gains: float32 [2048, 2], P(('dp', 'fsdp'))
The draws below stay inside these ranges and needn't reach their ends.
Inputs may be any that keep to these rules, and one draw needn't show every extreme that they name: Row s holds up to 4 proteins packed from position 0: each length is 0 or from 50 to 128, zeros come last, a row's lengths sum to at most 128, and some row holds one protein of length 128. prefix[s,k] is at most lengths[s,k]; it is 0 for an empty slot and equals lengths[s,k] for a protein of 128 residues.
All inputs are finite; a program needn't handle non-finite values.
Results may differ from the reference program's by a relative error of at most 0.014.
Values may be sent and summed in bfloat16 or wider, within the bound.
A program may use at most 384 MiB of HBM per device.

```python
import math
import jax
import jax.numpy as jnp
from jax import lax

D = 2048
HEADS = 16
HEAD_DIM = 128
FF = 5461
LAYERS = 24
SEQ = 128
DOCS = 4
MINLEN = 50
NSEQ = 32


def packed_sizes(key):
    raw_draw = jax.random.randint(jax.random.fold_in(key, 11), (NSEQ, DOCS), 0, 100)
    cubed = raw_draw * raw_draw * raw_draw
    doc_sizes = MINLEN + cubed * (SEQ - MINLEN) // 970299
    doc_ends = jnp.cumsum(doc_sizes, axis=1)
    fitted = jnp.where(doc_ends <= SEQ, doc_sizes, 0)
    chosen = jax.random.randint(jax.random.fold_in(key, 12), (), 0, NSEQ)
    single_doc = jnp.where(jnp.arange(DOCS) == 0, SEQ, 0)
    row_index = jnp.arange(NSEQ)
    return jnp.where((row_index == chosen)[:, None], single_doc[None, :], fitted).astype(jnp.int32)


def draw_lengths(key, part):
    return packed_sizes(key)


def draw_prefix(key, part):
    doc_sizes = packed_sizes(key)
    key = jax.random.fold_in(key, 5)
    prefix_share = jax.random.randint(key, (NSEQ, DOCS), 10, 91)
    shared = doc_sizes * prefix_share // 100
    return jnp.where(doc_sizes == SEQ, SEQ, shared).astype(jnp.int32)


def levels(stream_key, dims, cuts, least, high):
    level = 1.0
    for axis_at, blocks in cuts:
        steps = jax.random.uniform(jax.random.fold_in(jax.random.fold_in(stream_key, 6), axis_at), (blocks,), jnp.float32, least / len(cuts), high / len(cuts))
        level = level * jnp.repeat(jnp.exp(steps), dims[axis_at] // blocks).reshape((-1,) + (1,) * (len(dims) - 1 - axis_at))
    return level


def gaussian(stream_key, dims, width, bound, split=(), kind=jnp.bfloat16):
    drawn = width * jax.random.normal(stream_key, dims, jnp.float32)
    if split:
        drawn = drawn * levels(stream_key, dims, split, -0.22, 0.18)
    return jnp.clip(drawn, -bound, bound).astype(kind)


def setup_inputs(seed: int = 0) -> dict:
    splits = jax.random.split(jax.random.key(seed), 11)
    tokens = gaussian(splits[0], (NSEQ, SEQ, D), 1.0, 6.0, ((0, 32),))
    cotangent = gaussian(splits[1], (NSEQ, SEQ, D), 1.0, 6.0, ((0, 32),))
    lengths = draw_lengths(jax.random.fold_in(splits[10], 71), 0)
    prefix = draw_prefix(jax.random.fold_in(splits[10], 71), 0)
    qkv_weight = gaussian(splits[4], (D, 3 * D), D ** -0.5, 0.125, ((0, 32),))
    dense_weight = gaussian(splits[5], (D, D), (max(D // 256, 1)) ** -0.5, 2.0, ((0, 32),))
    ffin_weight = gaussian(splits[6], (D, 2 * FF), D ** -0.5, 0.125, ((0, 32),))
    ffout_weight = gaussian(splits[7], (D, FF), (max(FF // 32, 1)) ** -0.5, 0.4375, ((0, 32),))
    biases = gaussian(splits[8], (D, 7), 0.5, 3.0, ((0, 32),))
    norm_gains = jnp.clip(1.0 + 0.18 * jax.random.normal(splits[9], (D, 2), jnp.float32), 0.099609375, 1.8984375).astype(jnp.bfloat16)
    return dict(tokens=tokens, cotangent=cotangent, lengths=lengths, prefix=prefix, qkv_weight=qkv_weight, dense_weight=dense_weight, ffin_weight=ffin_weight, ffout_weight=ffout_weight, biases=biases, norm_gains=norm_gains)


MAXIMAL_ACCURACY = lax.Precision.HIGHEST
MASKED_SCORE = -1e+30
EPSILON = 1e-05
ROPE_BASE = 10000.0

@jax.custom_vjp
def lowered_input(v):
    return lax.optimization_barrier(v.astype(jnp.bfloat16)).astype(jnp.float32)

@jax.custom_vjp
def lowered_gradient(v):
    return v

def low_keep(v):
    return (lowered_input(v), None)

def low_pass(kept, grad):
    return (grad,)

def back_keep(v):
    return (v, None)

def back_low(kept, grad):
    return (lowered_input(grad),)
lowered_input.defvjp(low_keep, low_pass)
lowered_gradient.defvjp(back_keep, back_low)

def token_layout(lengths, prefix, seq_len):
    doc_count = lengths.shape[1]
    doc_ends = jnp.cumsum(lengths, axis=1)
    doc_starts = doc_ends - lengths
    positions = jnp.arange(seq_len, dtype=jnp.int32)
    doc_index = lax.optimization_barrier(jnp.sum((positions[None, :, None] >= doc_ends[:, None, :]).astype(jnp.int32), axis=2))
    member = doc_index[:, :, None] == jnp.arange(doc_count, dtype=jnp.int32)[None, None, :]
    start_at = lax.optimization_barrier(jnp.sum(jnp.where(member, doc_starts[:, None, :], 0), axis=2))
    prefix_at = lax.optimization_barrier(jnp.sum(jnp.where(member, prefix[:, None, :], 0), axis=2))
    valid_pos = positions[None, :] < doc_ends[:, -1:]
    local_pos = jnp.where(valid_pos, positions[None, :] - start_at, 0)
    same_doc = doc_index[:, :, None] == doc_index[:, None, :]
    earlier = (positions[:, None] >= positions[None, :])[None]
    in_prefix = local_pos[:, None, :] < prefix_at[:, :, None]
    inside = valid_pos[:, :, None] & valid_pos[:, None, :] & same_doc & (in_prefix | earlier)
    itself = jnp.logical_not(valid_pos)[:, :, None] & (positions[:, None] == positions[None, :])[None]
    return (inside | itself, local_pos, valid_pos)

def rotary_tables(local_pos, head_dim):
    half_dim = head_dim // 2
    inverse = ROPE_BASE ** (-jnp.arange(half_dim, dtype=jnp.float32) * 2.0 / head_dim)
    angles = local_pos.astype(jnp.float32)[..., None] * inverse
    return (jnp.cos(angles)[:, :, None, :], jnp.sin(angles)[:, :, None, :])

def rotate(values, cosine_table, sine_table):
    half_dim = values.shape[-1] // 2
    first_half = values[..., :half_dim]
    second_half = values[..., half_dim:]
    return jnp.concatenate([first_half * cosine_table - second_half * sine_table, second_half * cosine_table + first_half * sine_table], axis=-1)

def layer_norm(token_matrix, scale_vec, shift_vec):
    centered = token_matrix - lax.optimization_barrier(jnp.mean(token_matrix, axis=-1, keepdims=True))
    variance = lax.optimization_barrier(jnp.mean(centered * centered, axis=-1, keepdims=True))
    return centered * lax.rsqrt(variance + EPSILON) * scale_vec + shift_vec

def layer_block(token_matrix, query_key_value_weight, dense_matrix, input_weight, output_weight, bias_stacked_layers, gain_all, attention, cosine_table, sine_table):
    sequences, seq_len, model_width = token_matrix.shape
    score_scale = HEAD_DIM ** (-0.5)
    residual_scale = (2.0 * LAYERS) ** 0.5
    query_key_value_rows = lowered_gradient(jnp.einsum('png,gx->pnx', token_matrix, query_key_value_weight, precision=MAXIMAL_ACCURACY) + bias_stacked_layers[:, 0:3].T.reshape(-1))
    query_part = query_key_value_rows[..., :model_width].reshape(sequences, seq_len, HEADS, HEAD_DIM)
    key_part = query_key_value_rows[..., model_width:2 * model_width].reshape(sequences, seq_len, HEADS, HEAD_DIM)
    value_part = query_key_value_rows[..., 2 * model_width:].reshape(sequences, seq_len, HEADS, HEAD_DIM)
    q_low = lowered_input(rotate(query_part, cosine_table, sine_table))
    k_low = lowered_input(rotate(key_part, cosine_table, sine_table))
    v_low = lowered_input(value_part)
    scores = lowered_gradient(score_scale * jnp.einsum('sqhe,skhe->shqk', q_low, k_low, precision=MAXIMAL_ACCURACY))
    masked = jnp.where(attention[:, None], scores, MASKED_SCORE)
    row_max = lax.optimization_barrier(jnp.max(masked, axis=-1, keepdims=True))
    exponent = jnp.exp(masked - row_max)
    attn_probs = exponent / lax.optimization_barrier(jnp.sum(exponent, axis=-1, keepdims=True))
    context_vectors = lowered_input(lowered_gradient(jnp.einsum('shqk,skhe->sqhe', lowered_input(attn_probs), v_low, precision=MAXIMAL_ACCURACY)))
    context_vectors = context_vectors.reshape(sequences, seq_len, model_width)
    attention_output = lowered_gradient(jnp.einsum('png,gx->pnx', context_vectors, dense_matrix, precision=MAXIMAL_ACCURACY) + bias_stacked_layers[:, 3])
    first_normalized = layer_norm(residual_scale * token_matrix + attention_output, gain_all[:, 0], bias_stacked_layers[:, 4])
    inner_projection = lowered_gradient(jnp.einsum('png,gx->pnx', lowered_input(first_normalized), input_weight, precision=MAXIMAL_ACCURACY))
    hidden_units = output_weight.shape[1]
    activation_result = lowered_input(jax.nn.gelu(inner_projection[..., :hidden_units], approximate=False) * inner_projection[..., hidden_units:])
    residual_branch = lowered_gradient(jnp.einsum('vpz,rz->vpr', activation_result, output_weight, precision=MAXIMAL_ACCURACY) + bias_stacked_layers[:, 5])
    return layer_norm(residual_scale * first_normalized + residual_branch, gain_all[:, 1], bias_stacked_layers[:, 6])

def reference(tokens, cotangent, lengths, prefix, qkv_weight, dense_weight, ffin_weight, ffout_weight, biases, norm_gains):
    group_size = math.gcd(16, NSEQ)
    group_count = NSEQ // group_size
    params = (qkv_weight.astype(jnp.float32), dense_weight.astype(jnp.float32), ffin_weight.astype(jnp.float32), ffout_weight.astype(jnp.float32), biases.astype(jnp.float32), norm_gains.astype(jnp.float32))

    def one_group(grad_carry, pieces):
        token_matrix, cot_rows, group_lengths, group_prefix = pieces
        attention, local_pos, valid_pos = token_layout(group_lengths, group_prefix, SEQ)
        cosine_table, sine_table = rotary_tables(local_pos, HEAD_DIM)

        def apply_layer(rows_in, query_key_value_weight, dense_matrix, input_weight, output_weight, bias_stacked_layers, gain_all):
            return layer_block(rows_in, query_key_value_weight, dense_matrix, input_weight, output_weight, bias_stacked_layers, gain_all, attention, cosine_table, sine_table)
        result, back_fn = jax.vjp(apply_layer, token_matrix.astype(jnp.float32), params[0], params[1], params[2], params[3], params[4], params[5])
        grads = back_fn(cot_rows.astype(jnp.float32) * valid_pos[..., None].astype(jnp.float32))
        grad_carry = jax.tree.map(jnp.add, grad_carry, tuple(grads[1:]))
        return (grad_carry, (result.astype(jnp.bfloat16), grads[0]))
    zeros_init = tuple((jnp.zeros(matrix.shape, jnp.float32) for matrix in params))
    pieces_all = (tokens.reshape(group_count, group_size, SEQ, D), cotangent.reshape(group_count, group_size, SEQ, D), lengths.reshape(group_count, group_size, DOCS).astype(jnp.int32), prefix.reshape(group_count, group_size, DOCS).astype(jnp.int32))
    final, stacked = lax.scan(one_group, zeros_init, pieces_all)
    outputs, grad_rows = stacked
    return (outputs.reshape(NSEQ, SEQ, D), grad_rows.reshape(NSEQ, SEQ, D), final[0], final[1], final[2], final[3], final[4], final[5])
```

```python
import functools

import jax
import jax.numpy as jnp
from jax import lax
from jax.experimental import pallas as pl
from jax.experimental.pallas import tpu as pltpu
from jax.sharding import Mesh
from jax.sharding import PartitionSpec as P

HEADS = 16
LAYERS = 24
MASKED_SCORE = -1e30
EPSILON = 1e-05
ROPE_BASE = 10000.0

AXES = ("a", "b", "e", "f", "c")
TENSOR = ("b", "f", "c")
GROUP = 8
DEVICE_MESH = pl.DeviceIdType.MESH
BF16 = jnp.bfloat16
F32 = jnp.float32


def token_layout(lengths, prefix, seq_len):
    doc_count = lengths.shape[1]
    doc_ends = jnp.cumsum(lengths, axis=1)
    doc_starts = doc_ends - lengths
    positions = jnp.arange(seq_len, dtype=jnp.int32)
    doc_index = jnp.sum(
        (positions[None, :, None] >= doc_ends[:, None, :]).astype(jnp.int32), axis=2
    )
    member = doc_index[:, :, None] == jnp.arange(doc_count, dtype=jnp.int32)[None, None, :]
    start_at = jnp.sum(jnp.where(member, doc_starts[:, None, :], 0), axis=2)
    prefix_at = jnp.sum(jnp.where(member, prefix[:, None, :], 0), axis=2)
    valid_pos = positions[None, :] < doc_ends[:, -1:]
    local_pos = jnp.where(valid_pos, positions[None, :] - start_at, 0)
    same_doc = doc_index[:, :, None] == doc_index[:, None, :]
    earlier = (positions[:, None] >= positions[None, :])[None]
    in_prefix = local_pos[:, None, :] < prefix_at[:, :, None]
    inside = valid_pos[:, :, None] & valid_pos[:, None, :] & same_doc & (in_prefix | earlier)
    itself = (
        jnp.logical_not(valid_pos)[:, :, None] & (positions[:, None] == positions[None, :])[None]
    )
    return (inside | itself, local_pos, valid_pos)


def rotary_tables(local_pos, head_dim):
    half_dim = head_dim // 2
    inverse = ROPE_BASE ** (-jnp.arange(half_dim, dtype=jnp.float32) * 2.0 / head_dim)
    angles = local_pos.astype(jnp.float32)[..., None] * inverse
    return (jnp.cos(angles)[:, :, None, :], jnp.sin(angles)[:, :, None, :])


def rotate(values, cosine_table, sine_table):
    half_dim = values.shape[-1] // 2
    first_half = values[..., :half_dim]
    second_half = values[..., half_dim:]
    return jnp.concatenate(
        [
            first_half * cosine_table - second_half * sine_table,
            second_half * cosine_table + first_half * sine_table,
        ],
        axis=-1,
    )


def layer_norm(token_matrix, scale_vec, shift_vec):
    centered = token_matrix - jnp.mean(token_matrix, axis=-1, keepdims=True)
    variance = jnp.mean(centered * centered, axis=-1, keepdims=True)
    return centered * lax.rsqrt(variance + EPSILON) * scale_vec + shift_vec


def contract_rows(left_rows, right_rows):
    return lax.dot_general(
        left_rows, right_rows, (((0,), (0,)), ((), ())), preferred_element_type=F32
    )


def times_transposed(left_rows, weight_rows):
    return lax.dot_general(
        left_rows, weight_rows, (((1,), (1,)), ((), ())), preferred_element_type=F32
    )


def neighbours():
    b, f, c = (lax.axis_index(axis) for axis in TENSOR)
    slot = lambda bb, ff, cc: (bb * 2 + ff) * 2 + cc
    return b, f, c, slot


def greet(b, f, c):
    barrier = pltpu.get_barrier_semaphore()
    for target in ({"b": 1 - b}, {"f": 1 - f}, {"c": 1 - c}):
        pl.semaphore_signal(barrier, inc=1, device_id=target, device_id_type=DEVICE_MESH)
    pl.semaphore_wait(barrier, 3)


def gather_kernel(x_ref, o_ref, local_sem, send_sem, recv_sem):
    b, f, c, slot = neighbours()
    half = x_ref.shape[0] // 2
    low, high = pl.ds(0, half), pl.ds(half, half)
    me, nb, nf, dg = slot(b, f, c), slot(1 - b, f, c), slot(b, 1 - f, c), slot(1 - b, 1 - f, c)
    to_b, to_f, to_c = {"b": 1 - b}, {"f": 1 - f}, {"c": 1 - c}

    def copy(number, source, target, device):
        return pltpu.make_async_remote_copy(
            src_ref=source,
            dst_ref=target,
            send_sem=send_sem.at[number],
            recv_sem=recv_sem.at[number],
            device_id=device,
            device_id_type=DEVICE_MESH,
        )

    mine = pltpu.make_async_copy(x_ref, o_ref.at[me], local_sem)
    mine.start()
    greet(b, f, c)
    own = [
        copy(0, x_ref.at[low], o_ref.at[me, low], to_b),
        copy(1, x_ref.at[high], o_ref.at[me, high], to_f),
        copy(2, x_ref.at[high], o_ref.at[me, high], to_b),
        copy(3, x_ref.at[low], o_ref.at[me, low], to_f),
        copy(4, x_ref, o_ref.at[me], to_c),
    ]
    for one in own:
        one.start()
    own[0].wait_recv()
    relay_f = copy(5, o_ref.at[nb, low], o_ref.at[nb, low], to_f)
    relay_f.start()
    own[1].wait_recv()
    relay_b = copy(6, o_ref.at[nf, high], o_ref.at[nf, high], to_b)
    relay_b.start()
    own[2].wait_recv()
    over_b = copy(7, o_ref.at[nb], o_ref.at[nb], to_c)
    over_b.start()
    own[3].wait_recv()
    over_f = copy(8, o_ref.at[nf], o_ref.at[nf], to_c)
    over_f.start()
    relay_f.wait_recv()
    relay_b.wait_recv()
    over_d = copy(9, o_ref.at[dg], o_ref.at[dg], to_c)
    over_d.start()
    own[4].wait_recv()
    for one in (over_b, over_f, over_d):
        one.wait_recv()
    for one in own + [relay_f, relay_b, over_b, over_f, over_d]:
        one.wait_send()
    mine.wait()


def group_gather(x, collective_id):
    rows, width = x.shape
    out = pl.pallas_call(
        gather_kernel,
        out_shape=jax.ShapeDtypeStruct((GROUP, rows, width), x.dtype),
        in_specs=[pl.BlockSpec(memory_space=pl.ANY)],
        out_specs=pl.BlockSpec(memory_space=pl.ANY),
        scratch_shapes=[
            pltpu.SemaphoreType.DMA(()),
            pltpu.SemaphoreType.DMA((10,)),
            pltpu.SemaphoreType.DMA((10,)),
        ],
        compiler_params=pltpu.CompilerParams(collective_id=collective_id, has_side_effects=True),
        cost_estimate=pl.CostEstimate(
            flops=0, bytes_accessed=20 * GROUP * rows * width, transcendentals=0
        ),
    )(x)
    return out.reshape(GROUP * rows, width)


def scatter_kernel(
    p_ref, o_ref, own_ref, core_ref, out_ref, relay_ref, land_ref, local_sem, send_sem, recv_sem
):
    b, f, c, slot = neighbours()
    rows = own_ref.shape[1]
    half = rows // 2
    low, high = pl.ds(0, half), pl.ds(half, half)
    to_b, to_f, to_c = {"b": 1 - b}, {"f": 1 - f}, {"c": 1 - c}
    places = [(1 - b, 1 - f), (1 - b, f), (b, 1 - f), (b, f)]

    def copy(number, source, target, device):
        return pltpu.make_async_remote_copy(
            src_ref=source,
            dst_ref=target,
            send_sem=send_sem.at[number],
            recv_sem=recv_sem.at[number],
            device_id=device,
            device_id_type=DEVICE_MESH,
        )

    local = [
        pltpu.make_async_copy(p_ref.at[slot(*place, c)], own_ref.at[k], local_sem.at[k])
        for k, place in enumerate(places)
    ]
    for one in local:
        one.start()
    greet(b, f, c)
    core = [
        copy(k, p_ref.at[slot(*place, 1 - c)], core_ref.at[k], to_c)
        for k, place in enumerate(places)
    ]
    for one in core:
        one.start()
    step = 16

    def add(target, at, count, terms):
        @pl.loop(0, count // step)
        def _(i):
            window = pl.ds(pl.multiple_of(at + i * step, step), step)
            total = terms[0][window, :].astype(F32)
            for term in terms[1:]:
                total = total + term[window, :].astype(F32)
            target[window, :] = total.astype(target.dtype)

    local[0].wait()
    core[0].wait_recv()
    add(out_ref.at[0], 0, rows, [own_ref.at[0], core_ref.at[0]])
    diag_b = copy(4, out_ref.at[0, low], relay_ref.at[low], to_b)
    diag_b.start()
    diag_f = copy(5, out_ref.at[0, high], relay_ref.at[high], to_f)
    diag_f.start()
    local[1].wait()
    core[1].wait_recv()
    add(out_ref.at[1], 0, half, [own_ref.at[1], core_ref.at[1]])
    b_low = copy(6, out_ref.at[1, low], land_ref.at[0, low], to_b)
    b_low.start()
    local[2].wait()
    core[2].wait_recv()
    add(out_ref.at[2], half, half, [own_ref.at[2], core_ref.at[2]])
    f_high = copy(7, out_ref.at[2, high], land_ref.at[1, high], to_f)
    f_high.start()
    diag_f.wait_recv()
    add(out_ref.at[1], half, half, [own_ref.at[1], core_ref.at[1], relay_ref])
    b_high = copy(8, out_ref.at[1, high], land_ref.at[0, high], to_b)
    b_high.start()
    diag_b.wait_recv()
    add(out_ref.at[2], 0, half, [own_ref.at[2], core_ref.at[2], relay_ref])
    f_low = copy(9, out_ref.at[2, low], land_ref.at[1, low], to_f)
    f_low.start()
    local[3].wait()
    core[3].wait_recv()
    for one in (b_low, f_high, b_high, f_low):
        one.wait_recv()
    add(o_ref, 0, rows, [own_ref.at[3], core_ref.at[3], land_ref.at[0], land_ref.at[1]])
    for one in core + [diag_b, diag_f, b_low, f_high, b_high, f_low]:
        one.wait_send()


def group_scatter(partial, collective_id):
    rows, width = partial.shape[0] // GROUP, partial.shape[1]
    block = (rows, width)
    return pl.pallas_call(
        scatter_kernel,
        out_shape=jax.ShapeDtypeStruct(block, F32),
        in_specs=[pl.BlockSpec(memory_space=pl.ANY)],
        out_specs=pl.BlockSpec(memory_space=pltpu.VMEM),
        scratch_shapes=[
            pltpu.VMEM((4,) + block, BF16),
            pltpu.VMEM((4,) + block, BF16),
            pltpu.VMEM((3,) + block, BF16),
            pltpu.VMEM(block, BF16),
            pltpu.VMEM((2,) + block, BF16),
            pltpu.SemaphoreType.DMA((4,)),
            pltpu.SemaphoreType.DMA((10,)),
            pltpu.SemaphoreType.DMA((10,)),
        ],
        compiler_params=pltpu.CompilerParams(
            collective_id=collective_id, has_side_effects=True, vmem_limit_bytes=24 << 20
        ),
        cost_estimate=pl.CostEstimate(
            flops=0, bytes_accessed=20 * partial.size, transcendentals=0
        ),
    )(partial.astype(BF16).reshape((GROUP,) + block))


def exchange(x, axis):
    count = lax.axis_size(axis)
    me = lax.axis_index(axis)
    got = {0: x}
    for shift in range(1, count):
        got[shift] = lax.ppermute(x, axis, [(i, (i + shift) % count) for i in range(count)])
    if count == 2:
        first = me == 0
        return [jnp.where(first, x, got[1]), jnp.where(first, got[1], x)]
    whole = jnp.stack([got[s] for s in range(count)])
    order = (me - jnp.arange(count)) % count
    return [whole[order[k]] for k in range(count)]


def gather_weight(pieces):
    mine = lax.all_to_all(pieces, TENSOR, split_axis=0, concat_axis=0, tiled=True)
    rows, cols = mine.shape[1:]
    mine = mine.reshape(2, 4 * rows, cols)
    along_e = jnp.stack(exchange(mine, "e"), axis=1)
    along_a = jnp.stack(exchange(along_e, "a"), axis=0)
    return along_a.reshape(-1, cols)


def scatter_axis(x, axis):
    count = lax.axis_size(axis)
    me = lax.axis_index(axis)
    total = lax.dynamic_index_in_dim(x, me, 0, keepdims=False)
    for shift in range(1, count):
        out = lax.dynamic_index_in_dim(x, (me + shift) % count, 0, keepdims=False).astype(BF16)
        total = total + lax.ppermute(
            out, axis, [(i, (i + shift) % count) for i in range(count)]
        ).astype(F32)
    return total


def scatter_weight(grad):
    a, e = lax.axis_size("a"), lax.axis_size("e")
    cols = grad.shape[1]
    rows = grad.shape[0] // (a * e * GROUP)
    grad = scatter_axis(grad.reshape(a, 2, e, 4 * rows, cols), "a")
    grad = scatter_axis(jnp.swapaxes(grad, 0, 1), "e")
    grad = grad.reshape(GROUP, rows, cols).astype(BF16)
    return lax.all_to_all(grad, TENSOR, split_axis=0, concat_axis=0, tiled=True)


def on_device(
    tokens,
    cotangent,
    lengths,
    prefix,
    qkv_weight,
    dense_weight,
    ffin_weight,
    ffout_weight,
    biases,
    norm_gains,
):
    sequences, seq_len, model_width = tokens.shape
    head_count = HEADS
    head_dim = model_width // head_count
    my_heads = head_count // GROUP
    hidden_units = ffout_weight.shape[1]
    unit_cols = -(-hidden_units // (GROUP * 128)) * 128
    padded = unit_cols * GROUP
    slice_width = my_heads * head_dim
    score_scale = head_dim ** (-0.5)
    residual_scale = (2.0 * LAYERS) ** 0.5
    total_rows = sequences * seq_len
    group_rows = GROUP * total_rows
    own_rows = qkv_weight.shape[0]

    token_matrix = tokens.reshape(total_rows, model_width)
    tokens_all = group_gather(token_matrix, 0)

    qkv_pieces = (
        qkv_weight.reshape(own_rows, 3, GROUP, slice_width)
        .transpose(2, 0, 1, 3)
        .reshape(GROUP, own_rows, 3 * slice_width)
    )
    dense_pieces = dense_weight.reshape(own_rows, GROUP, slice_width).transpose(1, 0, 2)

    def unit_pieces(weight):
        wide = jnp.pad(weight, ((0, 0), (0, padded - hidden_units)))
        return wide.reshape(own_rows, GROUP, unit_cols).transpose(1, 0, 2)

    ffin_pieces = jnp.concatenate(
        [unit_pieces(ffin_weight[:, :hidden_units]), unit_pieces(ffin_weight[:, hidden_units:])],
        axis=2,
    )
    ffout_pieces = unit_pieces(ffout_weight)

    qkv_cols = gather_weight(qkv_pieces)
    dense_cols = gather_weight(dense_pieces)
    dense_rows = (
        lax.all_to_all(
            dense_cols.reshape(GROUP, slice_width, slice_width),
            TENSOR,
            split_axis=0,
            concat_axis=0,
            tiled=True,
        )
        .transpose(1, 0, 2)
        .reshape(slice_width, model_width)
    )
    ffin_cols = gather_weight(ffin_pieces)
    ffout_cols = gather_weight(ffout_pieces)

    small = lax.all_gather(
        jnp.concatenate([biases, norm_gains], axis=1), AXES, axis=0, tiled=True
    ).astype(F32)
    bias_vals, gain_vals = small[:, :7], small[:, 7:]
    layout = lax.all_gather(
        jnp.concatenate([lengths, prefix], axis=1), TENSOR, axis=0, tiled=True
    )
    docs = lengths.shape[1]
    attention, local_pos, _ = token_layout(layout[:, :docs], layout[:, docs:], seq_len)
    valid_pos = jnp.arange(seq_len, dtype=jnp.int32)[None, :] < jnp.sum(
        lengths, axis=1, keepdims=True
    )
    cosine_table, sine_table = rotary_tables(local_pos, head_dim)

    me = (lax.axis_index("b") * 2 + lax.axis_index("f")) * 2 + lax.axis_index("c")
    my_bias = lax.dynamic_index_in_dim(
        bias_vals[:, 0:3].T.reshape(3, GROUP, slice_width), me, 1, keepdims=False
    ).reshape(-1)

    query_key_value_rows = jnp.dot(tokens_all, qkv_cols, preferred_element_type=F32) + my_bias
    head_shape = (GROUP * sequences, seq_len, my_heads, head_dim)
    query_part = query_key_value_rows[:, :slice_width].reshape(head_shape)
    key_part = query_key_value_rows[:, slice_width : 2 * slice_width].reshape(head_shape)
    q_low = rotate(query_part, cosine_table, sine_table).astype(BF16)
    k_low = rotate(key_part, cosine_table, sine_table).astype(BF16)
    v_low = query_key_value_rows[:, 2 * slice_width :].reshape(head_shape).astype(BF16)
    scores = score_scale * jnp.einsum(
        "sqhe,skhe->shqk", q_low, k_low, preferred_element_type=F32
    )
    masked = jnp.where(attention[:, None], scores, MASKED_SCORE)
    row_max = jnp.max(masked, axis=-1, keepdims=True)
    exponent = jnp.exp(masked - row_max)
    row_total = jnp.sum(exponent, axis=-1, keepdims=True)
    attn_probs = exponent / row_total
    probs_low = attn_probs.astype(BF16)
    context_vectors = jnp.einsum("shqk,skhe->sqhe", probs_low, v_low, preferred_element_type=F32)
    ctx_low = context_vectors.reshape(group_rows, slice_width).astype(BF16)
    attention_output = (
        group_scatter(jnp.dot(ctx_low, dense_rows, preferred_element_type=F32), 1)
        + bias_vals[:, 3]
    )
    resid_one = residual_scale * token_matrix.astype(F32) + attention_output
    first_normalized, norm_one_back = jax.vjp(
        layer_norm, resid_one, gain_vals[:, 0], bias_vals[:, 4]
    )
    normed_all = group_gather(first_normalized.astype(BF16), 2)
    inner_projection = jnp.dot(normed_all, ffin_cols, preferred_element_type=F32)

    def gated_units(both_parts):
        return (
            jax.nn.gelu(both_parts[:, :unit_cols], approximate=False) * both_parts[:, unit_cols:]
        )

    activation_result, gated_back = jax.vjp(gated_units, inner_projection)
    act_low = activation_result.astype(BF16)
    residual_branch = group_scatter(times_transposed(act_low, ffout_cols), 3) + bias_vals[:, 5]
    resid_two = residual_scale * first_normalized + residual_branch
    result, norm_two_back = jax.vjp(layer_norm, resid_two, gain_vals[:, 1], bias_vals[:, 6])

    grad_out = cotangent.reshape(total_rows, model_width).astype(F32)
    grad_out = grad_out * valid_pos.reshape(total_rows, 1).astype(F32)
    d_resid_two, d_gain_two, d_bias_two = norm_two_back(grad_out)
    d_branch = d_resid_two.astype(BF16)
    d_branch_all = group_gather(d_branch, 4)
    d_act = jnp.dot(d_branch_all, ffout_cols, preferred_element_type=F32)
    (d_inner,) = gated_back(d_act)
    d_inner_low = d_inner.astype(BF16)
    ffout_grad = scatter_weight(contract_rows(d_branch_all, act_low))
    d_normed = residual_scale * d_resid_two + group_scatter(
        times_transposed(d_inner_low, ffin_cols), 5
    )
    ffin_grad = scatter_weight(contract_rows(normed_all, d_inner_low))
    d_resid_one, d_gain_one, d_bias_one = norm_one_back(d_normed)
    d_attn = d_resid_one.astype(BF16)
    d_attn_all = group_gather(d_attn, 6)
    d_ctx_low = times_transposed(d_attn_all, dense_rows).reshape(head_shape).astype(BF16)
    dense_grad_rows = contract_rows(ctx_low, d_attn_all).astype(BF16)
    dense_grad = scatter_weight(
        lax.all_to_all(
            dense_grad_rows.reshape(slice_width, GROUP, slice_width).transpose(1, 0, 2),
            TENSOR,
            split_axis=0,
            concat_axis=0,
            tiled=True,
        )
        .reshape(model_width, slice_width)
        .astype(F32)
    )
    d_probs = jnp.einsum("sqhe,skhe->shqk", d_ctx_low, v_low, preferred_element_type=F32)
    d_value = jnp.einsum("shqk,sqhe->skhe", probs_low, d_ctx_low, preferred_element_type=F32)
    d_scores = attn_probs * (d_probs - jnp.sum(attn_probs * d_probs, axis=-1, keepdims=True))
    d_scores_low = jnp.where(attention[:, None], d_scores, 0.0).astype(BF16)
    d_query = score_scale * jnp.einsum(
        "shqk,skhe->sqhe", d_scores_low, k_low, preferred_element_type=F32
    )
    d_key = score_scale * jnp.einsum(
        "shqk,sqhe->skhe", d_scores_low, q_low, preferred_element_type=F32
    )
    d_query = rotate(d_query, cosine_table, -sine_table).reshape(group_rows, slice_width)
    d_key = rotate(d_key, cosine_table, -sine_table).reshape(group_rows, slice_width)
    d_qkv_low = jnp.concatenate(
        [d_query, d_key, d_value.reshape(group_rows, slice_width)], axis=1
    ).astype(BF16)
    qkv_grad = scatter_weight(contract_rows(tokens_all, d_qkv_low))
    d_tokens = residual_scale * d_resid_one + group_scatter(
        times_transposed(d_qkv_low, qkv_cols), 7
    )

    qkv_sums = jnp.sum(d_qkv_low.astype(F32), axis=0).reshape(3, 1, slice_width)
    qkv_sums = jnp.where(
        (jnp.arange(GROUP) == me)[None, :, None], qkv_sums, jnp.zeros_like(qkv_sums)
    ).reshape(3, model_width)
    small_grads = jnp.concatenate(
        [
            qkv_sums,
            jnp.stack(
                [
                    jnp.sum(d_attn.astype(F32), axis=0),
                    d_bias_one,
                    jnp.sum(d_branch.astype(F32), axis=0),
                    d_bias_two,
                    d_gain_one,
                    d_gain_two,
                ]
            ),
        ]
    ).T
    small_grads = lax.psum_scatter(small_grads, AXES, scatter_dimension=0, tiled=True)

    def unit_columns(pieces):
        return (
            pieces.transpose(1, 0, 2).reshape(own_rows, padded)[:, :hidden_units].astype(F32)
        )

    grad_qkv = (
        qkv_grad.reshape(GROUP, own_rows, 3, slice_width)
        .transpose(1, 2, 0, 3)
        .reshape(own_rows, 3 * model_width)
        .astype(F32)
    )
    grad_dense = dense_grad.transpose(1, 0, 2).reshape(own_rows, model_width).astype(F32)
    grad_ffin = jnp.concatenate(
        [unit_columns(ffin_grad[:, :, :unit_cols]), unit_columns(ffin_grad[:, :, unit_cols:])],
        axis=1,
    )
    grad_ffout = unit_columns(ffout_grad)
    return (
        result.astype(BF16).reshape(sequences, seq_len, model_width),
        d_tokens.reshape(sequences, seq_len, model_width),
        grad_qkv,
        grad_dense,
        grad_ffin,
        grad_ffout,
        small_grads[:, :7],
        small_grads[:, 7:],
    )


def solution(mesh):
    dp, fsdp = mesh.shape["dp"], mesh.shape["fsdp"]
    fine = Mesh(mesh.devices.reshape(dp // 2, 2, fsdp // 4, 2, 2), AXES)
    cube, flat = P(AXES, None, None), P(AXES, None)
    return jax.shard_map(
        on_device,
        mesh=fine,
        in_specs=(cube, cube) + (flat,) * 8,
        out_specs=(cube, cube) + (flat,) * 6,
        check_vma=False,
    )
```

```python
import functools
import math

import jax
import jax.numpy as jnp
import numpy as np
from jax import lax
from jax.experimental import pallas as pl
from jax.experimental.pallas import tpu as pltpu
from jax.sharding import Mesh
from jax.sharding import PartitionSpec as P

HEADS = 16
LAYERS = 24
MASKED_SCORE = -1e30
EPSILON = 1e-05
ROPE_BASE = 10000.0

AXES = ("a", "b", "e", "f", "c")
GROUP = 8
LANES = 128
DEVICE_MESH = pl.DeviceIdType.MESH
BF16 = jnp.bfloat16
F32 = jnp.float32
NT = (((1,), (1,)), ((), ()))
TN = (((0,), (0,)), ((), ()))


def dot(left, right, dims=(((1,), (0,)), ((), ()))):
    return lax.dot_general(left, right, dims, preferred_element_type=F32)


def span(start, size):
    return pl.ds(pl.multiple_of(start, size), size)


class Wires:
    def __init__(self, send_sem, recv_sem):
        self.send_sem, self.recv_sem, self.count = send_sem, recv_sem, 0

    def take(self, numbers=1):
        first = self.count
        self.count += numbers
        return first

    def send(self, number, source, target, device):
        one = pltpu.make_async_remote_copy(
            src_ref=source,
            dst_ref=target,
            send_sem=self.send_sem.at[number],
            recv_sem=self.recv_sem.at[number],
            device_id=device,
            device_id_type=DEVICE_MESH,
        )
        one.start()
        return one

    def arrived(self, number, landing):
        pltpu.make_async_copy(landing, landing, self.recv_sem.at[number]).wait()


def sent(copies):
    for one in copies:
        one.wait_send()
    copies.clear()


def layer_kernel(
    sizes,
    x_ref,
    cot_ref,
    table_ref,
    qp_ref,
    dp_ref,
    ip_ref,
    op_ref,
    out_ref,
    gx_ref,
    oq_ref,
    od_ref,
    oi_ref,
    oo_ref,
    yq_ref,
    yi_ref,
    yo_ref,
    zq_ref,
    zi_ref,
    zo_ref,
    wq_ref,
    wd_ref,
    wi_ref,
    wo_ref,
    xg_ref,
    hg_ref,
    dg_ref,
    uf_ref,
    mb_ref,
    du_ref,
    qk_ref,
    cx_ref,
    dc_ref,
    pb_ref,
    core_ref,
    stage_ref,
    relay_ref,
    land_ref,
    sum_ref,
    xh_ref,
    dr_ref,
    rstd_ref,
    bt_ref,
    sg_ref,
    qb_ref,
    tm_ref,
    local_sem,
    send_sem,
    recv_sem,
):
    A, E, R, rows, width, sw, uc, alpha, scale = sizes
    a, b, e, f, c = (lax.axis_index(axis) for axis in AXES)
    qc = 3 * sw
    all_rows = GROUP * rows
    half_rows = all_rows // 2
    slot = lambda bb, ff, cc: cc * 4 + bb * 2 + ff
    me = slot(b, f, c)
    my_rows = span(me * rows, rows)
    flip = lambda v, d: lax.rem(v + d, 2)
    rank = lambda aa, bb, ee, ff, cc: (((aa * 2 + bb) * E + ee) * 2 + ff) * 2 + cc
    line = lambda aa, bb, ee, ff, cc: span(rank(aa, bb, ee, ff, cc) * R, R)
    block = lambda aa, bb, ee: span(((aa * 2 + bb) * E + ee) * 4 * R, 4 * R)
    half = lambda aa, bb: span((aa * 2 + bb) * E * 4 * R, E * 4 * R)
    wires = Wires(send_sem, recv_sem)
    peers = [(r // 4, r // 2 % 2, r % 2) for r in range(GROUP)]

    barrier = pltpu.get_barrier_semaphore()
    others = 0
    for da in range(A):
        for de in range(E):
            for db, df, dc in peers:
                if da + de + db + df + dc:
                    pl.semaphore_signal(
                        barrier,
                        inc=1,
                        device_id={
                            "a": lax.rem(a + da, A),
                            "b": flip(b, db),
                            "e": lax.rem(e + de, E),
                            "f": flip(f, df),
                            "c": flip(c, dc),
                        },
                        device_id_type=DEVICE_MESH,
                    )
                    others += 1
    pl.semaphore_wait(barrier, others)

    class Weight:
        def __init__(self, index, pieces, buf, out, ylanding, zlanding):
            self.index, self.pieces, self.buf, self.out = index, pieces, buf, out
            self.ylanding, self.zlanding = ylanding, zlanding
            self.copies = []
            self.tp, self.z, self.y = (
                wires.take(GROUP),
                wires.take(2 * (E - 1)),
                wires.take(2 * E * (A - 1)),
            )
            self.gtp, self.gz, self.gy = (
                wires.take(GROUP),
                wires.take(2 * (E - 1)),
                wires.take(2 * (A - 1)),
            )

        def send(self, *copy):
            self.copies.append(wires.send(*copy))

        def own(self):
            return pltpu.make_async_copy(
                self.pieces.at[me], self.buf.at[line(a, b, e, f, c)], local_sem.at[self.index]
            )

        def tp_send(self):
            self.own().start()
            for r in range(1, GROUP):
                db, df, dc = peers[r]
                bb, ff, cc = flip(b, db), flip(f, df), flip(c, dc)
                self.send(
                    self.tp + r,
                    self.pieces.at[slot(bb, ff, cc)],
                    self.buf.at[line(a, b, e, f, c)],
                    {"b": bb, "f": ff, "c": cc},
                )

        def tp_arrive(self, db):
            for r in range(4 * db, 4 * db + 4):
                if r == 0:
                    self.own().wait()
                else:
                    _, df, dc = peers[r]
                    wires.arrived(
                        self.tp + r, self.buf.at[line(a, flip(b, db), e, flip(f, df), flip(c, dc))]
                    )
            for s in range(1, E):
                rows_ = self.buf.at[block(a, flip(b, db), e)]
                self.send(
                    self.z + db * (E - 1) + s - 1, rows_, rows_, {"e": lax.rem(e + s, E)}
                )
            self.y_send(db, 0)

        def y_send(self, db, s):
            rows_ = self.buf.at[block(a, flip(b, db), lax.rem(e + E - s, E))]
            for t in range(1, A):
                self.send(
                    self.y + (db * E + s) * (A - 1) + t - 1, rows_, rows_, {"a": lax.rem(a + t, A)}
                )

        def z_arrive(self, db):
            for s in range(1, E):
                wires.arrived(
                    self.z + db * (E - 1) + s - 1,
                    self.buf.at[block(a, flip(b, db), lax.rem(e + E - s, E))],
                )
                self.y_send(db, s)

        def y_arrive(self):
            for db in range(2):
                for s in range(E):
                    for t in range(1, A):
                        wires.arrived(
                            self.y + (db * E + s) * (A - 1) + t - 1,
                            self.buf.at[
                                block(lax.rem(a + A - t, A), flip(b, db), lax.rem(e + E - s, E))
                            ],
                        )

        def add(self, landing, base, count):
            cols = self.buf.shape[1]
            temp = tm_ref.at[pl.ds(0, count), pl.ds(0, cols)]
            load = pltpu.make_async_copy(landing, temp, local_sem.at[3])
            load.start()
            load.wait()

            @pl.loop(0, count // 16)
            def _(i):
                here = pl.ds(pl.multiple_of(base + i * 16, 16), 16)
                there = span(i * 16, 16)
                self.buf[here, :] = (
                    self.buf[here, :].astype(F32) + tm_ref[there, 0:cols].astype(F32)
                ).astype(BF16)

        def gy_send(self, db):
            bb = flip(b, db)
            for t in range(1, A):
                to = lax.rem(a + t, A)
                self.send(
                    self.gy + db * (A - 1) + t - 1,
                    self.buf.at[half(to, bb)],
                    self.ylanding.at[t - 1, db],
                    {"a": to},
                )

        def gy_add(self, db):
            bb = flip(b, db)
            for t in range(1, A):
                landing = self.ylanding.at[t - 1, db]
                wires.arrived(self.gy + db * (A - 1) + t - 1, landing)
                self.add(landing, (a * 2 + bb) * E * 4 * R, E * 4 * R)
            for s in range(1, E):
                to = lax.rem(e + s, E)
                self.send(
                    self.gz + db * (E - 1) + s - 1,
                    self.buf.at[block(a, bb, to)],
                    self.zlanding.at[s - 1, db],
                    {"e": to},
                )

        def gz_add(self, db):
            bb = flip(b, db)
            for s in range(1, E):
                landing = self.zlanding.at[s - 1, db]
                wires.arrived(self.gz + db * (E - 1) + s - 1, landing)
                self.add(landing, ((a * 2 + bb) * E + e) * 4 * R, 4 * R)
            for r in range(4 * db, 4 * db + 4):
                _, df, dc = peers[r]
                ff, cc = flip(f, df), flip(c, dc)
                rows_ = self.buf.at[line(a, bb, e, ff, cc)]
                if r == 0:
                    pltpu.make_async_copy(rows_, self.out.at[me], local_sem.at[self.index]).start()
                else:
                    self.send(
                        self.gtp + r, rows_, self.out.at[me], {"b": bb, "f": ff, "c": cc}
                    )

        def g_end(self):
            for r in range(GROUP):
                db, df, dc = peers[r]
                if r == 0:
                    pltpu.make_async_copy(
                        self.buf.at[line(a, b, e, f, c)],
                        self.out.at[me],
                        local_sem.at[self.index],
                    ).wait()
                else:
                    wires.arrived(
                        self.gtp + r, self.out.at[slot(flip(b, db), flip(f, df), flip(c, dc))]
                    )

    q_w = Weight(0, qp_ref, wq_ref, oq_ref, yq_ref, zq_ref)
    i_w = Weight(1, ip_ref, wi_ref, oi_ref, yi_ref, zi_ref)
    o_w = Weight(2, op_ref, wo_ref, oo_ref, yo_ref, zo_ref)

    dense_pieces = wd_ref.shape[0] // R
    dense_first = wires.take(dense_pieces)
    dense_sends = wires.take(A * E)
    dense_back = wires.take(A * E)
    dense_back_sends = wires.take(dense_pieces)
    first_row = rank(a, b, e, f, c) * R
    head = first_row // LANES

    def dense_route(aa, ee):
        piece = (head // 8) * (LANES // R) + lax.rem(first_row, LANES) // R
        target = {
            "a": aa,
            "b": lax.rem(head // 4, 2),
            "e": ee,
            "f": lax.rem(head, 2),
            "c": lax.rem(head // 2, 2),
        }
        return piece, target

    def is_me(target):
        same = target["a"] == a
        for axis, mine in (("b", b), ("e", e), ("f", f), ("c", c)):
            same = same & (target[axis] == mine)
        return same

    def remote(source, landing, send, recv, target):
        return pltpu.make_async_remote_copy(
            src_ref=source,
            dst_ref=landing,
            send_sem=send_sem.at[send],
            recv_sem=recv_sem.at[recv],
            device_id=target,
            device_id_type=DEVICE_MESH,
        )

    def dense_out(start):
        for da in range(A):
            for de in range(E):
                piece, target = dense_route(lax.rem(a + da, A), lax.rem(e + de, E))
                landing = wd_ref.at[span(piece * R, R)]
                away = remote(
                    dp_ref, landing, dense_sends + da * E + de, dense_first + piece, target
                )
                if da + de:
                    away.start() if start else away.wait_send()
                else:
                    here = is_me(target)

                    @pl.when(here)
                    def _():
                        if start:
                            pltpu.make_async_copy(
                                dp_ref, landing, recv_sem.at[dense_first + piece]
                            ).start()

                    @pl.when(jnp.logical_not(here))
                    def _():
                        away.start() if start else away.wait_send()

    def dense_arrive():
        for piece in range(dense_pieces):
            wires.arrived(dense_first + piece, wd_ref.at[pl.ds(piece * R, R)])

    def dense_grad_out(start):
        for piece in range(dense_pieces):
            i, offset = piece * R // LANES, piece * R % LANES
            owner = ((i * 8 + b * 4 + c * 2 + f) * LANES + offset) // R
            target = {
                "a": owner // (8 * E),
                "b": lax.rem(owner // (4 * E), 2),
                "e": lax.rem(owner // 4, E),
                "f": lax.rem(owner // 2, 2),
                "c": lax.rem(owner, 2),
            }
            from_ = a * E + e
            source = wd_ref.at[pl.ds(piece * R, R)]
            away = remote(
                source, od_ref.at[from_], dense_back_sends + piece, dense_back + from_, target
            )
            here = is_me(target)

            @pl.when(here)
            def _():
                if start:
                    pltpu.make_async_copy(
                        source, od_ref.at[from_], recv_sem.at[dense_back + from_]
                    ).start()

            @pl.when(jnp.logical_not(here))
            def _():
                away.start() if start else away.wait_send()

    def dense_grad_arrive():
        for k in range(A * E):
            wires.arrived(dense_back + k, od_ref.at[k])

    to_b, to_f, to_c = {"b": 1 - b}, {"f": 1 - f}, {"c": 1 - c}
    nb, nf, dg = slot(1 - b, f, c), slot(b, 1 - f, c), slot(1 - b, 1 - f, c)

    class Gather:
        def __init__(self, buf):
            self.buf, self.first, self.copies = buf, wires.take(10), []

        def part(self, place, which):
            if which is None:
                return self.buf.at[span(place * rows, rows)]
            return self.buf.at[span(place * rows + which * (rows // 2), rows // 2)]

        def copy(self, number, place, which, device):
            here = self.part(place, which)
            self.copies.append(wires.send(self.first + number, here, here, device))

        def landed(self, number, place, which):
            wires.arrived(self.first + number, self.part(place, which))

        def start(self):
            self.copy(0, me, 0, to_b)
            self.copy(1, me, 1, to_f)
            self.copy(2, me, 1, to_b)
            self.copy(3, me, 0, to_f)
            self.copy(4, me, None, to_c)

        def relay(self):
            self.landed(0, nb, 0)
            self.copy(5, nb, 0, to_f)
            self.landed(1, nf, 1)
            self.copy(6, nf, 1, to_b)
            self.landed(2, nb, 1)
            self.copy(7, nb, None, to_c)
            self.landed(3, nf, 0)
            self.copy(8, nf, None, to_c)

        def finish(self):
            self.landed(5, dg, 0)
            self.landed(6, dg, 1)
            self.copy(9, dg, None, to_c)
            other = 1 - c
            self.landed(4, slot(b, f, other), None)
            self.landed(7, slot(1 - b, f, other), None)
            self.landed(8, slot(b, 1 - f, other), None)
            self.landed(9, slot(1 - b, 1 - f, other), None)

    step = 16
    places = [(1 - b, 1 - f), (1 - b, f), (b, 1 - f), (b, f)]

    def accumulate(target, at, count, terms):
        @pl.loop(0, count // step)
        def _(i):
            window = pl.ds(pl.multiple_of(at + i * step, step), step)
            total = terms[0][window, :].astype(F32)
            for term in terms[1:]:
                total = total + term[window, :].astype(F32)
            target[window, :] = total.astype(target.dtype)

    def scatter(multiply, meanwhile=None):
        first, copies = wires.take(10), []

        def send(*copy):
            copies.append(wires.send(*copy))

        multiply((1 - c) * half_rows, half_rows)
        for k, (bb, ff) in enumerate(places):
            send(
                first + k,
                pb_ref.at[span(slot(bb, ff, 1 - c) * rows, rows)],
                core_ref.at[pl.ds(k * rows, rows)],
                to_c,
            )
        multiply(c * half_rows, half_rows)
        own = [pb_ref.at[span(slot(bb, ff, c) * rows, rows)] for bb, ff in places]
        core = [core_ref.at[pl.ds(k * rows, rows)] for k in range(4)]
        mid = rows // 2
        low, high = pl.ds(0, mid), pl.ds(mid, mid)
        if meanwhile is not None:
            meanwhile()
        wires.arrived(first, core[0])
        accumulate(stage_ref.at[0], 0, rows, [own[0], core[0]])
        send(first + 4, stage_ref.at[0, low], relay_ref.at[low], to_b)
        send(first + 5, stage_ref.at[0, high], relay_ref.at[high], to_f)
        wires.arrived(first + 1, core[1])
        accumulate(stage_ref.at[1], 0, mid, [own[1], core[1]])
        send(first + 6, stage_ref.at[1, low], land_ref.at[0, low], to_b)
        wires.arrived(first + 2, core[2])
        accumulate(stage_ref.at[2], mid, mid, [own[2], core[2]])
        send(first + 7, stage_ref.at[2, high], land_ref.at[1, high], to_f)
        wires.arrived(first + 5, relay_ref.at[high])
        accumulate(stage_ref.at[1], mid, mid, [own[1], core[1], relay_ref])
        send(first + 8, stage_ref.at[1, high], land_ref.at[0, high], to_b)
        wires.arrived(first + 4, relay_ref.at[low])
        accumulate(stage_ref.at[2], 0, mid, [own[2], core[2], relay_ref])
        send(first + 9, stage_ref.at[2, low], land_ref.at[1, low], to_f)
        wires.arrived(first + 3, core[3])
        wires.arrived(first + 6, land_ref.at[0, low])
        wires.arrived(first + 7, land_ref.at[1, high])
        wires.arrived(first + 8, land_ref.at[0, high])
        wires.arrived(first + 9, land_ref.at[1, low])
        accumulate(sum_ref, 0, rows, [own[3], core[3], land_ref.at[0], land_ref.at[1]])
        sent(copies)

    def blocks(count_m, count_n, body):
        @pl.loop(0, count_m * count_n)
        def _(k):
            body(k // count_n, lax.rem(k, count_n))

    def onto_partial(left, weight, cols):
        def multiply(first, count):
            def body(m, n):
                here = pl.ds(pl.multiple_of(first, half_rows) + m * 512, 512)
                pb_ref[here, span(n * 512, 512)] = dot(
                    left[here, :], weight[span(n * 512, 512), 0:cols], NT
                ).astype(BF16)

            blocks(count // 512, width // 512, body)

        return multiply

    q_w.tp_send()
    own_x = pltpu.make_async_copy(x_ref, xg_ref.at[my_rows], local_sem.at[4])
    own_x.start()
    dense_out(True)
    sg_ref[...] = jnp.zeros_like(sg_ref)
    q_w.tp_arrive(0)
    q_w.tp_arrive(1)
    own_x.wait()
    tokens = Gather(xg_ref)
    tokens.start()
    i_w.tp_send()
    tokens.relay()
    q_w.z_arrive(0)
    tokens.finish()
    q_w.z_arrive(1)
    i_w.tp_arrive(0)
    i_w.tp_arrive(1)
    o_w.tp_send()
    q_w.y_arrive()

    @pl.loop(0, width // LANES)
    def _(k):
        here = span(k * LANES, LANES)
        turned = wq_ref[here, qc : qc + LANES].astype(F32).T
        bt_ref[:, here] = turned[0:16, :]

    heads = [i * 8 + b * 4 + c * 2 + f for i in range(sw // LANES)]
    for t in range(3):
        for i, number in enumerate(heads):
            at = t * sw + i * LANES
            qb_ref[0:1, at : at + LANES] = bt_ref[t : t + 1, span(number * LANES, LANES)]

    def projection(m, n):
        here, cols = span(m * 512, 512), span(n * sw, sw)
        uf_ref[here, cols] = (
            dot(xg_ref[here, 0:width], wq_ref[:, cols]) + qb_ref[0:1, cols]
        )

    blocks(all_rows // 512, 3, projection)

    row_at = lax.broadcasted_iota(jnp.int32, (rows, rows), 0)
    col_at = lax.broadcasted_iota(jnp.int32, (rows, rows), 1)

    def sequence(s):
        here = span(s * rows, rows)
        info = xg_ref[here, width : width + LANES].astype(F32)
        turned = info.T
        allowed = (info[:, 0:1] == turned[0:1, :]) & (
            (turned[2:3, :] < info[:, 1:2]) | (col_at <= row_at)
        )
        picked = (info[:, 2:3] == col_at.astype(F32)).astype(BF16)
        parts = dot(picked, table_ref[...])
        cos_sin = parts[:, 0:LANES] + parts[:, LANES : 2 * LANES] + parts[:, 2 * LANES :]
        swapped = pltpu.roll(cos_sin, LANES // 2, axis=1)
        first = col_at < LANES // 2
        cosine = jnp.where(first, cos_sin, swapped)
        sine = jnp.where(first, -swapped, cos_sin)
        return here, allowed, cosine, sine

    def turn(value, cosine, sine):
        return value * cosine + pltpu.roll(value, LANES // 2, axis=1) * sine

    def softmax(q, k, allowed):
        scores = jnp.where(allowed, scale * dot(q, k, NT), MASKED_SCORE)
        power = jnp.exp(scores - jnp.max(scores, axis=1, keepdims=True))
        return power / jnp.sum(power, axis=1, keepdims=True)

    @pl.loop(0, GROUP)
    def _(s):
        here, allowed, cosine, sine = sequence(s)
        for i in range(sw // LANES):
            cols = [pl.ds(t * sw + i * LANES, LANES) for t in range(3)]
            q = turn(uf_ref[here, cols[0]], cosine, sine).astype(BF16)
            k = turn(uf_ref[here, cols[1]], cosine, sine).astype(BF16)
            v = uf_ref[here, cols[2]].astype(BF16)
            qk_ref[here, cols[0]] = q
            qk_ref[here, cols[1]] = k
            qk_ref[here, cols[2]] = v
            probs = softmax(q, k, allowed).astype(BF16)
            cx_ref[here, i * LANES : (i + 1) * LANES] = dot(probs, v).astype(BF16)

    dense_arrive()

    def dense_partial(first, count):
        def body(m, n):
            here = pl.ds(pl.multiple_of(first, half_rows) + m * 512, 512)
            cols = span(n * 512, 512)
            pb_ref[here, cols] = dot(cx_ref[here, :], wd_ref[:, cols]).astype(BF16)

        blocks(count // 512, width // 512, body)

    scatter(dense_partial, lambda: i_w.z_arrive(0))

    def row_loop(body):
        @pl.loop(0, rows // 16)
        def _(i):
            body(span(i * 16, 16), span(me * rows + i * 16, 16))

    def normalize(value):
        centered = value - jnp.mean(value, axis=1, keepdims=True)
        rstd = lax.rsqrt(jnp.mean(centered * centered, axis=1, keepdims=True) + EPSILON)
        return centered * rstd, rstd

    def first_norm(here, there):
        value = (
            alpha * xg_ref[there, 0:width].astype(F32) + sum_ref[here, :] + bt_ref[3:4, :]
        )
        unit, rstd = normalize(value)
        xh_ref[here, :] = unit
        rstd_ref[here, :] = jnp.broadcast_to(rstd, (16, LANES))
        hg_ref[there, :] = (unit * bt_ref[7:8, :] + bt_ref[4:5, :]).astype(BF16)

    row_loop(first_norm)
    normed = Gather(hg_ref)
    normed.start()
    normed.relay()
    normed.finish()
    i_w.z_arrive(1)
    o_w.tp_arrive(0)
    o_w.tp_arrive(1)
    i_w.y_arrive()

    def units(m, n):
        here = span(m * 512, 512)
        gate_cols = span(n * 256, 256)
        up_cols = span(uc + n * 256, 256)
        left = hg_ref[here, :]
        gate = dot(left, wi_ref[:, gate_cols])
        up = dot(left, wi_ref[:, up_cols])
        cdf = 0.5 * (1.0 + lax.erf(gate * (0.5**0.5)))
        density = jnp.exp(-0.5 * gate * gate) * (1.0 / math.sqrt(2.0 * math.pi))
        act = gate * cdf
        mb_ref[here, gate_cols] = (act * up).astype(BF16)
        uf_ref[here, gate_cols] = (cdf + gate * density) * up
        uf_ref[here, up_cols] = act

    blocks(all_rows // 512, uc // 256, units)
    o_w.z_arrive(0)
    o_w.z_arrive(1)
    o_w.y_arrive()
    scatter(onto_partial(mb_ref, wo_ref, uc))

    def add_row(row, value):
        sg_ref[row : row + 1, :] += jnp.sum(value, axis=0, keepdims=True)

    def norm_back(grad, gain, unit, rstd):
        scaled = grad * gain
        return rstd * (
            scaled
            - jnp.mean(scaled, axis=1, keepdims=True)
            - unit * jnp.mean(scaled * unit, axis=1, keepdims=True)
        )

    def second_norm(here, there):
        normed_one = xh_ref[here, :] * bt_ref[7:8, :] + bt_ref[4:5, :]
        unit, rstd = normalize(alpha * normed_one + sum_ref[here, :] + bt_ref[5:6, :])
        out_ref[here, :] = (unit * bt_ref[8:9, :] + bt_ref[6:7, :]).astype(BF16)
        grad = cot_ref[here, :].astype(F32)
        back = norm_back(grad, bt_ref[8:9, :], unit, rstd)
        low = back.astype(BF16)
        dr_ref[here, :] = back
        dg_ref[there, :] = low
        add_row(5, low.astype(F32))
        add_row(6, grad)
        add_row(8, grad * unit)

    row_loop(second_norm)
    branch = Gather(dg_ref)
    branch.start()
    branch.relay()
    branch.finish()

    def units_back(m, n):
        here = span(m * 512, 512)
        gate_cols, up_cols = span(n * 256, 256), span(uc + n * 256, 256)
        grad = dot(dg_ref[here, :], wo_ref[:, gate_cols])
        du_ref[here, gate_cols] = (uf_ref[here, gate_cols] * grad).astype(BF16)
        du_ref[here, up_cols] = (uf_ref[here, up_cols] * grad).astype(BF16)

    blocks(all_rows // 512, uc // 256, units_back)

    def weight_grad(left, right, target, cols, bn):
        def body(m, n):
            here, there = span(m * 512, 512), span(n * bn, bn)
            target[here, there] = dot(left[:, here], right[:, there], TN).astype(BF16)

        blocks(width // 512, cols // bn, body)

    sent(o_w.copies)
    weight_grad(dg_ref, mb_ref, wo_ref, uc, uc)
    o_w.gy_send(0)
    o_w.gy_send(1)

    def in_grad():
        sent(i_w.copies)
        weight_grad(hg_ref, du_ref, wi_ref, 2 * uc, uc)
        i_w.gy_send(0)
        i_w.gy_send(1)

    sent(branch.copies)
    scatter(onto_partial(du_ref, wi_ref, 2 * uc), in_grad)

    def first_norm_back(here, there):
        grad = alpha * dr_ref[here, :] + sum_ref[here, :]
        unit = xh_ref[here, :]
        back = norm_back(grad, bt_ref[7:8, :], unit, rstd_ref[here, 0:1])
        low = back.astype(BF16)
        dr_ref[here, :] = back
        dg_ref[there, :] = low
        add_row(3, low.astype(F32))
        add_row(4, grad)
        add_row(7, grad * unit)

    row_loop(first_norm_back)
    attended = Gather(dg_ref)
    attended.start()
    o_w.gy_add(0)
    attended.relay()
    attended.finish()

    def context_back(m, n):
        here = span(m * 512, 512)
        dc_ref[here, :] = dot(dg_ref[here, :], wd_ref[...], NT).astype(BF16)

    blocks(all_rows // 512, 1, context_back)

    def dense_grad(m, n):
        cols = span(n * 512, 512)
        wd_ref[:, cols] = dot(cx_ref[...], dg_ref[:, cols], TN).astype(BF16)

    dense_out(False)
    blocks(1, width // 512, dense_grad)
    dense_grad_out(True)
    o_w.gy_add(1)

    @pl.loop(0, GROUP)
    def _(s):
        here, allowed, cosine, sine = sequence(s)
        for i, number in enumerate(heads):
            cols = [pl.ds(t * sw + i * LANES, LANES) for t in range(3)]
            q, k, v = (qk_ref[here, one] for one in cols)
            grad = dc_ref[here, i * LANES : (i + 1) * LANES]
            probs = softmax(q, k, allowed)
            d_probs = dot(grad, v, NT)
            d_value = dot(probs.astype(BF16), grad, TN)
            d_scores = probs * (d_probs - jnp.sum(probs * d_probs, axis=1, keepdims=True))
            low = jnp.where(allowed, d_scores, 0.0).astype(BF16)
            d_query = turn(scale * dot(low, k), cosine, -sine)
            d_key = turn(scale * dot(low, q, TN), cosine, -sine)
            for t, value in enumerate((d_query, d_key, d_value)):
                value = value.astype(BF16)
                mb_ref[here, cols[t]] = value
                lanes = span(number * LANES, LANES)
                sg_ref[t : t + 1, lanes] += jnp.sum(value.astype(F32), axis=0, keepdims=True)

    o_w.gz_add(0)
    o_w.gz_add(1)
    i_w.gy_add(0)

    def qkv_grad():
        sent(q_w.copies)
        weight_grad(xg_ref, mb_ref, wq_ref, qc, qc)

        @pl.loop(0, width // LANES)
        def _(k):
            here = span(k * LANES, LANES)
            wq_ref[here, qc : qc + LANES] = sg_ref[:, here].T.astype(BF16)

        q_w.gy_send(0)
        q_w.gy_send(1)

    scatter(onto_partial(mb_ref, wq_ref, qc), qkv_grad)

    def tokens_back(here, there):
        gx_ref[here, :] = alpha * dr_ref[here, :] + sum_ref[here, :]

    row_loop(tokens_back)

    i_w.gz_add(0)
    i_w.gy_add(1)
    i_w.gz_add(1)
    q_w.gy_add(0)
    q_w.gy_add(1)
    q_w.gz_add(0)
    q_w.gz_add(1)
    for weight in (o_w, i_w, q_w):
        weight.g_end()
    dense_grad_out(False)
    dense_grad_arrive()
    for flow in (q_w, i_w, o_w, tokens, normed, attended):
        sent(flow.copies)


def on_device(
    tokens,
    cotangent,
    lengths,
    prefix,
    qkv_weight,
    dense_weight,
    ffin_weight,
    ffout_weight,
    biases,
    norm_gains,
):
    _, rows, width = tokens.shape
    A, E = lax.axis_size("a"), lax.axis_size("e")
    R = qkv_weight.shape[0]
    head_dim = width // HEADS
    my_heads = HEADS // GROUP
    hidden = ffout_weight.shape[1]
    uc = -(-hidden // (GROUP * 256)) * 256
    padded = uc * GROUP
    sw = my_heads * head_dim
    qc = 3 * sw
    qe = qc + LANES
    docs = lengths.shape[1]

    ends = jnp.cumsum(lengths, axis=1)
    positions = jnp.arange(rows, dtype=jnp.int32)[:, None]
    index = jnp.sum((positions >= ends).astype(jnp.int32), axis=1, keepdims=True)
    member = index == jnp.arange(docs, dtype=jnp.int32)[None, :]
    start_at = jnp.sum(jnp.where(member, ends - lengths, 0), axis=1, keepdims=True)
    prefix_at = jnp.sum(jnp.where(member, prefix, 0), axis=1, keepdims=True)
    valid = positions < ends[:, -1:]
    key = jnp.where(valid, index, docs + positions)
    local_pos = jnp.where(valid, positions - start_at, 0)
    info = jnp.concatenate([key, prefix_at, local_pos], axis=1).astype(BF16)
    x_ext = jnp.concatenate(
        [tokens.reshape(rows, width), jnp.pad(info, ((0, 0), (0, LANES - 3)))], axis=1
    )
    cot = jnp.where(valid, cotangent.reshape(rows, width), 0).astype(BF16)

    inverse = np.float32(ROPE_BASE) ** (
        -np.arange(head_dim // 2, dtype=np.float32) * np.float32(2.0 / head_dim)
    )
    angles = np.arange(rows, dtype=np.float32)[:, None] * inverse.astype(np.float32)
    rest = np.concatenate([np.cos(angles), np.sin(angles)], axis=1).astype(np.float32)
    terms = []
    for _ in range(3):
        terms.append(rest.astype(BF16))
        rest = rest - terms[-1].astype(np.float32)
    table = jnp.asarray(np.concatenate(terms, axis=1))

    qkv_pieces = (
        qkv_weight.reshape(R, 3, my_heads, 2, 2, 2, head_dim)
        .transpose(4, 3, 5, 0, 1, 2, 6)
        .reshape(GROUP, R, qc)
    )
    small = jnp.concatenate([biases, norm_gains], axis=1)
    small = jnp.pad(small, ((0, 0), (0, LANES - small.shape[1])))
    qkv_pieces = jnp.concatenate(
        [qkv_pieces, jnp.broadcast_to(small, (GROUP, R, LANES))], axis=2
    )

    def unit_pieces(weight):
        wide = jnp.pad(weight, ((0, 0), (0, padded - hidden)))
        return wide.reshape(R, GROUP, uc).transpose(1, 0, 2)

    ffin_pieces = jnp.concatenate(
        [unit_pieces(ffin_weight[:, :hidden]), unit_pieces(ffin_weight[:, hidden:])], axis=2
    )
    ffout_pieces = unit_pieces(ffout_weight)

    wires = 3 * (2 * GROUP + 4 * (E - 1) + 2 * E * (A - 1) + 2 * (A - 1))
    wires += 2 * (sw // R) + 2 * A * E + 8 * 10
    group_rows = GROUP * rows
    sizes = (A, E, R, rows, width, sw, uc, (2.0 * LAYERS) ** 0.5, head_dim ** (-0.5))
    shape = jax.ShapeDtypeStruct
    anywhere, vmem = pl.BlockSpec(memory_space=pl.ANY), pl.BlockSpec(memory_space=pltpu.VMEM)
    cols = (qe, 2 * uc, uc)
    results = pl.pallas_call(
        functools.partial(layer_kernel, sizes),
        out_shape=[
            shape((rows, width), BF16),
            shape((rows, width), F32),
            shape((GROUP, R, qe), BF16),
            shape((A * E, R, width), BF16),
            shape((GROUP, R, 2 * uc), BF16),
            shape((GROUP, R, uc), BF16),
        ]
        + [shape((A - 1, 2, E * 4 * R, n), BF16) for n in cols]
        + [shape((E - 1, 2, 4 * R, n), BF16) for n in cols],
        in_specs=[anywhere, vmem, vmem] + [anywhere] * 4,
        out_specs=[vmem, vmem] + [anywhere] * 10,
        scratch_shapes=[
            pltpu.VMEM((width, qe), BF16),
            pltpu.VMEM((sw, width), BF16),
            pltpu.VMEM((width, 2 * uc), BF16),
            pltpu.VMEM((width, uc), BF16),
            pltpu.VMEM((group_rows, width + LANES), BF16),
            pltpu.VMEM((group_rows, width), BF16),
            pltpu.VMEM((group_rows, width), BF16),
            pltpu.VMEM((group_rows, 2 * uc), F32),
            pltpu.VMEM((group_rows, uc), BF16),
            pltpu.VMEM((group_rows, 2 * uc), BF16),
            pltpu.VMEM((group_rows, qc), BF16),
            pltpu.VMEM((group_rows, sw), BF16),
            pltpu.VMEM((group_rows, sw), BF16),
            pltpu.VMEM((group_rows, width), BF16),
            pltpu.VMEM((4 * rows, width), BF16),
            pltpu.VMEM((3, rows, width), BF16),
            pltpu.VMEM((rows, width), BF16),
            pltpu.VMEM((2, rows, width), BF16),
            pltpu.VMEM((rows, width), F32),
            pltpu.VMEM((rows, width), F32),
            pltpu.VMEM((rows, width), F32),
            pltpu.VMEM((rows, LANES), F32),
            pltpu.VMEM((16, width), F32),
            pltpu.VMEM((LANES, width), F32),
            pltpu.VMEM((8, qc), F32),
            pltpu.VMEM((E * 4 * R, 2 * uc), BF16),
            pltpu.SemaphoreType.DMA((5,)),
            pltpu.SemaphoreType.DMA((wires,)),
            pltpu.SemaphoreType.DMA((wires,)),
        ],
        compiler_params=pltpu.CompilerParams(
            collective_id=0, has_side_effects=True, vmem_limit_bytes=63 << 20
        ),
    )(x_ext, cot, table, qkv_pieces, dense_weight, ffin_pieces, ffout_pieces)
    result, d_tokens, qkv_grad, dense_grad, ffin_grad, ffout_grad = results[:6]

    def unit_columns(pieces):
        return pieces.transpose(1, 0, 2).reshape(R, padded)[:, :hidden].astype(F32)

    grad_qkv = (
        qkv_grad[:, :, :qc]
        .reshape(2, 2, 2, R, 3, my_heads, head_dim)
        .transpose(3, 4, 5, 1, 0, 2, 6)
        .reshape(R, 3 * width)
        .astype(F32)
    )
    small_grads = jnp.sum(qkv_grad[:, :, qc:].astype(F32), axis=0)
    return (
        result.reshape(tokens.shape),
        d_tokens.reshape(tokens.shape),
        grad_qkv,
        jnp.sum(dense_grad.astype(F32), axis=0),
        jnp.concatenate(
            [unit_columns(ffin_grad[:, :, :uc]), unit_columns(ffin_grad[:, :, uc:])], axis=1
        ),
        unit_columns(ffout_grad),
        small_grads[:, :7],
        small_grads[:, 7:9],
    )


def solution(mesh):
    dp, fsdp = mesh.shape["dp"], mesh.shape["fsdp"]
    fine = Mesh(mesh.devices.reshape(dp // 2, 2, fsdp // 4, 2, 2), AXES)
    cube, flat = P(AXES, None, None), P(AXES, None)
    return jax.shard_map(
        on_device,
        mesh=fine,
        in_specs=(cube, cube) + (flat,) * 8,
        out_specs=(cube, cube) + (flat,) * 6,
        check_vma=False,
    )
```

```python
import functools
import math

import jax
import jax.numpy as jnp
import numpy as np
from jax import lax
from jax.experimental import pallas as pl
from jax.experimental.pallas import tpu as pltpu
from jax.sharding import Mesh
from jax.sharding import PartitionSpec as P

HEADS = 16
LAYERS = 24
MASKED_SCORE = -1e30
EPSILON = 1e-05
ROPE_BASE = 10000.0

AXES = ("a", "b", "e", "f", "c")
GROUP = 8
LANES = 128
DEVICE_MESH = pl.DeviceIdType.MESH
BF16 = jnp.bfloat16
F32 = jnp.float32
NT = (((1,), (1,)), ((), ()))
TN = (((0,), (0,)), ((), ()))


def dot(left, right, dims=(((1,), (0,)), ((), ()))):
    return lax.dot_general(left, right, dims, preferred_element_type=F32)


def span(start, size):
    return pl.ds(pl.multiple_of(start, size), size)


class Wires:
    def __init__(self, send_sem, recv_sem):
        self.send_sem, self.recv_sem, self.count = send_sem, recv_sem, 0

    def take(self, numbers=1):
        first = self.count
        self.count += numbers
        return first

    def send(self, number, source, target, device):
        one = pltpu.make_async_remote_copy(
            src_ref=source,
            dst_ref=target,
            send_sem=self.send_sem.at[number],
            recv_sem=self.recv_sem.at[number],
            device_id=device,
            device_id_type=DEVICE_MESH,
        )
        one.start()
        return one

    def arrived(self, number, landing):
        pltpu.make_async_copy(landing, landing, self.recv_sem.at[number]).wait()


def sent(copies):
    for one in copies:
        one.wait_send()
    copies.clear()


def layer_kernel(
    sizes,
    x_ref,
    cot_ref,
    table_ref,
    sp_ref,
    qp_ref,
    dp_ref,
    ip_ref,
    op_ref,
    out_ref,
    gx_ref,
    os_ref,
    oq_ref,
    od_ref,
    oi_ref,
    oo_ref,
    ys_ref,
    yq_ref,
    yd_ref,
    yi_ref,
    yo_ref,
    zs_ref,
    zq_ref,
    zd_ref,
    zi_ref,
    zo_ref,
    ws_ref,
    wq_ref,
    wd_ref,
    wi_ref,
    wo_ref,
    go_ref,
    xg_ref,
    hg_ref,
    dg_ref,
    uf_ref,
    mb_ref,
    du_ref,
    qk_ref,
    cx_ref,
    dc_ref,
    pb_ref,
    core_ref,
    stage_ref,
    relay_ref,
    land_ref,
    sum_ref,
    xh_ref,
    dr_ref,
    rstd_ref,
    bt_ref,
    sg_ref,
    qb_ref,
    tm_ref,
    td_ref,
    local_sem,
    send_sem,
    recv_sem,
):
    A, E, R, rows, width, sw, uc, alpha, scale = sizes
    a, b, e, f, c = (lax.axis_index(axis) for axis in AXES)
    qc = 3 * sw
    all_rows = GROUP * rows
    half_rows = all_rows // 2
    slot = lambda bb, ff, cc: cc * 4 + bb * 2 + ff
    me = slot(b, f, c)
    my_rows = span(me * rows, rows)
    flip = lambda v, d: lax.rem(v + d, 2)
    rank = lambda aa, bb, ee, ff, cc: (((aa * 2 + bb) * E + ee) * 2 + ff) * 2 + cc
    wires = Wires(send_sem, recv_sem)
    peers = [(r // 4, r // 2 % 2, r % 2) for r in range(GROUP)]

    barrier = pltpu.get_barrier_semaphore()
    others = 0
    for da in range(A):
        for de in range(E):
            for db, df, dc in peers:
                if da + de + db + df + dc:
                    pl.semaphore_signal(
                        barrier,
                        inc=1,
                        device_id={
                            "a": lax.rem(a + da, A),
                            "b": flip(b, db),
                            "e": lax.rem(e + de, E),
                            "f": flip(f, df),
                            "c": flip(c, dc),
                        },
                        device_id_type=DEVICE_MESH,
                    )
                    others += 1
    pl.semaphore_wait(barrier, others)

    class Weight:
        def __init__(self, index, pieces, buf, out, ylanding, zlanding):
            self.index, self.pieces, self.buf, self.out = index, pieces, buf, out
            self.ylanding, self.zlanding = ylanding, zlanding
            self.R = pieces.shape[1]
            self.copies = []
            self.tp, self.z, self.y = (
                wires.take(GROUP),
                wires.take(2 * (E - 1)),
                wires.take(2 * E * (A - 1)),
            )
            self.gtp, self.gz, self.gy = (
                wires.take(GROUP),
                wires.take(2 * (E - 1)),
                wires.take(2 * (A - 1)),
            )

        def send(self, *copy):
            self.copies.append(wires.send(*copy))

        def line(self, aa, bb, ee, ff, cc):
            return span(rank(aa, bb, ee, ff, cc) * self.R, self.R)

        def block(self, aa, bb, ee):
            return span(((aa * 2 + bb) * E + ee) * 4 * self.R, 4 * self.R)

        def half(self, aa, bb):
            return span((aa * 2 + bb) * E * 4 * self.R, E * 4 * self.R)

        def own(self):
            return pltpu.make_async_copy(
                self.pieces.at[me], self.buf.at[self.line(a, b, e, f, c)], local_sem.at[self.index]
            )

        def tp_send(self):
            self.own().start()
            for r in range(1, GROUP):
                db, df, dc = peers[r]
                bb, ff, cc = flip(b, db), flip(f, df), flip(c, dc)
                self.send(
                    self.tp + r,
                    self.pieces.at[slot(bb, ff, cc)],
                    self.buf.at[self.line(a, b, e, f, c)],
                    {"b": bb, "f": ff, "c": cc},
                )

        def tp_wait(self, db):
            for r in range(4 * db, 4 * db + 4):
                if r == 0:
                    self.own().wait()
                else:
                    _, df, dc = peers[r]
                    wires.arrived(
                        self.tp + r, self.buf.at[self.line(a, flip(b, db), e, flip(f, df), flip(c, dc))]
                    )

        def z_send(self, db):
            rows_ = self.buf.at[self.block(a, flip(b, db), e)]
            for s in range(1, E):
                self.send(
                    self.z + db * (E - 1) + s - 1, rows_, rows_, {"e": lax.rem(e + s, E)}
                )

        def y_send(self, db, s):
            rows_ = self.buf.at[self.block(a, flip(b, db), lax.rem(e + E - s, E))]
            for t in range(1, A):
                self.send(
                    self.y + (db * E + s) * (A - 1) + t - 1, rows_, rows_, {"a": lax.rem(a + t, A)}
                )

        def z_arrive(self, db):
            for s in range(1, E):
                wires.arrived(
                    self.z + db * (E - 1) + s - 1,
                    self.buf.at[self.block(a, flip(b, db), lax.rem(e + E - s, E))],
                )
                self.y_send(db, s)

        def y_arrive(self):
            for db in range(2):
                for s in range(E):
                    for t in range(1, A):
                        wires.arrived(
                            self.y + (db * E + s) * (A - 1) + t - 1,
                            self.buf.at[
                                self.block(lax.rem(a + A - t, A), flip(b, db), lax.rem(e + E - s, E))
                            ],
                        )

        def add(self, landing, base, count):
            cols = self.buf.shape[1]
            temp = tm_ref.at[pl.ds(0, count), pl.ds(0, cols)]
            load = pltpu.make_async_copy(landing, temp, local_sem.at[4])
            load.start()
            load.wait()

            @pl.loop(0, count // 16)
            def _(i):
                here = pl.ds(pl.multiple_of(base + i * 16, 16), 16)
                there = span(i * 16, 16)
                self.buf[here, :] = (
                    self.buf[here, :].astype(F32) + tm_ref[there, 0:cols].astype(F32)
                ).astype(BF16)

        def gy_send(self, db):
            bb = flip(b, db)
            for t in range(1, A):
                to = lax.rem(a + t, A)
                self.send(
                    self.gy + db * (A - 1) + t - 1,
                    self.buf.at[self.half(to, bb)],
                    self.ylanding.at[t - 1, db],
                    {"a": to},
                )

        def gy_add(self, db):
            bb = flip(b, db)
            for t in range(1, A):
                landing = self.ylanding.at[t - 1, db]
                wires.arrived(self.gy + db * (A - 1) + t - 1, landing)
                self.add(landing, (a * 2 + bb) * E * 4 * self.R, E * 4 * self.R)
            for s in range(1, E):
                to = lax.rem(e + s, E)
                self.send(
                    self.gz + db * (E - 1) + s - 1,
                    self.buf.at[self.block(a, bb, to)],
                    self.zlanding.at[s - 1, db],
                    {"e": to},
                )

        def gz_add(self, db):
            bb = flip(b, db)
            for s in range(1, E):
                landing = self.zlanding.at[s - 1, db]
                wires.arrived(self.gz + db * (E - 1) + s - 1, landing)
                self.add(landing, ((a * 2 + bb) * E + e) * 4 * self.R, 4 * self.R)
            for r in range(4 * db, 4 * db + 4):
                _, df, dc = peers[r]
                ff, cc = flip(f, df), flip(c, dc)
                rows_ = self.buf.at[self.line(a, bb, e, ff, cc)]
                if r == 0:
                    pltpu.make_async_copy(rows_, self.out.at[me], local_sem.at[self.index]).start()
                else:
                    self.send(
                        self.gtp + r, rows_, self.out.at[me], {"b": bb, "f": ff, "c": cc}
                    )

        def g_end(self):
            for r in range(GROUP):
                db, df, dc = peers[r]
                if r == 0:
                    pltpu.make_async_copy(
                        self.buf.at[self.line(a, b, e, f, c)],
                        self.out.at[me],
                        local_sem.at[self.index],
                    ).wait()
                else:
                    wires.arrived(
                        self.gtp + r, self.out.at[slot(flip(b, db), flip(f, df), flip(c, dc))]
                    )

    s_w = Weight(3, sp_ref, ws_ref, os_ref, ys_ref, zs_ref)
    q_w = Weight(0, qp_ref, wq_ref, oq_ref, yq_ref, zq_ref)
    i_w = Weight(1, ip_ref, wi_ref, oi_ref, yi_ref, zi_ref)
    o_w = Weight(2, op_ref, wo_ref, oo_ref, yo_ref, zo_ref)

    def remote(source, landing, send, recv, target):
        return pltpu.make_async_remote_copy(
            src_ref=source,
            dst_ref=landing,
            send_sem=send_sem.at[send],
            recv_sem=recv_sem.at[recv],
            device_id=target,
            device_id_type=DEVICE_MESH,
        )

    class Dense:
        def __init__(self):
            self.pieces = wd_ref.shape[0] // R
            self.first = wires.take(self.pieces)
            self.push = wires.take(1)
            self.zs = wires.take(self.pieces * (E - 1))
            self.ys = wires.take(self.pieces * (A - 1))
            self.gy = wires.take(self.pieces * (A - 1))
            self.gz = wires.take(self.pieces * (E - 1))
            self.back = wires.take(1)
            self.back_sends = wires.take(self.pieces)
            self.owners = []
            for piece in range(self.pieces):
                i, offset = piece * R // LANES, piece * R % LANES
                owner = ((i * 8 + b * 4 + c * 2 + f) * LANES + offset) // R
                self.owners.append(
                    {
                        "a": owner // (8 * E),
                        "b": lax.rem(owner // (4 * E), 2),
                        "e": lax.rem(owner // 4, E),
                        "f": lax.rem(owner // 2, 2),
                        "c": lax.rem(owner, 2),
                    }
                )

        def rows(self, piece):
            return wd_ref.at[pl.ds(piece * R, R)]

        def each(self, test, body):
            for piece, owner in enumerate(self.owners):
                same_a, same_e = owner["a"] == a, owner["e"] == e

                @pl.when(test(same_a, same_e))
                def _():
                    body(piece, owner)

        def local_or_remote(self, target, source, landing, send, recv, start):
            here = target["b"] == b
            for axis, mine in (("f", f), ("c", c)):
                here = here & (target[axis] == mine)
            away = remote(source, landing, send, recv, target)

            @pl.when(here)
            def _():
                if start:
                    pltpu.make_async_copy(source, landing, recv_sem.at[recv]).start()

            @pl.when(jnp.logical_not(here))
            def _():
                away.start() if start else away.wait_send()

        def out(self, start):
            first_row = rank(a, b, e, f, c) * R
            head = first_row // LANES
            piece = (head // 8) * (LANES // R) + lax.rem(first_row, LANES) // R
            target = {
                "b": lax.rem(head // 4, 2),
                "f": lax.rem(head, 2),
                "c": lax.rem(head // 2, 2),
            }
            landing = wd_ref.at[span(piece * R, R)]
            self.local_or_remote(target, dp_ref, landing, self.push, self.first + piece, start)

        def z(self, piece, s):
            rows_ = self.rows(piece)
            number = self.zs + piece * (E - 1) + s - 1
            return remote(rows_, rows_, number, self.first + piece, {"e": lax.rem(e + s, E)})

        def y(self, piece, t):
            rows_ = self.rows(piece)
            number = self.ys + piece * (A - 1) + t - 1
            return remote(rows_, rows_, number, self.first + piece, {"a": lax.rem(a + t, A)})

        def arrived(self, piece, _=None):
            wires.arrived(self.first + piece, self.rows(piece))

        def z_send(self):
            def body(piece, owner):
                self.arrived(piece)
                for s in range(1, E):
                    self.z(piece, s).start()

            self.each(lambda same_a, same_e: same_a & same_e, body)

        def y_send(self):
            self.each(lambda same_a, same_e: same_a & jnp.logical_not(same_e), self.arrived)

            def body(piece, owner):
                for t in range(1, A):
                    self.y(piece, t).start()

            self.each(lambda same_a, same_e: same_a, body)

        def y_arrive(self):
            self.each(lambda same_a, same_e: jnp.logical_not(same_a), self.arrived)

        def sent(self):
            self.out(False)

            def over_z(piece, owner):
                for s in range(1, E):
                    self.z(piece, s).wait_send()

            def over_y(piece, owner):
                for t in range(1, A):
                    self.y(piece, t).wait_send()

            self.each(lambda same_a, same_e: same_a & same_e, over_z)
            self.each(lambda same_a, same_e: same_a, over_y)

        def g_y(self, piece, t):
            to = lax.rem(a + t, A)
            number = self.gy + piece * (A - 1) + t - 1
            copy = remote(self.rows(piece), yd_ref.at[t - 1, piece], number, number, {"a": to})
            return to, copy

        def gy_send(self, start=True):
            for piece, owner in enumerate(self.owners):
                for t in range(1, A):
                    to, copy = self.g_y(piece, t)

                    @pl.when(owner["a"] == to)
                    def _():
                        copy.start() if start else copy.wait_send()

        def add(self, landing, piece):
            load = pltpu.make_async_copy(landing, td_ref, local_sem.at[4])
            load.start()
            load.wait()

            @pl.loop(0, R // 16)
            def _(i):
                here, there = span(piece * R + i * 16, 16), span(i * 16, 16)
                wd_ref[here, :] = (
                    wd_ref[here, :].astype(F32) + td_ref[there, :].astype(F32)
                ).astype(BF16)

        def g_z(self, piece, s):
            to = lax.rem(e + s, E)
            number = self.gz + piece * (E - 1) + s - 1
            copy = remote(self.rows(piece), zd_ref.at[s - 1, piece], number, number, {"e": to})
            return to, copy

        def gz_send(self, start=True):
            for piece, owner in enumerate(self.owners):
                for s in range(1, E):
                    to, copy = self.g_z(piece, s)

                    @pl.when((owner["a"] == a) & (owner["e"] == to))
                    def _():
                        copy.start() if start else copy.wait_send()

        def gy_add(self):
            def body(piece, owner):
                for t in range(1, A):
                    landing = yd_ref.at[t - 1, piece]
                    wires.arrived(self.gy + piece * (A - 1) + t - 1, landing)
                    self.add(landing, piece)

            self.each(lambda same_a, same_e: same_a, body)
            self.gz_send()

        def home(self, piece, owner, start):
            target = {axis: owner[axis] for axis in ("b", "f", "c")}
            self.local_or_remote(
                target, self.rows(piece), od_ref, self.back_sends + piece, self.back, start
            )

        def gz_add(self):
            def body(piece, owner):
                for s in range(1, E):
                    landing = zd_ref.at[s - 1, piece]
                    wires.arrived(self.gz + piece * (E - 1) + s - 1, landing)
                    self.add(landing, piece)
                self.home(piece, owner, True)

            self.each(lambda same_a, same_e: same_a & same_e, body)

        def g_end(self):
            wires.arrived(self.back, od_ref)
            self.gy_send(False)
            self.gz_send(False)
            self.each(
                lambda same_a, same_e: same_a & same_e,
                lambda piece, owner: self.home(piece, owner, False),
            )

    dense = Dense()

    to_b, to_f, to_c = {"b": 1 - b}, {"f": 1 - f}, {"c": 1 - c}
    nb, nf, dg = slot(1 - b, f, c), slot(b, 1 - f, c), slot(1 - b, 1 - f, c)

    class Gather:
        def __init__(self, buf, lean):
            self.buf, self.first, self.copies, self.lean = buf, wires.take(10), [], lean

        def part(self, place, which):
            if which is None:
                return self.buf.at[span(place * rows, rows)]
            return self.buf.at[span(place * rows + which * (rows // 2), rows // 2)]

        def copy(self, number, place, which, device):
            here = self.part(place, which)
            self.copies.append(wires.send(self.first + number, here, here, device))

        def landed(self, number, place, which):
            wires.arrived(self.first + number, self.part(place, which))

        def start(self):
            self.copy(0, me, 0, to_b)
            self.copy(1, me, 1, to_f)
            self.copy(2, me, 1, to_b)
            self.copy(3, me, 0, to_f)
            self.copy(4, me, None, to_c)

        def relay(self):
            if self.lean:
                self.landed(1, nf, 1)
                self.copy(6, nf, 1, to_b)
                self.landed(3, nf, 0)
                self.copy(5, nf, 0, to_b)
                self.copy(8, nf, None, to_c)
                self.landed(0, nb, 0)
                self.landed(2, nb, 1)
                self.copy(7, nb, None, to_c)
                return
            self.landed(0, nb, 0)
            self.copy(5, nb, 0, to_f)
            self.landed(1, nf, 1)
            self.copy(6, nf, 1, to_b)
            self.landed(2, nb, 1)
            self.copy(7, nb, None, to_c)
            self.landed(3, nf, 0)
            self.copy(8, nf, None, to_c)

        def finish(self):
            self.landed(5, dg, 0)
            self.landed(6, dg, 1)
            self.copy(9, dg, None, to_c)
            other = 1 - c
            self.landed(4, slot(b, f, other), None)
            self.landed(7, slot(1 - b, f, other), None)
            self.landed(8, slot(b, 1 - f, other), None)
            self.landed(9, slot(1 - b, 1 - f, other), None)

    step = 16
    places = [(1 - b, 1 - f), (1 - b, f), (b, 1 - f), (b, f)]

    def accumulate(target, at, count, terms):
        @pl.loop(0, count // step)
        def _(i):
            window = pl.ds(pl.multiple_of(at + i * step, step), step)
            total = terms[0][window, :].astype(F32)
            for term in terms[1:]:
                total = total + term[window, :].astype(F32)
            target[window, :] = total.astype(target.dtype)

    def scatter(multiply, lean, early=None, late=None):
        first, copies = wires.take(10), []

        def send(*copy):
            copies.append(wires.send(*copy))

        multiply((1 - c) * half_rows, half_rows)
        for k, (bb, ff) in enumerate(places):
            send(
                first + k,
                pb_ref.at[span(slot(bb, ff, 1 - c) * rows, rows)],
                core_ref.at[pl.ds(k * rows, rows)],
                to_c,
            )
        multiply(c * half_rows, half_rows)
        own = [pb_ref.at[span(slot(bb, ff, c) * rows, rows)] for bb, ff in places]
        core = [core_ref.at[pl.ds(k * rows, rows)] for k in range(4)]
        mid = rows // 2
        low, high = pl.ds(0, mid), pl.ds(mid, mid)
        early, late = (hook or (lambda: None) for hook in (early, late))
        wires.arrived(first, core[0])
        accumulate(stage_ref.at[0], 0, rows, [own[0], core[0]])
        if lean:
            send(first + 4, stage_ref.at[0], relay_ref, to_b)
            wires.arrived(first + 1, core[1])
            accumulate(stage_ref.at[1], 0, rows, [own[1], core[1]])
            send(first + 6, stage_ref.at[1], land_ref.at[0], to_b)
            early()
            wires.arrived(first + 2, core[2])
            wires.arrived(first + 4, relay_ref)
            accumulate(stage_ref.at[2], 0, rows, [own[2], core[2], relay_ref])
            send(first + 7, stage_ref.at[2], land_ref.at[1], to_f)
            late()
            wires.arrived(first + 3, core[3])
            wires.arrived(first + 6, land_ref.at[0])
            wires.arrived(first + 7, land_ref.at[1])
        else:
            send(first + 4, stage_ref.at[0, low], relay_ref.at[low], to_b)
            send(first + 5, stage_ref.at[0, high], relay_ref.at[high], to_f)
            wires.arrived(first + 1, core[1])
            accumulate(stage_ref.at[1], 0, mid, [own[1], core[1]])
            send(first + 6, stage_ref.at[1, low], land_ref.at[0, low], to_b)
            wires.arrived(first + 2, core[2])
            accumulate(stage_ref.at[2], mid, mid, [own[2], core[2]])
            send(first + 7, stage_ref.at[2, high], land_ref.at[1, high], to_f)
            early()
            wires.arrived(first + 5, relay_ref.at[high])
            accumulate(stage_ref.at[1], mid, mid, [own[1], core[1], relay_ref])
            send(first + 8, stage_ref.at[1, high], land_ref.at[0, high], to_b)
            wires.arrived(first + 4, relay_ref.at[low])
            accumulate(stage_ref.at[2], 0, mid, [own[2], core[2], relay_ref])
            send(first + 9, stage_ref.at[2, low], land_ref.at[1, low], to_f)
            late()
            wires.arrived(first + 3, core[3])
            wires.arrived(first + 6, land_ref.at[0, low])
            wires.arrived(first + 7, land_ref.at[1, high])
            wires.arrived(first + 8, land_ref.at[0, high])
            wires.arrived(first + 9, land_ref.at[1, low])
        accumulate(sum_ref, 0, rows, [own[3], core[3], land_ref.at[0], land_ref.at[1]])
        sent(copies)

    def blocks(count_m, count_n, body):
        @pl.loop(0, count_m * count_n)
        def _(k):
            body(k // count_n, lax.rem(k, count_n))

    def onto_partial(left, weight, cols):
        def multiply(first, count):
            def body(m, n):
                here = pl.ds(pl.multiple_of(first, half_rows) + m * 512, 512)
                pb_ref[here, span(n * 512, 512)] = dot(
                    left[here, :], weight[span(n * 512, 512), 0:cols], NT
                ).astype(BF16)

            blocks(count // 512, width // 512, body)

        return multiply

    q_w.tp_send()
    s_w.tp_send()
    dense.out(True)
    own_x = pltpu.make_async_copy(x_ref, xg_ref.at[my_rows], local_sem.at[5])
    own_x.start()
    sg_ref[...] = jnp.zeros_like(sg_ref)
    tokens = Gather(xg_ref, True)
    for db in range(2):
        q_w.tp_wait(db)
        q_w.z_send(db)
        q_w.y_send(db, 0)
    own_x.wait()
    tokens.start()
    i_w.tp_send()
    for db in range(2):
        s_w.tp_wait(db)
        s_w.z_send(db)
        s_w.y_send(db, 0)
    dense.z_send()
    q_w.z_arrive(0)
    tokens.relay()
    i_w.tp_wait(0)
    i_w.z_send(0)
    i_w.y_send(0, 0)
    q_w.z_arrive(1)
    s_w.z_arrive(0)
    s_w.z_arrive(1)
    i_w.tp_wait(1)
    dense.y_send()
    i_w.y_send(1, 0)
    tokens.finish()
    o_w.tp_send()
    s_w.y_arrive()
    q_w.y_arrive()

    lane = lax.broadcasted_iota(jnp.int32, (16, LANES), 1)

    @pl.loop(0, width // LANES)
    def _(k):
        line = jnp.zeros((16, LANES), F32)
        for j in range(LANES // R):
            part = ws_ref[span((k * (LANES // R) + j) * 16, 16), :].astype(F32)
            if j:
                part = pltpu.roll(part, j * R, axis=1)
            line = jnp.where(lane // R == j, part, line)
        bt_ref[:, span(k * LANES, LANES)] = line

    heads = [i * 8 + b * 4 + c * 2 + f for i in range(sw // LANES)]
    for t in range(3):
        for i, number in enumerate(heads):
            at = t * sw + i * LANES
            qb_ref[0:1, at : at + LANES] = bt_ref[t : t + 1, span(number * LANES, LANES)]

    def projection(m, n):
        here, cols = span(m * 512, 512), span(n * sw, sw)
        uf_ref[here, cols] = (
            dot(xg_ref[here, 0:width], wq_ref[:, cols]) + qb_ref[0:1, cols]
        )

    blocks(all_rows // 512, 3, projection)

    row_at = lax.broadcasted_iota(jnp.int32, (rows, rows), 0)
    col_at = lax.broadcasted_iota(jnp.int32, (rows, rows), 1)

    def sequence(s):
        here = span(s * rows, rows)
        info = xg_ref[here, width : width + LANES].astype(F32)
        turned = info.T
        allowed = (info[:, 0:1] == turned[0:1, :]) & (
            (turned[2:3, :] < info[:, 1:2]) | (col_at <= row_at)
        )
        picked = (info[:, 2:3] == col_at.astype(F32)).astype(BF16)
        parts = dot(picked, table_ref[...])
        cos_sin = parts[:, 0:LANES] + parts[:, LANES : 2 * LANES] + parts[:, 2 * LANES :]
        swapped = pltpu.roll(cos_sin, LANES // 2, axis=1)
        first = col_at < LANES // 2
        cosine = jnp.where(first, cos_sin, swapped)
        sine = jnp.where(first, -swapped, cos_sin)
        return here, allowed, cosine, sine

    def turn(value, cosine, sine):
        return value * cosine + pltpu.roll(value, LANES // 2, axis=1) * sine

    def softmax(q, k, allowed):
        scores = jnp.where(allowed, scale * dot(q, k, NT), MASKED_SCORE)
        power = jnp.exp(scores - jnp.max(scores, axis=1, keepdims=True))
        return power / jnp.sum(power, axis=1, keepdims=True)

    @pl.loop(0, GROUP)
    def _(s):
        here, allowed, cosine, sine = sequence(s)
        for i in range(sw // LANES):
            cols = [pl.ds(t * sw + i * LANES, LANES) for t in range(3)]
            q = turn(uf_ref[here, cols[0]], cosine, sine).astype(BF16)
            k = turn(uf_ref[here, cols[1]], cosine, sine).astype(BF16)
            v = uf_ref[here, cols[2]].astype(BF16)
            qk_ref[here, cols[0]] = q
            qk_ref[here, cols[1]] = k
            qk_ref[here, cols[2]] = v
            probs = softmax(q, k, allowed).astype(BF16)
            cx_ref[here, i * LANES : (i + 1) * LANES] = dot(probs, v).astype(BF16)

    i_w.z_send(1)
    dense.y_arrive()

    def dense_partial(first, count):
        def body(m, n):
            here = pl.ds(pl.multiple_of(first, half_rows) + m * 512, 512)
            cols = span(n * 512, 512)
            pb_ref[here, cols] = dot(cx_ref[here, :], wd_ref[:, cols]).astype(BF16)

        blocks(count // 512, width // 512, body)

    scatter(dense_partial, True, lambda: i_w.z_arrive(0))
    for db in range(2):
        o_w.tp_wait(db)
        o_w.z_send(db)

    def row_loop(body):
        @pl.loop(0, rows // 16)
        def _(i):
            body(span(i * 16, 16), span(me * rows + i * 16, 16))

    def normalize(value):
        centered = value - jnp.mean(value, axis=1, keepdims=True)
        rstd = lax.rsqrt(jnp.mean(centered * centered, axis=1, keepdims=True) + EPSILON)
        return centered * rstd, rstd

    def first_norm(here, there):
        value = (
            alpha * xg_ref[there, 0:width].astype(F32) + sum_ref[here, :] + bt_ref[3:4, :]
        )
        unit, rstd = normalize(value)
        xh_ref[here, :] = unit
        rstd_ref[here, :] = jnp.broadcast_to(rstd, (16, LANES))
        hg_ref[there, :] = (unit * bt_ref[7:8, :] + bt_ref[4:5, :]).astype(BF16)

    row_loop(first_norm)
    normed = Gather(hg_ref, True)
    normed.start()
    o_w.y_send(0, 0)
    o_w.y_send(1, 0)
    normed.relay()
    i_w.z_arrive(1)
    normed.finish()
    i_w.y_arrive()

    def units(m, n):
        here = span(m * 512, 512)
        gate_cols = span(n * 256, 256)
        up_cols = span(uc + n * 256, 256)
        left = hg_ref[here, :]
        gate = dot(left, wi_ref[:, gate_cols])
        up = dot(left, wi_ref[:, up_cols])
        cdf = 0.5 * (1.0 + lax.erf(gate * (0.5**0.5)))
        density = jnp.exp(-0.5 * gate * gate) * (1.0 / math.sqrt(2.0 * math.pi))
        act = gate * cdf
        mb_ref[here, gate_cols] = (act * up).astype(BF16)
        uf_ref[here, gate_cols] = (cdf + gate * density) * up
        uf_ref[here, up_cols] = act

    blocks(all_rows // 512, uc // 256, units)
    o_w.z_arrive(0)
    o_w.z_arrive(1)
    o_w.y_arrive()
    scatter(onto_partial(mb_ref, wo_ref, uc), False)

    def add_row(row, value):
        sg_ref[row : row + 1, :] += jnp.sum(value, axis=0, keepdims=True)

    def norm_back(grad, gain, unit, rstd):
        scaled = grad * gain
        return rstd * (
            scaled
            - jnp.mean(scaled, axis=1, keepdims=True)
            - unit * jnp.mean(scaled * unit, axis=1, keepdims=True)
        )

    def second_norm(here, there):
        normed_one = xh_ref[here, :] * bt_ref[7:8, :] + bt_ref[4:5, :]
        unit, rstd = normalize(alpha * normed_one + sum_ref[here, :] + bt_ref[5:6, :])
        out_ref[here, :] = (unit * bt_ref[8:9, :] + bt_ref[6:7, :]).astype(BF16)
        grad = cot_ref[here, :].astype(F32)
        back = norm_back(grad, bt_ref[8:9, :], unit, rstd)
        low = back.astype(BF16)
        dr_ref[here, :] = back
        dg_ref[there, :] = low
        add_row(5, low.astype(F32))
        add_row(6, grad)
        add_row(8, grad * unit)

    row_loop(second_norm)
    branch = Gather(dg_ref, False)
    branch.start()
    branch.relay()
    branch.finish()

    def units_back(m, n):
        here = span(m * 512, 512)
        gate_cols, up_cols = span(n * 256, 256), span(uc + n * 256, 256)
        grad = dot(dg_ref[here, :], wo_ref[:, gate_cols])
        du_ref[here, gate_cols] = (uf_ref[here, gate_cols] * grad).astype(BF16)
        du_ref[here, up_cols] = (uf_ref[here, up_cols] * grad).astype(BF16)

    def weight_grad(left, right, target, cols, bn):
        def body(m, n):
            here, there = span(m * 512, 512), span(n * bn, bn)
            target[here, there] = dot(left[:, here], right[:, there], TN).astype(BF16)

        blocks(width // 512, cols // bn, body)

    sent(o_w.copies)
    weight_grad(dg_ref, mb_ref, go_ref, uc, uc)
    o_w.buf = go_ref
    o_w.gy_send(0)
    o_w.gy_send(1)
    blocks(all_rows // 512, uc // 256, units_back)

    def in_grad():
        sent(i_w.copies)
        weight_grad(hg_ref, du_ref, wi_ref, 2 * uc, uc)
        i_w.gy_send(0)
        i_w.gy_send(1)

    sent(branch.copies)
    scatter(onto_partial(du_ref, wi_ref, 2 * uc), False, in_grad, lambda: o_w.gy_add(0))

    def first_norm_back(here, there):
        grad = alpha * dr_ref[here, :] + sum_ref[here, :]
        unit = xh_ref[here, :]
        back = norm_back(grad, bt_ref[7:8, :], unit, rstd_ref[here, 0:1])
        low = back.astype(BF16)
        dr_ref[here, :] = back
        dg_ref[there, :] = low
        add_row(3, low.astype(F32))
        add_row(4, grad)
        add_row(7, grad * unit)

    row_loop(first_norm_back)
    attended = Gather(dg_ref, True)
    attended.start()
    o_w.gy_add(1)
    attended.relay()
    attended.finish()

    def context_back(m, n):
        here = span(m * 512, 512)
        dc_ref[here, :] = dot(dg_ref[here, :], wd_ref[...], NT).astype(BF16)

    blocks(all_rows // 512, 1, context_back)

    def dense_grad(m, n):
        cols = span(n * 512, 512)
        wd_ref[:, cols] = dot(cx_ref[...], dg_ref[:, cols], TN).astype(BF16)

    dense.sent()
    blocks(1, width // 512, dense_grad)
    dense.gy_send()

    @pl.loop(0, GROUP)
    def _(s):
        here, allowed, cosine, sine = sequence(s)
        for i, number in enumerate(heads):
            cols = [pl.ds(t * sw + i * LANES, LANES) for t in range(3)]
            q, k, v = (qk_ref[here, one] for one in cols)
            grad = dc_ref[here, i * LANES : (i + 1) * LANES]
            probs = softmax(q, k, allowed)
            d_probs = dot(grad, v, NT)
            d_value = dot(probs.astype(BF16), grad, TN)
            d_scores = probs * (d_probs - jnp.sum(probs * d_probs, axis=1, keepdims=True))
            low = jnp.where(allowed, d_scores, 0.0).astype(BF16)
            d_query = turn(scale * dot(low, k), cosine, -sine)
            d_key = turn(scale * dot(low, q, TN), cosine, -sine)
            for t, value in enumerate((d_query, d_key, d_value)):
                value = value.astype(BF16)
                mb_ref[here, cols[t]] = value
                lanes = span(number * LANES, LANES)
                sg_ref[t : t + 1, lanes] += jnp.sum(value.astype(F32), axis=0, keepdims=True)

    i_w.gy_add(0)

    def qkv_grad():
        sent(q_w.copies)
        weight_grad(xg_ref, mb_ref, wq_ref, qc, qc)

        q_w.gy_send(0)
        q_w.gy_send(1)
        sent(s_w.copies)

        @pl.loop(0, width // LANES)
        def _(k):
            line = sg_ref[:, span(k * LANES, LANES)]
            for j in range(LANES // R):
                part = line if j == 0 else pltpu.roll(line, LANES - j * R, axis=1)
                ws_ref[span((k * (LANES // R) + j) * 16, 16), :] = part.astype(BF16)

        s_w.gy_send(0)
        s_w.gy_send(1)

    def late_adds():
        i_w.gy_add(1)

    scatter(onto_partial(mb_ref, wq_ref, qc), True, qkv_grad, late_adds)

    def tokens_back(here, there):
        gx_ref[here, :] = alpha * dr_ref[here, :] + sum_ref[here, :]

    row_loop(tokens_back)

    dense.gy_add()
    o_w.gz_add(0)
    o_w.gz_add(1)
    q_w.gy_add(0)
    q_w.gy_add(1)
    s_w.gy_add(0)
    s_w.gy_add(1)
    dense.gz_add()
    i_w.gz_add(0)
    i_w.gz_add(1)
    q_w.gz_add(0)
    q_w.gz_add(1)
    s_w.gz_add(0)
    s_w.gz_add(1)
    for weight in (dense, o_w, i_w, q_w, s_w):
        weight.g_end()
    for flow in (q_w, i_w, o_w, s_w, tokens, normed, attended):
        sent(flow.copies)


def on_device(
    tokens,
    cotangent,
    lengths,
    prefix,
    qkv_weight,
    dense_weight,
    ffin_weight,
    ffout_weight,
    biases,
    norm_gains,
):
    _, rows, width = tokens.shape
    A, E = lax.axis_size("a"), lax.axis_size("e")
    R = qkv_weight.shape[0]
    head_dim = width // HEADS
    my_heads = HEADS // GROUP
    hidden = ffout_weight.shape[1]
    uc = -(-hidden // (GROUP * 256)) * 256
    padded = uc * GROUP
    sw = my_heads * head_dim
    qc = 3 * sw
    docs = lengths.shape[1]

    ends = jnp.cumsum(lengths, axis=1)
    positions = jnp.arange(rows, dtype=jnp.int32)[:, None]
    index = jnp.sum((positions >= ends).astype(jnp.int32), axis=1, keepdims=True)
    member = index == jnp.arange(docs, dtype=jnp.int32)[None, :]
    start_at = jnp.sum(jnp.where(member, ends - lengths, 0), axis=1, keepdims=True)
    prefix_at = jnp.sum(jnp.where(member, prefix, 0), axis=1, keepdims=True)
    valid = positions < ends[:, -1:]
    key = jnp.where(valid, index, docs + positions)
    local_pos = jnp.where(valid, positions - start_at, 0)
    info = jnp.concatenate([key, prefix_at, local_pos], axis=1).astype(BF16)
    x_ext = jnp.concatenate(
        [tokens.reshape(rows, width), jnp.pad(info, ((0, 0), (0, LANES - 3)))], axis=1
    )
    cot = jnp.where(valid, cotangent.reshape(rows, width), 0).astype(BF16)

    inverse = np.float32(ROPE_BASE) ** (
        -np.arange(head_dim // 2, dtype=np.float32) * np.float32(2.0 / head_dim)
    )
    angles = np.arange(rows, dtype=np.float32)[:, None] * inverse.astype(np.float32)
    rest = np.concatenate([np.cos(angles), np.sin(angles)], axis=1).astype(np.float32)
    terms = []
    for _ in range(3):
        terms.append(rest.astype(BF16))
        rest = rest - terms[-1].astype(np.float32)
    table = jnp.asarray(np.concatenate(terms, axis=1))

    qkv_pieces = (
        qkv_weight.reshape(R, 3, my_heads, 2, 2, 2, head_dim)
        .transpose(4, 3, 5, 0, 1, 2, 6)
        .reshape(GROUP, R, qc)
    )
    small = jnp.concatenate([biases, norm_gains], axis=1).T
    small = jnp.pad(small, ((0, 16 - small.shape[0]), (0, LANES - R)))
    small_pieces = jnp.broadcast_to(small, (GROUP, 16, LANES))

    def unit_pieces(weight):
        wide = jnp.pad(weight, ((0, 0), (0, padded - hidden)))
        return wide.reshape(R, GROUP, uc).transpose(1, 0, 2)

    ffin_pieces = jnp.concatenate(
        [unit_pieces(ffin_weight[:, :hidden]), unit_pieces(ffin_weight[:, hidden:])], axis=2
    )
    ffout_pieces = unit_pieces(ffout_weight)

    wires = 4 * (2 * GROUP + 4 * (E - 1) + 2 * E * (A - 1) + 2 * (A - 1))
    wires += (sw // R) * 2 * (A + E) + 2 + 8 * 10
    group_rows = GROUP * rows
    sizes = (A, E, R, rows, width, sw, uc, (2.0 * LAYERS) ** 0.5, head_dim ** (-0.5))
    shape = jax.ShapeDtypeStruct
    anywhere, vmem = pl.BlockSpec(memory_space=pl.ANY), pl.BlockSpec(memory_space=pltpu.VMEM)
    landings = [(64, LANES), (4 * R, qc), None, (4 * R, 2 * uc), (4 * R, uc)]
    dense_landing = (sw // R, R, width)
    results = pl.pallas_call(
        functools.partial(layer_kernel, sizes),
        out_shape=[
            shape((rows, width), BF16),
            shape((rows, width), F32),
            shape((GROUP, 16, LANES), BF16),
            shape((GROUP, R, qc), BF16),
            shape((R, width), BF16),
            shape((GROUP, R, 2 * uc), BF16),
            shape((GROUP, R, uc), BF16),
        ]
        + [
            shape((A - 1,) + ((2, E * one[0], one[1]) if one else dense_landing), BF16)
            for one in landings
        ]
        + [
            shape((E - 1,) + ((2,) + one if one else dense_landing), BF16)
            for one in landings
        ],
        in_specs=[anywhere, vmem, vmem] + [anywhere] * 5,
        out_specs=[vmem, vmem] + [anywhere] * 15,
        scratch_shapes=[
            pltpu.VMEM((width // R * 16, LANES), BF16),
            pltpu.VMEM((width, qc), BF16),
            pltpu.VMEM((sw, width), BF16),
            pltpu.VMEM((width, 2 * uc), BF16),
            pltpu.VMEM((width, uc), BF16),
            pltpu.VMEM((width, uc), BF16),
            pltpu.VMEM((group_rows, width + LANES), BF16),
            pltpu.VMEM((group_rows, width), BF16),
            pltpu.VMEM((group_rows, width), BF16),
            pltpu.VMEM((group_rows, 2 * uc), F32),
            pltpu.VMEM((group_rows, uc), BF16),
            pltpu.VMEM((group_rows, 2 * uc), BF16),
            pltpu.VMEM((group_rows, qc), BF16),
            pltpu.VMEM((group_rows, sw), BF16),
            pltpu.VMEM((group_rows, sw), BF16),
            pltpu.VMEM((group_rows, width), BF16),
            pltpu.VMEM((4 * rows, width), BF16),
            pltpu.VMEM((3, rows, width), BF16),
            pltpu.VMEM((rows, width), BF16),
            pltpu.VMEM((2, rows, width), BF16),
            pltpu.VMEM((rows, width), F32),
            pltpu.VMEM((rows, width), F32),
            pltpu.VMEM((rows, width), F32),
            pltpu.VMEM((rows, LANES), F32),
            pltpu.VMEM((16, width), F32),
            pltpu.VMEM((16, width), F32),
            pltpu.VMEM((8, qc), F32),
            pltpu.VMEM((E * 4 * R, 2 * uc), BF16),
            pltpu.VMEM((R, width), BF16),
            pltpu.SemaphoreType.DMA((6,)),
            pltpu.SemaphoreType.DMA((wires,)),
            pltpu.SemaphoreType.DMA((wires,)),
        ],
        compiler_params=pltpu.CompilerParams(
            collective_id=0, has_side_effects=True, vmem_limit_bytes=63 << 20
        ),
    )(x_ext, cot, table, small_pieces, qkv_pieces, dense_weight, ffin_pieces, ffout_pieces)
    result, d_tokens, small_grads, qkv_grad, dense_grad, ffin_grad, ffout_grad = results[:7]

    def unit_columns(pieces):
        return pieces.transpose(1, 0, 2).reshape(R, padded)[:, :hidden].astype(F32)

    grad_qkv = (
        qkv_grad.reshape(2, 2, 2, R, 3, my_heads, head_dim)
        .transpose(3, 4, 5, 1, 0, 2, 6)
        .reshape(R, 3 * width)
        .astype(F32)
    )
    small_grads = jnp.sum(small_grads.astype(F32), axis=0)[:, :R].T
    return (
        result.reshape(tokens.shape),
        d_tokens.reshape(tokens.shape),
        grad_qkv,
        dense_grad.astype(F32),
        jnp.concatenate(
            [unit_columns(ffin_grad[:, :, :uc]), unit_columns(ffin_grad[:, :, uc:])], axis=1
        ),
        unit_columns(ffout_grad),
        small_grads[:, :7],
        small_grads[:, 7:9],
    )


def solution(mesh):
    dp, fsdp = mesh.shape["dp"], mesh.shape["fsdp"]
    fine = Mesh(mesh.devices.reshape(dp // 2, 2, fsdp // 4, 2, 2), AXES)
    cube, flat = P(AXES, None, None), P(AXES, None)
    return jax.shard_map(
        on_device,
        mesh=fine,
        in_specs=(cube, cube) + (flat,) * 8,
        out_specs=(cube, cube) + (flat,) * 6,
        check_vma=False,
    )
```

```python
import functools
import math

import jax
import jax.numpy as jnp
import numpy as np
from jax import lax
from jax.experimental import pallas as pl
from jax.experimental.pallas import tpu as pltpu
from jax.sharding import Mesh
from jax.sharding import PartitionSpec as P

HEADS = 16
LAYERS = 24
MASKED_SCORE = -1e30
EPSILON = 1e-05
ROPE_BASE = 10000.0

AXES = ("a", "b", "e", "f", "c")
GROUP = 8
LANES = 128
SHARED = 6
DEVICE_MESH = pl.DeviceIdType.MESH
BF16 = jnp.bfloat16
F32 = jnp.float32
NT = (((1,), (1,)), ((), ()))
TN = (((0,), (0,)), ((), ()))


def dot(left, right, dims=(((1,), (0,)), ((), ()))):
    return lax.dot_general(left, right, dims, preferred_element_type=F32)


def span(start, size):
    return pl.ds(pl.multiple_of(start, size), size)


class Wires:
    def __init__(self, send_sem, recv_sem):
        self.send_sem, self.recv_sem, self.count = send_sem, recv_sem, 0

    def take(self, numbers=1):
        first = self.count
        self.count += numbers
        return first

    def send(self, number, source, target, device, condition=None):
        one = pltpu.make_async_remote_copy(
            src_ref=source,
            dst_ref=target,
            send_sem=self.send_sem.at[number],
            recv_sem=self.recv_sem.at[number],
            device_id=device,
            device_id_type=DEVICE_MESH,
        )
        when(condition, one.start)
        return condition, one

    def arrived(self, number, landing, condition=None):
        when(condition, pltpu.make_async_copy(landing, landing, self.recv_sem.at[number]).wait)


def when(condition, body):
    if condition is None:
        body()
    else:
        pl.when(condition)(body)


def sent(copies):
    for condition, one in copies:
        when(condition, one.wait_send)
    copies.clear()


def layer_kernel(
    sizes,
    len_ref,
    pre_ref,
    cot_ref,
    table_ref,
    x_ref,
    sp_ref,
    qp_ref,
    dp_ref,
    gp_ref,
    up_ref,
    op_ref,
    out_ref,
    gx_ref,
    os_ref,
    oq_ref,
    od_ref,
    og_ref,
    ou_ref,
    oo_ref,
    ys_ref,
    yq_ref,
    yd_ref,
    yg_ref,
    yu_ref,
    yo_ref,
    zs_ref,
    zq_ref,
    zd_ref,
    zg_ref,
    zu_ref,
    zo_ref,
    ws_ref,
    wq_ref,
    wd_ref,
    wg_ref,
    wu_ref,
    wo_ref,
    go_ref,
    xg_ref,
    hg_ref,
    dg_ref,
    uf_ref,
    mb_ref,
    du_ref,
    qk_ref,
    cx_ref,
    dc_ref,
    pb_ref,
    core_ref,
    stage_ref,
    relay_ref,
    land_ref,
    sum_ref,
    xh_ref,
    dr_ref,
    rstd_ref,
    valid_ref,
    bt_ref,
    sg_ref,
    qb_ref,
    tm_ref,
    td_ref,
    local_sem,
    send_sem,
    recv_sem,
):
    A, E, R, rows, width, sw, uc, larger, alpha, scale = sizes
    a, b, e, f, c = (lax.axis_index(axis) for axis in AXES)
    qc = 3 * sw
    all_rows = GROUP * rows
    half_rows = all_rows // 2
    slot = lambda bb, ff, cc: cc * 4 + bb * 2 + ff
    me = slot(b, f, c)
    my_rows = span(me * rows, rows)
    flip = lambda v, d: lax.rem(v + d, 2)
    rank = lambda aa, bb, ee, ff, cc: (((aa * 2 + bb) * E + ee) * 2 + ff) * 2 + cc
    wires = Wires(send_sem, recv_sem)
    peers = [(r // 4, r // 2 % 2, r % 2) for r in range(GROUP)]

    barrier = pltpu.get_barrier_semaphore()
    others = 0
    for da in range(A):
        for de in range(E):
            for db, df, dc in peers:
                if da + de + db + df + dc:
                    pl.semaphore_signal(
                        barrier,
                        inc=1,
                        device_id={
                            "a": lax.rem(a + da, A),
                            "b": flip(b, db),
                            "e": lax.rem(e + de, E),
                            "f": flip(f, df),
                            "c": flip(c, dc),
                        },
                        device_id_type=DEVICE_MESH,
                    )
                    others += 1
    pl.semaphore_wait(barrier, others)

    class Weight:
        def __init__(self, index, parts, pieces, buf, out, ylanding, zlanding):
            self.index, self.parts, self.pieces, self.buf, self.out = index, parts, pieces, buf, out
            self.ylanding, self.zlanding = ylanding, zlanding
            self.R = pieces.shape[1]
            self.copies = []
            take = lambda count: wires.take(count * len(parts))
            self.tp, self.z, self.y = take(GROUP), take(2 * (E - 1)), take(2 * E * (A - 1))
            self.gtp, self.gz, self.gy = take(GROUP), take(2 * (E - 1)), take(2 * (A - 1))

        def each(self, member, body):
            for k, (first, size, extra) in enumerate(self.parts):
                body(k, pl.ds(first, size), member < larger if extra else None)

        def send(self, first, number, source, target, device, member=me):
            def body(k, cols, condition):
                self.copies.append(
                    wires.send(
                        first + number * len(self.parts) + k,
                        source.at[:, cols],
                        target.at[:, cols],
                        device,
                        condition,
                    )
                )

            self.each(member, body)

        def arrived(self, first, number, landing, member=me):
            def body(k, cols, condition):
                wires.arrived(
                    first + number * len(self.parts) + k, landing.at[:, cols], condition
                )

            self.each(member, body)

        def line(self, aa, bb, ee, ff, cc):
            return span(rank(aa, bb, ee, ff, cc) * self.R, self.R)

        def block(self, aa, bb, ee):
            return span(((aa * 2 + bb) * E + ee) * 4 * self.R, 4 * self.R)

        def half(self, aa, bb):
            return span((aa * 2 + bb) * E * 4 * self.R, E * 4 * self.R)

        def piece(self, place):
            return self.pieces.at[place if self.pieces.shape[0] > 1 else 0]

        def own(self):
            return pltpu.make_async_copy(
                self.piece(me), self.buf.at[self.line(a, b, e, f, c)], local_sem.at[self.index]
            )

        def tp_send(self):
            self.own().start()
            for r in range(1, GROUP):
                db, df, dc = peers[r]
                bb, ff, cc = flip(b, db), flip(f, df), flip(c, dc)
                place = slot(bb, ff, cc)
                self.send(
                    self.tp,
                    r,
                    self.piece(place),
                    self.buf.at[self.line(a, b, e, f, c)],
                    {"b": bb, "f": ff, "c": cc},
                    place,
                )

        def tp_wait(self, db):
            for r in range(4 * db, 4 * db + 4):
                if r == 0:
                    self.own().wait()
                else:
                    _, df, dc = peers[r]
                    rows_ = self.line(a, flip(b, db), e, flip(f, df), flip(c, dc))
                    self.arrived(self.tp, r, self.buf.at[rows_])

        def z_send(self, db):
            rows_ = self.buf.at[self.block(a, flip(b, db), e)]
            for s in range(1, E):
                self.send(self.z, db * (E - 1) + s - 1, rows_, rows_, {"e": lax.rem(e + s, E)})

        def y_send(self, db, s):
            rows_ = self.buf.at[self.block(a, flip(b, db), lax.rem(e + E - s, E))]
            for t in range(1, A):
                number = (db * E + s) * (A - 1) + t - 1
                self.send(self.y, number, rows_, rows_, {"a": lax.rem(a + t, A)})

        def z_arrive(self, db):
            for s in range(1, E):
                rows_ = self.block(a, flip(b, db), lax.rem(e + E - s, E))
                self.arrived(self.z, db * (E - 1) + s - 1, self.buf.at[rows_])
                self.y_send(db, s)

        def y_arrive(self):
            for db in range(2):
                for s in range(E):
                    for t in range(1, A):
                        rows_ = self.block(
                            lax.rem(a + A - t, A), flip(b, db), lax.rem(e + E - s, E)
                        )
                        self.arrived(
                            self.y, (db * E + s) * (A - 1) + t - 1, self.buf.at[rows_]
                        )

        def add(self, landing, base, count):
            def load(k, cols, condition):
                copy = pltpu.make_async_copy(
                    landing.at[:, cols],
                    tm_ref.at[pl.ds(0, count), cols],
                    local_sem.at[SHARED + k],
                )
                when(condition, copy.start)

                def total():
                    copy.wait()

                    @pl.loop(0, count // 16)
                    def _(i):
                        here = pl.ds(pl.multiple_of(base + i * 16, 16), 16)
                        there = span(i * 16, 16)
                        self.buf[here, cols] = (
                            self.buf[here, cols].astype(F32) + tm_ref[there, cols].astype(F32)
                        ).astype(BF16)

                return lambda: when(condition, total)

            totals = []
            self.each(me, lambda *part: totals.append(load(*part)))
            for total in totals:
                total()

        def gy_send(self, db):
            for t in range(1, A):
                to = lax.rem(a + t, A)
                self.send(
                    self.gy,
                    db * (A - 1) + t - 1,
                    self.buf.at[self.half(to, flip(b, db))],
                    self.ylanding.at[t - 1, db],
                    {"a": to},
                )

        def gy_add(self, db):
            bb = flip(b, db)
            for t in range(1, A):
                landing = self.ylanding.at[t - 1, db]
                self.arrived(self.gy, db * (A - 1) + t - 1, landing)
                self.add(landing, (a * 2 + bb) * E * 4 * self.R, E * 4 * self.R)
            for s in range(1, E):
                to = lax.rem(e + s, E)
                self.send(
                    self.gz,
                    db * (E - 1) + s - 1,
                    self.buf.at[self.block(a, bb, to)],
                    self.zlanding.at[s - 1, db],
                    {"e": to},
                )

        def gz_add(self, db):
            bb = flip(b, db)
            for s in range(1, E):
                landing = self.zlanding.at[s - 1, db]
                self.arrived(self.gz, db * (E - 1) + s - 1, landing)
                self.add(landing, ((a * 2 + bb) * E + e) * 4 * self.R, 4 * self.R)
            for r in range(4 * db, 4 * db + 4):
                _, df, dc = peers[r]
                ff, cc = flip(f, df), flip(c, dc)
                rows_ = self.buf.at[self.line(a, bb, e, ff, cc)]
                if r == 0:
                    pltpu.make_async_copy(rows_, self.out.at[me], local_sem.at[self.index]).start()
                else:
                    self.send(self.gtp, r, rows_, self.out.at[me], {"b": bb, "f": ff, "c": cc})

        def g_end(self):
            for r in range(GROUP):
                db, df, dc = peers[r]
                if r == 0:
                    pltpu.make_async_copy(
                        self.buf.at[self.line(a, b, e, f, c)],
                        self.out.at[me],
                        local_sem.at[self.index],
                    ).wait()
                else:
                    place = slot(flip(b, db), flip(f, df), flip(c, dc))
                    self.arrived(self.gtp, r, self.out.at[place], place)

    tile = uc - LANES
    shares = [(0, tile, False), (tile, LANES, True)]
    s_w = Weight(0, [(0, LANES, False)], sp_ref, ws_ref, os_ref, ys_ref, zs_ref)
    q_w = Weight(1, [(0, qc, False)], qp_ref, wq_ref, oq_ref, yq_ref, zq_ref)
    g_w = Weight(2, shares, gp_ref, wg_ref, og_ref, yg_ref, zg_ref)
    u_w = Weight(3, shares, up_ref, wu_ref, ou_ref, yu_ref, zu_ref)
    o_w = Weight(4, shares, op_ref, wo_ref, oo_ref, yo_ref, zo_ref)

    def remote(source, landing, send, recv, target):
        return pltpu.make_async_remote_copy(
            src_ref=source,
            dst_ref=landing,
            send_sem=send_sem.at[send],
            recv_sem=recv_sem.at[recv],
            device_id=target,
            device_id_type=DEVICE_MESH,
        )

    class Dense:
        def __init__(self):
            self.pieces = wd_ref.shape[0] // R
            self.first = wires.take(self.pieces)
            self.push = wires.take(1)
            self.zs = wires.take(self.pieces * (E - 1))
            self.ys = wires.take(self.pieces * (A - 1))
            self.gy = wires.take(self.pieces * (A - 1))
            self.gz = wires.take(self.pieces * (E - 1))
            self.back = wires.take(1)
            self.back_sends = wires.take(self.pieces)
            self.owners = []
            for piece in range(self.pieces):
                i, offset = piece * R // LANES, piece * R % LANES
                owner = ((i * 8 + b * 4 + c * 2 + f) * LANES + offset) // R
                self.owners.append(
                    {
                        "a": owner // (8 * E),
                        "b": lax.rem(owner // (4 * E), 2),
                        "e": lax.rem(owner // 4, E),
                        "f": lax.rem(owner // 2, 2),
                        "c": lax.rem(owner, 2),
                    }
                )

        def rows(self, piece):
            return wd_ref.at[pl.ds(piece * R, R)]

        def each(self, test, body):
            for piece, owner in enumerate(self.owners):
                same_a, same_e = owner["a"] == a, owner["e"] == e

                @pl.when(test(same_a, same_e))
                def _():
                    body(piece, owner)

        def local_or_remote(self, target, source, landing, send, recv, start):
            here = target["b"] == b
            for axis, mine in (("f", f), ("c", c)):
                here = here & (target[axis] == mine)
            away = remote(source, landing, send, recv, target)

            @pl.when(here)
            def _():
                if start:
                    pltpu.make_async_copy(source, landing, recv_sem.at[recv]).start()

            @pl.when(jnp.logical_not(here))
            def _():
                away.start() if start else away.wait_send()

        def out(self, start):
            first_row = rank(a, b, e, f, c) * R
            head = first_row // LANES
            piece = (head // 8) * (LANES // R) + lax.rem(first_row, LANES) // R
            target = {
                "b": lax.rem(head // 4, 2),
                "f": lax.rem(head, 2),
                "c": lax.rem(head // 2, 2),
            }
            landing = wd_ref.at[span(piece * R, R)]
            self.local_or_remote(target, dp_ref, landing, self.push, self.first + piece, start)

        def z(self, piece, s):
            rows_ = self.rows(piece)
            number = self.zs + piece * (E - 1) + s - 1
            return remote(rows_, rows_, number, self.first + piece, {"e": lax.rem(e + s, E)})

        def y(self, piece, t):
            rows_ = self.rows(piece)
            number = self.ys + piece * (A - 1) + t - 1
            return remote(rows_, rows_, number, self.first + piece, {"a": lax.rem(a + t, A)})

        def arrived(self, piece, _=None):
            wires.arrived(self.first + piece, self.rows(piece))

        def z_send(self):
            def body(piece, owner):
                self.arrived(piece)
                for s in range(1, E):
                    self.z(piece, s).start()

            self.each(lambda same_a, same_e: same_a & same_e, body)

        def y_send(self):
            self.each(lambda same_a, same_e: same_a & jnp.logical_not(same_e), self.arrived)

            def body(piece, owner):
                for t in range(1, A):
                    self.y(piece, t).start()

            self.each(lambda same_a, same_e: same_a, body)

        def y_arrive(self):
            self.each(lambda same_a, same_e: jnp.logical_not(same_a), self.arrived)

        def sent(self):
            self.out(False)

            def over_z(piece, owner):
                for s in range(1, E):
                    self.z(piece, s).wait_send()

            def over_y(piece, owner):
                for t in range(1, A):
                    self.y(piece, t).wait_send()

            self.each(lambda same_a, same_e: same_a & same_e, over_z)
            self.each(lambda same_a, same_e: same_a, over_y)

        def g_y(self, piece, t):
            to = lax.rem(a + t, A)
            number = self.gy + piece * (A - 1) + t - 1
            copy = remote(self.rows(piece), yd_ref.at[t - 1, piece], number, number, {"a": to})
            return to, copy

        def gy_send(self, start=True):
            for piece, owner in enumerate(self.owners):
                for t in range(1, A):
                    to, copy = self.g_y(piece, t)

                    @pl.when(owner["a"] == to)
                    def _():
                        copy.start() if start else copy.wait_send()

        def add(self, landing, piece):
            load = pltpu.make_async_copy(landing, td_ref, local_sem.at[SHARED])
            load.start()
            load.wait()

            @pl.loop(0, R // 16)
            def _(i):
                here, there = span(piece * R + i * 16, 16), span(i * 16, 16)
                wd_ref[here, :] = (
                    wd_ref[here, :].astype(F32) + td_ref[there, :].astype(F32)
                ).astype(BF16)

        def g_z(self, piece, s):
            to = lax.rem(e + s, E)
            number = self.gz + piece * (E - 1) + s - 1
            copy = remote(self.rows(piece), zd_ref.at[s - 1, piece], number, number, {"e": to})
            return to, copy

        def gz_send(self, start=True):
            for piece, owner in enumerate(self.owners):
                for s in range(1, E):
                    to, copy = self.g_z(piece, s)

                    @pl.when((owner["a"] == a) & (owner["e"] == to))
                    def _():
                        copy.start() if start else copy.wait_send()

        def gy_add(self):
            def body(piece, owner):
                for t in range(1, A):
                    landing = yd_ref.at[t - 1, piece]
                    wires.arrived(self.gy + piece * (A - 1) + t - 1, landing)
                    self.add(landing, piece)

            self.each(lambda same_a, same_e: same_a, body)
            self.gz_send()

        def home(self, piece, owner, start):
            target = {axis: owner[axis] for axis in ("b", "f", "c")}
            self.local_or_remote(
                target, self.rows(piece), od_ref, self.back_sends + piece, self.back, start
            )

        def gz_add(self):
            def body(piece, owner):
                for s in range(1, E):
                    landing = zd_ref.at[s - 1, piece]
                    wires.arrived(self.gz + piece * (E - 1) + s - 1, landing)
                    self.add(landing, piece)
                self.home(piece, owner, True)

            self.each(lambda same_a, same_e: same_a & same_e, body)

        def g_end(self):
            wires.arrived(self.back, od_ref)
            self.gy_send(False)
            self.gz_send(False)
            self.each(
                lambda same_a, same_e: same_a & same_e,
                lambda piece, owner: self.home(piece, owner, False),
            )

    dense = Dense()

    to_b, to_f, to_c = {"b": 1 - b}, {"f": 1 - f}, {"c": 1 - c}
    nb, nf, dg = slot(1 - b, f, c), slot(b, 1 - f, c), slot(1 - b, 1 - f, c)

    class Gather:
        def __init__(self, buf, lean):
            self.buf, self.first, self.copies, self.lean = buf, wires.take(10), [], lean

        def part(self, place, which):
            if which is None:
                return self.buf.at[span(place * rows, rows)]
            return self.buf.at[span(place * rows + which * (rows // 2), rows // 2)]

        def copy(self, number, place, which, device):
            here = self.part(place, which)
            self.copies.append(wires.send(self.first + number, here, here, device))

        def landed(self, number, place, which):
            wires.arrived(self.first + number, self.part(place, which))

        def start(self):
            self.copy(0, me, 0, to_b)
            self.copy(1, me, 1, to_f)
            self.copy(2, me, 1, to_b)
            self.copy(3, me, 0, to_f)
            self.copy(4, me, None, to_c)

        def relay(self):
            if self.lean:
                self.landed(1, nf, 1)
                self.copy(6, nf, 1, to_b)
                self.landed(3, nf, 0)
                self.copy(5, nf, 0, to_b)
                self.copy(8, nf, None, to_c)
                self.landed(0, nb, 0)
                self.landed(2, nb, 1)
                self.copy(7, nb, None, to_c)
                return
            self.landed(0, nb, 0)
            self.copy(5, nb, 0, to_f)
            self.landed(1, nf, 1)
            self.copy(6, nf, 1, to_b)
            self.landed(2, nb, 1)
            self.copy(7, nb, None, to_c)
            self.landed(3, nf, 0)
            self.copy(8, nf, None, to_c)

        def finish(self):
            self.landed(5, dg, 0)
            self.landed(6, dg, 1)
            self.copy(9, dg, None, to_c)
            other = 1 - c
            self.landed(4, slot(b, f, other), None)
            self.landed(7, slot(1 - b, f, other), None)
            self.landed(8, slot(b, 1 - f, other), None)
            self.landed(9, slot(1 - b, 1 - f, other), None)

    step = 16
    places = [(1 - b, 1 - f), (1 - b, f), (b, 1 - f), (b, f)]

    def accumulate(target, at, count, terms):
        @pl.loop(0, count // step)
        def _(i):
            window = pl.ds(pl.multiple_of(at + i * step, step), step)
            total = terms[0][window, :].astype(F32)
            for term in terms[1:]:
                total = total + term[window, :].astype(F32)
            target[window, :] = total.astype(target.dtype)

    def scatter(multiply, lean, early=None, late=None):
        first, copies = wires.take(10), []

        def send(*copy):
            copies.append(wires.send(*copy))

        multiply((1 - c) * half_rows, half_rows)
        for k, (bb, ff) in enumerate(places):
            send(
                first + k,
                pb_ref.at[span(slot(bb, ff, 1 - c) * rows, rows)],
                core_ref.at[pl.ds(k * rows, rows)],
                to_c,
            )
        multiply(c * half_rows, half_rows)
        own = [pb_ref.at[span(slot(bb, ff, c) * rows, rows)] for bb, ff in places]
        core = [core_ref.at[pl.ds(k * rows, rows)] for k in range(4)]
        mid = rows // 2
        low, high = pl.ds(0, mid), pl.ds(mid, mid)
        early, late = (hook or (lambda: None) for hook in (early, late))
        wires.arrived(first, core[0])
        accumulate(stage_ref.at[0], 0, rows, [own[0], core[0]])
        if lean:
            send(first + 4, stage_ref.at[0], relay_ref, to_b)
            wires.arrived(first + 1, core[1])
            accumulate(stage_ref.at[1], 0, rows, [own[1], core[1]])
            send(first + 6, stage_ref.at[1], land_ref.at[0], to_b)
            early()
            wires.arrived(first + 2, core[2])
            wires.arrived(first + 4, relay_ref)
            accumulate(stage_ref.at[2], 0, rows, [own[2], core[2], relay_ref])
            send(first + 7, stage_ref.at[2], land_ref.at[1], to_f)
            late()
            wires.arrived(first + 3, core[3])
            wires.arrived(first + 6, land_ref.at[0])
            wires.arrived(first + 7, land_ref.at[1])
        else:
            send(first + 4, stage_ref.at[0, low], relay_ref.at[low], to_b)
            send(first + 5, stage_ref.at[0, high], relay_ref.at[high], to_f)
            wires.arrived(first + 1, core[1])
            accumulate(stage_ref.at[1], 0, mid, [own[1], core[1]])
            send(first + 6, stage_ref.at[1, low], land_ref.at[0, low], to_b)
            wires.arrived(first + 2, core[2])
            accumulate(stage_ref.at[2], mid, mid, [own[2], core[2]])
            send(first + 7, stage_ref.at[2, high], land_ref.at[1, high], to_f)
            early()
            wires.arrived(first + 5, relay_ref.at[high])
            accumulate(stage_ref.at[1], mid, mid, [own[1], core[1], relay_ref])
            send(first + 8, stage_ref.at[1, high], land_ref.at[0, high], to_b)
            wires.arrived(first + 4, relay_ref.at[low])
            accumulate(stage_ref.at[2], 0, mid, [own[2], core[2], relay_ref])
            send(first + 9, stage_ref.at[2, low], land_ref.at[1, low], to_f)
            late()
            wires.arrived(first + 3, core[3])
            wires.arrived(first + 6, land_ref.at[0, low])
            wires.arrived(first + 7, land_ref.at[1, high])
            wires.arrived(first + 8, land_ref.at[0, high])
            wires.arrived(first + 9, land_ref.at[1, low])
        accumulate(sum_ref, 0, rows, [own[3], core[3], land_ref.at[0], land_ref.at[1]])
        sent(copies)

    def blocks(count_m, count_n, body):
        @pl.loop(0, count_m * count_n)
        def _(k):
            body(k // count_n, lax.rem(k, count_n))

    def onto_partial(*terms):
        def multiply(first, count):
            def body(m, n):
                here = pl.ds(pl.multiple_of(first, half_rows) + m * 512, 512)
                there = span(n * 512, 512)
                total = sum(dot(left[here, :], weight[there, :], NT) for left, weight in terms)
                pb_ref[here, there] = total.astype(BF16)

            blocks(count // 512, width // 512, body)

        return multiply

    q_w.tp_send()
    s_w.tp_send()
    dense.out(True)
    own_x = pltpu.make_async_copy(
        x_ref.at[0], xg_ref.at[my_rows, pl.ds(0, width)], local_sem.at[5]
    )
    own_x.start()
    sg_ref[...] = jnp.zeros_like(sg_ref)

    @pl.when(me >= larger)
    def _():
        for weight in (g_w, u_w, o_w):
            weight.buf[:, tile:] = jnp.zeros((width, LANES), BF16)

    at = lax.broadcasted_iota(jnp.int32, (rows, LANES), 0)
    lane = lax.broadcasted_iota(jnp.int32, (rows, LANES), 1)
    docs = len_ref.shape[1]
    key, prefix_at, local_pos, valid, first = at + docs, at * 0, at * 0, at < 0, 0
    for k in range(docs):
        last = first + len_ref[0, k]
        member = (at >= first) & (at < last)
        key = jnp.where(member, k, key)
        prefix_at = jnp.where(member, pre_ref[0, k], prefix_at)
        local_pos = jnp.where(member, at - first, local_pos)
        valid = valid | member
        first = last
    info = jnp.where(lane == 0, key, jnp.where(lane == 1, prefix_at, local_pos))
    xg_ref[my_rows, width:] = info.astype(F32).astype(BF16)
    valid_ref[...] = jnp.where(valid, 1.0, 0.0)

    tokens = Gather(xg_ref, True)
    for db in range(2):
        q_w.tp_wait(db)
        q_w.z_send(db)
        q_w.y_send(db, 0)
    own_x.wait()
    tokens.start()
    g_w.tp_send()
    for db in range(2):
        s_w.tp_wait(db)
        s_w.z_send(db)
        s_w.y_send(db, 0)
    dense.z_send()
    u_w.tp_send()
    q_w.z_arrive(0)
    tokens.relay()
    g_w.tp_wait(0)
    g_w.z_send(0)
    g_w.y_send(0, 0)
    q_w.z_arrive(1)
    s_w.z_arrive(0)
    s_w.z_arrive(1)
    dense.y_send()
    g_w.tp_wait(1)
    g_w.z_send(1)
    g_w.y_send(1, 0)
    tokens.finish()
    o_w.tp_send()
    s_w.y_arrive()
    q_w.y_arrive()

    lane = lane[0:16, :]

    @pl.loop(0, width // LANES)
    def _(k):
        line = jnp.zeros((16, LANES), F32)
        for j in range(LANES // R):
            part = ws_ref[span((k * (LANES // R) + j) * 16, 16), :].astype(F32)
            if j:
                part = pltpu.roll(part, j * R, axis=1)
            line = jnp.where(lane // R == j, part, line)
        bt_ref[:, span(k * LANES, LANES)] = line

    heads = [i * 8 + b * 4 + c * 2 + f for i in range(sw // LANES)]
    for t in range(3):
        for i, number in enumerate(heads):
            at = t * sw + i * LANES
            qb_ref[0:1, at : at + LANES] = bt_ref[t : t + 1, span(number * LANES, LANES)]

    def projection(m, n):
        here, cols = span(m * 512, 512), span(n * sw, sw)
        uf_ref[here, cols] = (
            dot(xg_ref[here, 0:width], wq_ref[:, cols]) + qb_ref[0:1, cols]
        )

    blocks(all_rows // 512, 3, projection)

    row_at = lax.broadcasted_iota(jnp.int32, (rows, rows), 0)
    col_at = lax.broadcasted_iota(jnp.int32, (rows, rows), 1)

    def sequence(s):
        here = span(s * rows, rows)
        info = xg_ref[here, width : width + LANES].astype(F32)
        turned = info.T
        allowed = (info[:, 0:1] == turned[0:1, :]) & (
            (turned[2:3, :] < info[:, 1:2]) | (col_at <= row_at)
        )
        picked = (info[:, 2:3] == col_at.astype(F32)).astype(BF16)
        parts = dot(picked, table_ref[...])
        cos_sin = parts[:, 0:LANES] + parts[:, LANES : 2 * LANES] + parts[:, 2 * LANES :]
        swapped = pltpu.roll(cos_sin, LANES // 2, axis=1)
        first = col_at < LANES // 2
        cosine = jnp.where(first, cos_sin, swapped)
        sine = jnp.where(first, -swapped, cos_sin)
        return here, allowed, cosine, sine

    def turn(value, cosine, sine):
        return value * cosine + pltpu.roll(value, LANES // 2, axis=1) * sine

    def softmax(q, k, allowed):
        scores = jnp.where(allowed, scale * dot(q, k, NT), MASKED_SCORE)
        power = jnp.exp(scores - jnp.max(scores, axis=1, keepdims=True))
        return power / jnp.sum(power, axis=1, keepdims=True)

    @pl.loop(0, GROUP)
    def _(s):
        here, allowed, cosine, sine = sequence(s)
        for i in range(sw // LANES):
            cols = [pl.ds(t * sw + i * LANES, LANES) for t in range(3)]
            q = turn(uf_ref[here, cols[0]], cosine, sine).astype(BF16)
            k = turn(uf_ref[here, cols[1]], cosine, sine).astype(BF16)
            v = uf_ref[here, cols[2]].astype(BF16)
            qk_ref[here, cols[0]] = q
            qk_ref[here, cols[1]] = k
            qk_ref[here, cols[2]] = v
            probs = softmax(q, k, allowed).astype(BF16)
            cx_ref[here, i * LANES : (i + 1) * LANES] = dot(probs, v).astype(BF16)

    u_w.tp_wait(0)
    u_w.tp_wait(1)
    u_w.z_send(0)
    u_w.z_send(1)
    g_w.z_arrive(0)
    dense.y_arrive()

    def dense_partial(first, count):
        def body(m, n):
            here = pl.ds(pl.multiple_of(first, half_rows) + m * 512, 512)
            cols = span(n * 512, 512)
            pb_ref[here, cols] = dot(cx_ref[here, :], wd_ref[:, cols]).astype(BF16)

        blocks(count // 512, width // 512, body)

    def more_units():
        u_w.y_send(0, 0)
        u_w.y_send(1, 0)

    scatter(dense_partial, True, lambda: g_w.z_arrive(1), more_units)
    for db in range(2):
        o_w.tp_wait(db)
        o_w.z_send(db)

    def row_loop(body):
        @pl.loop(0, rows // 16)
        def _(i):
            body(span(i * 16, 16), span(me * rows + i * 16, 16))

    def normalize(value):
        centered = value - jnp.mean(value, axis=1, keepdims=True)
        rstd = lax.rsqrt(jnp.mean(centered * centered, axis=1, keepdims=True) + EPSILON)
        return centered * rstd, rstd

    def first_norm(here, there):
        value = (
            alpha * xg_ref[there, 0:width].astype(F32) + sum_ref[here, :] + bt_ref[3:4, :]
        )
        unit, rstd = normalize(value)
        xh_ref[here, :] = unit
        rstd_ref[here, :] = jnp.broadcast_to(rstd, (16, LANES))
        hg_ref[there, :] = (unit * bt_ref[7:8, :] + bt_ref[4:5, :]).astype(BF16)

    row_loop(first_norm)
    normed = Gather(hg_ref, True)
    normed.start()
    u_w.z_arrive(0)
    normed.relay()
    o_w.y_send(0, 0)
    o_w.y_send(1, 0)
    u_w.z_arrive(1)
    normed.finish()
    g_w.y_arrive()
    u_w.y_arrive()

    def units(m, n):
        here = span(m * 512, 512)
        gate_cols = span(n * 256, 256)
        up_cols = span(uc + n * 256, 256)
        left = hg_ref[here, :]
        gate = dot(left, wg_ref[:, gate_cols])
        up = dot(left, wu_ref[:, gate_cols])
        cdf = 0.5 * (1.0 + lax.erf(gate * (0.5**0.5)))
        density = jnp.exp(-0.5 * gate * gate) * (1.0 / math.sqrt(2.0 * math.pi))
        act = gate * cdf
        mb_ref[here, gate_cols] = (act * up).astype(BF16)
        uf_ref[here, gate_cols] = (cdf + gate * density) * up
        uf_ref[here, up_cols] = act

    blocks(all_rows // 512, uc // 256, units)
    o_w.z_arrive(0)
    o_w.z_arrive(1)
    o_w.y_arrive()
    scatter(onto_partial((mb_ref, wo_ref)), False)

    def add_row(row, value):
        sg_ref[row : row + 1, :] += jnp.sum(value, axis=0, keepdims=True)

    def norm_back(grad, gain, unit, rstd):
        scaled = grad * gain
        return rstd * (
            scaled
            - jnp.mean(scaled, axis=1, keepdims=True)
            - unit * jnp.mean(scaled * unit, axis=1, keepdims=True)
        )

    def second_norm(here, there):
        normed_one = xh_ref[here, :] * bt_ref[7:8, :] + bt_ref[4:5, :]
        unit, rstd = normalize(alpha * normed_one + sum_ref[here, :] + bt_ref[5:6, :])
        out_ref[here, :] = (unit * bt_ref[8:9, :] + bt_ref[6:7, :]).astype(BF16)
        grad = cot_ref[0, here, :].astype(F32) * valid_ref[here, 0:1]
        back = norm_back(grad, bt_ref[8:9, :], unit, rstd)
        low = back.astype(BF16)
        dr_ref[here, :] = back
        dg_ref[there, :] = low
        add_row(5, low.astype(F32))
        add_row(6, grad)
        add_row(8, grad * unit)

    row_loop(second_norm)
    branch = Gather(dg_ref, False)
    branch.start()
    branch.relay()
    branch.finish()

    def units_back(m, n):
        here = span(m * 512, 512)
        gate_cols, up_cols = span(n * 256, 256), span(uc + n * 256, 256)
        grad = dot(dg_ref[here, :], wo_ref[:, gate_cols])
        du_ref[here, gate_cols] = (uf_ref[here, gate_cols] * grad).astype(BF16)
        du_ref[here, up_cols] = (uf_ref[here, up_cols] * grad).astype(BF16)

    def weight_grad(left, right, target, cols, bn):
        def body(m, n):
            here, there = span(m * 512, 512), span(n * bn, bn)
            target[here, there] = dot(left[:, here], right[:, there], TN).astype(BF16)

        blocks(width // 512, cols // bn, body)

    sent(o_w.copies)
    weight_grad(dg_ref, mb_ref, go_ref, uc, uc)
    o_w.buf = go_ref
    o_w.gy_send(0)
    o_w.gy_send(1)
    blocks(all_rows // 512, uc // 256, units_back)

    du_gate = du_ref.at[:, pl.ds(0, uc)]
    du_up = du_ref.at[:, pl.ds(uc, uc)]

    def in_grad():
        for weight, right in ((g_w, du_gate), (u_w, du_up)):
            sent(weight.copies)
            weight_grad(hg_ref, right, weight.buf, uc, uc)
            weight.gy_send(0)
            weight.gy_send(1)

    sent(branch.copies)
    scatter(
        onto_partial((du_gate, wg_ref), (du_up, wu_ref)), False, in_grad, lambda: o_w.gy_add(0)
    )

    def first_norm_back(here, there):
        grad = alpha * dr_ref[here, :] + sum_ref[here, :]
        unit = xh_ref[here, :]
        back = norm_back(grad, bt_ref[7:8, :], unit, rstd_ref[here, 0:1])
        low = back.astype(BF16)
        dr_ref[here, :] = back
        dg_ref[there, :] = low
        add_row(3, low.astype(F32))
        add_row(4, grad)
        add_row(7, grad * unit)

    row_loop(first_norm_back)
    attended = Gather(dg_ref, True)
    attended.start()
    o_w.gy_add(1)
    attended.relay()
    g_w.gy_add(0)
    attended.finish()

    def context_back(m, n):
        here = span(m * 512, 512)
        dc_ref[here, :] = dot(dg_ref[here, :], wd_ref[...], NT).astype(BF16)

    blocks(all_rows // 512, 1, context_back)

    def dense_grad(m, n):
        cols = span(n * 512, 512)
        wd_ref[:, cols] = dot(cx_ref[...], dg_ref[:, cols], TN).astype(BF16)

    dense.sent()
    blocks(1, width // 512, dense_grad)
    dense.gy_send()
    g_w.gy_add(1)

    @pl.loop(0, GROUP)
    def _(s):
        here, allowed, cosine, sine = sequence(s)
        for i, number in enumerate(heads):
            cols = [pl.ds(t * sw + i * LANES, LANES) for t in range(3)]
            q, k, v = (qk_ref[here, one] for one in cols)
            grad = dc_ref[here, i * LANES : (i + 1) * LANES]
            probs = softmax(q, k, allowed)
            d_probs = dot(grad, v, NT)
            d_value = dot(probs.astype(BF16), grad, TN)
            d_scores = probs * (d_probs - jnp.sum(probs * d_probs, axis=1, keepdims=True))
            low = jnp.where(allowed, d_scores, 0.0).astype(BF16)
            d_query = turn(scale * dot(low, k), cosine, -sine)
            d_key = turn(scale * dot(low, q, TN), cosine, -sine)
            for t, value in enumerate((d_query, d_key, d_value)):
                value = value.astype(BF16)
                mb_ref[here, cols[t]] = value
                lanes = span(number * LANES, LANES)
                sg_ref[t : t + 1, lanes] += jnp.sum(value.astype(F32), axis=0, keepdims=True)

    u_w.gy_add(0)

    def qkv_grad():
        sent(q_w.copies)
        weight_grad(xg_ref, mb_ref, wq_ref, qc, qc)

        q_w.gy_send(0)
        q_w.gy_send(1)
        sent(s_w.copies)

        @pl.loop(0, width // LANES)
        def _(k):
            line = sg_ref[:, span(k * LANES, LANES)]
            for j in range(LANES // R):
                part = line if j == 0 else pltpu.roll(line, LANES - j * R, axis=1)
                ws_ref[span((k * (LANES // R) + j) * 16, 16), :] = part.astype(BF16)

        s_w.gy_send(0)
        s_w.gy_send(1)

    scatter(onto_partial((mb_ref, wq_ref)), True, qkv_grad, lambda: u_w.gy_add(1))

    def tokens_back(here, there):
        gx_ref[here, :] = alpha * dr_ref[here, :] + sum_ref[here, :]

    row_loop(tokens_back)

    dense.gy_add()
    o_w.gz_add(0)
    o_w.gz_add(1)
    q_w.gy_add(0)
    q_w.gy_add(1)
    s_w.gy_add(0)
    s_w.gy_add(1)
    for db in range(2):
        g_w.gz_add(db)
    for db in range(2):
        u_w.gz_add(db)
    dense.gz_add()
    for db in range(2):
        q_w.gz_add(db)
    for db in range(2):
        s_w.gz_add(db)
    for weight in (dense, o_w, g_w, u_w, q_w, s_w):
        weight.g_end()
    for flow in (q_w, g_w, u_w, o_w, s_w, tokens, normed, attended):
        sent(flow.copies)


def on_device(
    tokens,
    cotangent,
    lengths,
    prefix,
    qkv_weight,
    dense_weight,
    ffin_weight,
    ffout_weight,
    biases,
    norm_gains,
):
    _, rows, width = tokens.shape
    A, E = lax.axis_size("a"), lax.axis_size("e")
    R = qkv_weight.shape[0]
    head_dim = width // HEADS
    my_heads = HEADS // GROUP
    hidden = ffout_weight.shape[1]
    tiles = -(-hidden // LANES)
    larger = tiles % GROUP
    uc = (tiles // GROUP + 1) * LANES
    smaller = uc - LANES
    sw = my_heads * head_dim
    qc = 3 * sw

    inverse = np.float32(ROPE_BASE) ** (
        -np.arange(head_dim // 2, dtype=np.float32) * np.float32(2.0 / head_dim)
    )
    angles = np.arange(rows, dtype=np.float32)[:, None] * inverse.astype(np.float32)
    rest = np.concatenate([np.cos(angles), np.sin(angles)], axis=1).astype(np.float32)
    terms = []
    for _ in range(3):
        terms.append(rest.astype(BF16))
        rest = rest - terms[-1].astype(np.float32)
    table = jnp.asarray(np.concatenate(terms, axis=1))

    qkv_pieces = (
        qkv_weight.reshape(R, 3, my_heads, 2, 2, 2, head_dim)
        .transpose(4, 3, 5, 0, 1, 2, 6)
        .reshape(GROUP, R, qc)
    )
    small = jnp.concatenate([biases, norm_gains], axis=1).T
    small = jnp.pad(small, ((0, 16 - small.shape[0]), (0, LANES - R)))
    small_pieces = small[None]

    def unit_pieces(weight):
        wide = jnp.pad(weight, ((0, 0), (0, tiles * LANES - hidden)))
        first = wide[:, : larger * uc].reshape(R, larger, uc)
        rest = wide[:, larger * uc :].reshape(R, GROUP - larger, smaller)
        rest = jnp.pad(rest, ((0, 0), (0, 0), (0, LANES)))
        return jnp.concatenate([first, rest], axis=1).transpose(1, 0, 2)

    gate_pieces = unit_pieces(ffin_weight[:, :hidden])
    up_pieces = unit_pieces(ffin_weight[:, hidden:])
    ffout_pieces = unit_pieces(ffout_weight)

    wires = 8 * (2 * GROUP + 4 * (E - 1) + 2 * E * (A - 1) + 2 * (A - 1))
    wires += (sw // R) * 2 * (A + E) + 2 + 8 * 10
    group_rows = GROUP * rows
    sizes = (A, E, R, rows, width, sw, uc, larger, (2.0 * LAYERS) ** 0.5, head_dim ** (-0.5))
    shape = jax.ShapeDtypeStruct
    anywhere, vmem = pl.BlockSpec(memory_space=pl.ANY), pl.BlockSpec(memory_space=pltpu.VMEM)
    landings = [(64, LANES), (4 * R, qc), None] + [(4 * R, uc)] * 3
    dense_landing = (sw // R, R, width)
    results = pl.pallas_call(
        functools.partial(layer_kernel, sizes),
        out_shape=[
            shape((rows, width), BF16),
            shape((rows, width), F32),
            shape((GROUP, 16, LANES), BF16),
            shape((GROUP, R, qc), BF16),
            shape((R, width), BF16),
        ]
        + [shape((GROUP, R, uc), BF16)] * 3
        + [
            shape((A - 1,) + ((2, E * one[0], one[1]) if one else dense_landing), BF16)
            for one in landings
        ]
        + [
            shape((E - 1,) + ((2,) + one if one else dense_landing), BF16)
            for one in landings
        ],
        in_specs=[pl.BlockSpec(memory_space=pltpu.SMEM)] * 2 + [vmem] * 2 + [anywhere] * 7,
        out_specs=[vmem, vmem] + [anywhere] * 18,
        scratch_shapes=[
            pltpu.VMEM((width // R * 16, LANES), BF16),
            pltpu.VMEM((width, qc), BF16),
            pltpu.VMEM((sw, width), BF16),
            pltpu.VMEM((width, uc), BF16),
            pltpu.VMEM((width, uc), BF16),
            pltpu.VMEM((width, uc), BF16),
            pltpu.VMEM((width, uc), BF16),
            pltpu.VMEM((group_rows, width + LANES), BF16),
            pltpu.VMEM((group_rows, width), BF16),
            pltpu.VMEM((group_rows, width), BF16),
            pltpu.VMEM((group_rows, 2 * uc), F32),
            pltpu.VMEM((group_rows, uc), BF16),
            pltpu.VMEM((group_rows, 2 * uc), BF16),
            pltpu.VMEM((group_rows, qc), BF16),
            pltpu.VMEM((group_rows, sw), BF16),
            pltpu.VMEM((group_rows, sw), BF16),
            pltpu.VMEM((group_rows, width), BF16),
            pltpu.VMEM((4 * rows, width), BF16),
            pltpu.VMEM((3, rows, width), BF16),
            pltpu.VMEM((rows, width), BF16),
            pltpu.VMEM((2, rows, width), BF16),
            pltpu.VMEM((rows, width), F32),
            pltpu.VMEM((rows, width), F32),
            pltpu.VMEM((rows, width), F32),
            pltpu.VMEM((rows, LANES), F32),
            pltpu.VMEM((rows, LANES), F32),
            pltpu.VMEM((16, width), F32),
            pltpu.VMEM((16, width), F32),
            pltpu.VMEM((8, qc), F32),
            pltpu.VMEM((E * 4 * R, max(uc, qc)), BF16),
            pltpu.VMEM((R, width), BF16),
            pltpu.SemaphoreType.DMA((SHARED + 2,)),
            pltpu.SemaphoreType.DMA((wires,)),
            pltpu.SemaphoreType.DMA((wires,)),
        ],
        compiler_params=pltpu.CompilerParams(
            collective_id=0, has_side_effects=True, vmem_limit_bytes=63 << 20
        ),
    )(
        lengths,
        prefix,
        cotangent,
        table,
        tokens,
        small_pieces,
        qkv_pieces,
        dense_weight,
        gate_pieces,
        up_pieces,
        ffout_pieces,
    )
    result, d_tokens, small_grads, qkv_grad, dense_grad, gate_grad, up_grad, ffout_grad = results[:8]

    def unit_columns(pieces):
        turned = pieces.transpose(1, 0, 2)
        first = turned[:, :larger].reshape(R, larger * uc)
        rest = turned[:, larger:, :smaller].reshape(R, (GROUP - larger) * smaller)
        return jnp.concatenate([first, rest], axis=1)[:, :hidden].astype(F32)

    grad_qkv = (
        qkv_grad.reshape(2, 2, 2, R, 3, my_heads, head_dim)
        .transpose(3, 4, 5, 1, 0, 2, 6)
        .reshape(R, 3 * width)
        .astype(F32)
    )
    small_grads = jnp.sum(small_grads.astype(F32), axis=0)[:, :R].T
    return (
        result.reshape(tokens.shape),
        d_tokens.reshape(tokens.shape),
        grad_qkv,
        dense_grad.astype(F32),
        jnp.concatenate(
            [unit_columns(gate_grad), unit_columns(up_grad)], axis=1
        ),
        unit_columns(ffout_grad),
        small_grads[:, :7],
        small_grads[:, 7:9],
    )


def solution(mesh):
    dp, fsdp = mesh.shape["dp"], mesh.shape["fsdp"]
    fine = Mesh(mesh.devices.reshape(dp // 2, 2, fsdp // 4, 2, 2), AXES)
    cube, flat = P(AXES, None, None), P(AXES, None)
    return jax.shard_map(
        on_device,
        mesh=fine,
        in_specs=(cube, cube) + (flat,) * 8,
        out_specs=(cube, cube) + (flat,) * 6,
        check_vma=False,
    )
```

```python
import functools
import math

import jax
import jax.numpy as jnp
import numpy as np
from jax import lax
from jax.experimental import pallas as pl
from jax.experimental.pallas import tpu as pltpu
from jax.sharding import Mesh
from jax.sharding import PartitionSpec as P

HEADS = 16
LAYERS = 24
MASKED_SCORE = -1e30
EPSILON = 1e-05
ROPE_BASE = 10000.0

AXES = ("a", "b", "e", "f", "c")
GROUP = 8
LANES = 128
SHARED = 6
DEVICE_MESH = pl.DeviceIdType.MESH
BF16 = jnp.bfloat16
F32 = jnp.float32
NT = (((1,), (1,)), ((), ()))
TN = (((0,), (0,)), ((), ()))


def dot(left, right, dims=(((1,), (0,)), ((), ()))):
    return lax.dot_general(left, right, dims, preferred_element_type=F32)


def span(start, size):
    return pl.ds(pl.multiple_of(start, size), size)


class Wires:
    def __init__(self, send_sem, recv_sem):
        self.send_sem, self.recv_sem, self.count = send_sem, recv_sem, 0

    def take(self, numbers=1):
        first = self.count
        self.count += numbers
        return first

    def send(self, number, source, target, device, condition=None):
        one = pltpu.make_async_remote_copy(
            src_ref=source,
            dst_ref=target,
            send_sem=self.send_sem.at[number],
            recv_sem=self.recv_sem.at[number],
            device_id=device,
            device_id_type=DEVICE_MESH,
        )
        when(condition, one.start)
        return condition, one

    def arrived(self, number, landing, condition=None):
        when(condition, pltpu.make_async_copy(landing, landing, self.recv_sem.at[number]).wait)


def when(condition, body):
    if condition is None:
        body()
    else:
        pl.when(condition)(body)


def sent(copies):
    for condition, one in copies:
        when(condition, one.wait_send)
    copies.clear()


def layer_kernel(
    sizes,
    len_ref,
    pre_ref,
    cot_ref,
    table_ref,
    bias_ref,
    gain_ref,
    x_ref,
    rq_ref,
    dp_ref,
    ri_ref,
    ro_ref,
    out_ref,
    gx_ref,
    fq_ref,
    fi_ref,
    fo_ref,
    os_ref,
    od_ref,
    ys_ref,
    yq_ref,
    yd_ref,
    yg_ref,
    yu_ref,
    yo_ref,
    zs_ref,
    zq_ref,
    zd_ref,
    zg_ref,
    zu_ref,
    zo_ref,
    sp_ref,
    ws_ref,
    wq_ref,
    wd_ref,
    wg_ref,
    wu_ref,
    wo_ref,
    go_ref,
    xg_ref,
    hg_ref,
    dg_ref,
    uf_ref,
    mb_ref,
    du_ref,
    qk_ref,
    cx_ref,
    dc_ref,
    pb_ref,
    core_ref,
    stage_ref,
    relay_ref,
    land_ref,
    sum_ref,
    xh_ref,
    dr_ref,
    rstd_ref,
    valid_ref,
    bt_ref,
    sg_ref,
    qb_ref,
    tm_ref,
    td_ref,
    local_sem,
    send_sem,
    recv_sem,
):
    A, E, R, rows, width, sw, uc, larger, alpha, scale = sizes
    a, b, e, f, c = (lax.axis_index(axis) for axis in AXES)
    qc = 3 * sw
    all_rows = GROUP * rows
    half_rows = all_rows // 2
    slot = lambda bb, ff, cc: cc * 4 + bb * 2 + ff
    me = slot(b, f, c)
    my_rows = span(me * rows, rows)
    flip = lambda v, d: lax.rem(v + d, 2)
    rank = lambda aa, bb, ee, ff, cc: (((aa * 2 + bb) * E + ee) * 2 + ff) * 2 + cc
    wires = Wires(send_sem, recv_sem)
    peers = [(r // 4, r // 2 % 2, r % 2) for r in range(GROUP)]

    loads = [
        pltpu.make_async_copy(raw, final, local_sem.at[SHARED + 2 + k])
        for k, (raw, final) in enumerate(((rq_ref, fq_ref), (ri_ref, fi_ref), (ro_ref, fo_ref)))
    ]
    for load in loads:
        load.start()

    barrier = pltpu.get_barrier_semaphore()
    others = 0
    for da in range(A):
        for de in range(E):
            for db, df, dc in peers:
                if da + de + db + df + dc:
                    pl.semaphore_signal(
                        barrier,
                        inc=1,
                        device_id={
                            "a": lax.rem(a + da, A),
                            "b": flip(b, db),
                            "e": lax.rem(e + de, E),
                            "f": flip(f, df),
                            "c": flip(c, dc),
                        },
                        device_id_type=DEVICE_MESH,
                    )
                    others += 1
    pl.semaphore_wait(barrier, others)

    class Weight:
        def __init__(self, index, R, parts, piece, buf, out, ylanding, zlanding):
            self.index, self.R, self.parts, self.buf = index, R, parts, buf
            self.piece, self.out = piece, out
            self.ylanding, self.zlanding = ylanding, zlanding
            self.copies = []
            take = lambda count: wires.take(count * len(parts))
            self.tp, self.z, self.y = take(GROUP), take(2 * (E - 1)), take(2 * E * (A - 1))
            self.gtp, self.gz, self.gy = take(GROUP), take(2 * (E - 1)), take(2 * E * (A - 1))

        def each(self, member, body):
            for k, (first, size, extra) in enumerate(self.parts):
                body(k, pl.ds(first, size), member < larger if extra else None)

        def send(self, first, number, source, target, device, member=me):
            def body(k, cols, condition):
                self.copies.append(
                    wires.send(
                        first + number * len(self.parts) + k,
                        source.at[:, cols],
                        target.at[:, cols],
                        device,
                        condition,
                    )
                )

            self.each(member, body)

        def arrived(self, first, number, landing, member=me):
            def body(k, cols, condition):
                wires.arrived(
                    first + number * len(self.parts) + k, landing.at[:, cols], condition
                )

            self.each(member, body)

        def line(self, aa, bb, ee, ff, cc):
            return span(rank(aa, bb, ee, ff, cc) * self.R, self.R)

        def block(self, aa, bb, ee):
            return span(((aa * 2 + bb) * E + ee) * 4 * self.R, 4 * self.R)

        def own(self):
            return pltpu.make_async_copy(
                self.piece(me), self.buf.at[self.line(a, b, e, f, c)], local_sem.at[self.index]
            )

        def tp_send(self):
            self.own().start()
            for r in range(1, GROUP):
                db, df, dc = peers[r]
                bb, ff, cc = flip(b, db), flip(f, df), flip(c, dc)
                place = slot(bb, ff, cc)
                self.send(
                    self.tp,
                    r,
                    self.piece(place),
                    self.buf.at[self.line(a, b, e, f, c)],
                    {"b": bb, "f": ff, "c": cc},
                    place,
                )

        def tp_wait(self, db):
            for r in range(4 * db, 4 * db + 4):
                if r == 0:
                    self.own().wait()
                else:
                    _, df, dc = peers[r]
                    rows_ = self.line(a, flip(b, db), e, flip(f, df), flip(c, dc))
                    self.arrived(self.tp, r, self.buf.at[rows_])

        def z_send(self, db):
            rows_ = self.buf.at[self.block(a, flip(b, db), e)]
            for s in range(1, E):
                self.send(self.z, db * (E - 1) + s - 1, rows_, rows_, {"e": lax.rem(e + s, E)})

        def y_send(self, db, s):
            rows_ = self.buf.at[self.block(a, flip(b, db), lax.rem(e + E - s, E))]
            for t in range(1, A):
                number = (db * E + s) * (A - 1) + t - 1
                self.send(self.y, number, rows_, rows_, {"a": lax.rem(a + t, A)})

        def z_arrive(self, db):
            for s in range(1, E):
                rows_ = self.block(a, flip(b, db), lax.rem(e + E - s, E))
                self.arrived(self.z, db * (E - 1) + s - 1, self.buf.at[rows_])
                self.y_send(db, s)

        def y_arrive(self):
            for db in range(2):
                for s in range(E):
                    for t in range(1, A):
                        rows_ = self.block(
                            lax.rem(a + A - t, A), flip(b, db), lax.rem(e + E - s, E)
                        )
                        self.arrived(
                            self.y, (db * E + s) * (A - 1) + t - 1, self.buf.at[rows_]
                        )

        def add(self, landing, base, count):
            def load(k, cols, condition):
                copy = pltpu.make_async_copy(
                    landing.at[:, cols],
                    tm_ref.at[pl.ds(0, count), cols],
                    local_sem.at[SHARED + k],
                )
                when(condition, copy.start)

                def total():
                    copy.wait()

                    @pl.loop(0, count // 16)
                    def _(i):
                        here = pl.ds(pl.multiple_of(base + i * 16, 16), 16)
                        there = span(i * 16, 16)
                        self.buf[here, cols] = (
                            self.buf[here, cols].astype(F32) + tm_ref[there, cols].astype(F32)
                        ).astype(BF16)

                return lambda: when(condition, total)

            totals = []
            self.each(me, lambda *part: totals.append(load(*part)))
            for total in totals:
                total()

        def gy_send(self):
            for s in (*range(1, E), 0):
                for db in range(2):
                    for t in range(1, A):
                        to = lax.rem(a + t, A)
                        self.send(
                            self.gy,
                            (db * E + s) * (A - 1) + t - 1,
                            self.buf.at[self.block(to, flip(b, db), lax.rem(e + s, E))],
                            self.ylanding.at[t - 1, db, s],
                            {"a": to},
                        )

        def gy_add(self, db, s):
            bb, to = flip(b, db), lax.rem(e + s, E)
            for t in range(1, A):
                landing = self.ylanding.at[t - 1, db, s]
                self.arrived(self.gy, (db * E + s) * (A - 1) + t - 1, landing)
                self.add(landing, ((a * 2 + bb) * E + to) * 4 * self.R, 4 * self.R)
            if s:
                self.send(
                    self.gz,
                    db * (E - 1) + s - 1,
                    self.buf.at[self.block(a, bb, to)],
                    self.zlanding.at[s - 1, db],
                    {"e": to},
                )

        def gy_away(self, db):
            for s in range(1, E):
                self.gy_add(db, s)

        def home(self):
            for db in range(2):
                self.gy_add(db, 0)
            for db in range(2):
                self.gz_add(db)

        def gz_add(self, db):
            bb = flip(b, db)
            for s in range(1, E):
                landing = self.zlanding.at[s - 1, db]
                self.arrived(self.gz, db * (E - 1) + s - 1, landing)
                self.add(landing, ((a * 2 + bb) * E + e) * 4 * self.R, 4 * self.R)
            for r in range(4 * db, 4 * db + 4):
                _, df, dc = peers[r]
                ff, cc = flip(f, df), flip(c, dc)
                rows_ = self.buf.at[self.line(a, bb, e, ff, cc)]
                if r == 0:
                    pltpu.make_async_copy(rows_, self.out(me), local_sem.at[self.index]).start()
                else:
                    self.send(self.gtp, r, rows_, self.out(me), {"b": bb, "f": ff, "c": cc})

        def g_end(self):
            for r in range(GROUP):
                db, df, dc = peers[r]
                if r == 0:
                    pltpu.make_async_copy(
                        self.buf.at[self.line(a, b, e, f, c)],
                        self.out(me),
                        local_sem.at[self.index],
                    ).wait()
                else:
                    place = slot(flip(b, db), flip(f, df), flip(c, dc))
                    self.arrived(self.gtp, r, self.out(place), place)

    tile = uc - LANES
    shares = [(0, tile, False), (tile, LANES, True)]

    def quarter(ref, down, right):
        return lambda place: ref.at[
            span((down * GROUP + place) * R, R), pl.ds(right * uc, uc)
        ]

    def weight(index, parts, down, right, *rest):
        buf, ylanding, zlanding = rest
        piece, out = quarter(du_ref, down, right), quarter(hg_ref, down, right)
        return Weight(index, R, parts, piece, buf, out, ylanding, zlanding)

    s_w = Weight(
        0,
        16,
        [(0, LANES, False)],
        lambda place: sp_ref,
        ws_ref,
        lambda place: os_ref.at[place],
        ys_ref,
        zs_ref,
    )
    q_w = weight(1, [(0, qc, False)], 0, 0, wq_ref, yq_ref, zq_ref)
    g_w = weight(2, shares, 0, 1, wg_ref, yg_ref, zg_ref)
    u_w = weight(3, shares, 1, 0, wu_ref, yu_ref, zu_ref)
    o_w = weight(4, shares, 1, 1, wo_ref, yo_ref, zo_ref)

    hidden = fo_ref.shape[1]
    tiles = -(-hidden // LANES)
    tile_lane = lax.broadcasted_iota(jnp.int32, (R, LANES), 1)

    def lanes_of(ref, start, valid=LANES):
        def aligned(m):
            width_ = min(LANES, ref.shape[1] - m * LANES)
            part = ref[:, m * LANES : m * LANES + max(width_, 0)].astype(F32) if width_ > 0 else None
            if width_ >= LANES:
                return part
            if part is None:
                return jnp.zeros((R, LANES), F32)
            return jnp.concatenate([part, jnp.zeros((R, LANES - width_), F32)], axis=1)

        base, off = divmod(start, LANES)
        value = aligned(base)
        if off:
            back = LANES - off
            value = jnp.where(
                tile_lane < back,
                pltpu.roll(value, back, axis=1),
                pltpu.roll(aligned(base + 1), back, axis=1),
            )
        return jnp.where(tile_lane < valid, value, 0.0) if valid < LANES else value

    def member_tiles():
        for place in range(GROUP):
            first = place * (uc // LANES - 1) + min(place, larger)
            for k in range(uc // LANES - (place >= larger)):
                yield place, k, first + k

    def cut(ref, start, down, right):
        for place, k, number in member_tiles():
            at = (down * GROUP + place) * R, right * uc + k * LANES
            du_ref[at[0] : at[0] + R, at[1] : at[1] + LANES] = lanes_of(
                ref, start + number * LANES, min(LANES, hidden - number * LANES)
            ).astype(BF16)
        for place in range(larger, GROUP):
            at = (down * GROUP + place) * R, (right + 1) * uc - LANES
            du_ref[at[0] : at[0] + R, at[1] : at[1] + LANES] = jnp.zeros((R, LANES), BF16)

    def home_tiles(down, right):
        found = {}
        for place, k, number in member_tiles():
            at = (down * GROUP + place) * R, right * uc + k * LANES
            found[number] = at
        return lambda number: hg_ref[
            found[number][0] : found[number][0] + R, found[number][1] : found[number][1] + LANES
        ].astype(F32)

    def join(ref, groups):
        total = hidden * len(groups)
        for number in range(-(-total // LANES)):
            value = None
            for k, tile_of in enumerate(groups):
                shift = k * hidden % LANES
                first = number - k * hidden // LANES
                for piece in (first, first - 1) if shift else (first,):
                    if not 0 <= piece < tiles:
                        continue
                    start = k * hidden + piece * LANES - number * LANES
                    end = min(start + LANES, (k + 1) * hidden - number * LANES)
                    if start >= LANES or end <= 0:
                        continue
                    part = tile_of(piece)
                    if shift:
                        part = pltpu.roll(part, shift, axis=1)
                    if value is None:
                        value = part
                    else:
                        value = jnp.where((tile_lane >= start) & (tile_lane < end), part, value)
            size = min(LANES, total - number * LANES)
            ref[:, number * LANES : number * LANES + size] = value[:, :size].astype(BF16)

    def qkv_places():
        for place in range(GROUP):
            cc, bb, ff = place // 4, place // 2 % 2, place % 2
            for t in range(3):
                for i in range(sw // LANES):
                    number = i * 8 + bb * 4 + cc * 2 + ff
                    yield place * R, t * sw + i * LANES, t * width + number * LANES

    def cut_qkv():
        for row, col, start in qkv_places():
            du_ref[row : row + R, col : col + LANES] = fq_ref[:, start : start + LANES]

    def join_qkv():
        for row, col, start in qkv_places():
            fq_ref[:, start : start + LANES] = hg_ref[row : row + R, col : col + LANES]

    def remote(source, landing, send, recv, target):
        return pltpu.make_async_remote_copy(
            src_ref=source,
            dst_ref=landing,
            send_sem=send_sem.at[send],
            recv_sem=recv_sem.at[recv],
            device_id=target,
            device_id_type=DEVICE_MESH,
        )

    class Dense:
        def __init__(self):
            self.pieces = wd_ref.shape[0] // R
            self.first = wires.take(self.pieces)
            self.push = wires.take(1)
            self.zs = wires.take(self.pieces * (E - 1))
            self.ys = wires.take(self.pieces * (A - 1))
            self.gy = wires.take(self.pieces * (A - 1))
            self.gz = wires.take(self.pieces * (E - 1))
            self.back = wires.take(1)
            self.back_sends = wires.take(self.pieces)
            self.owners = []
            for piece in range(self.pieces):
                i, offset = piece * R // LANES, piece * R % LANES
                owner = ((i * 8 + b * 4 + c * 2 + f) * LANES + offset) // R
                self.owners.append(
                    {
                        "a": owner // (8 * E),
                        "b": lax.rem(owner // (4 * E), 2),
                        "e": lax.rem(owner // 4, E),
                        "f": lax.rem(owner // 2, 2),
                        "c": lax.rem(owner, 2),
                    }
                )

        def rows(self, piece):
            return wd_ref.at[pl.ds(piece * R, R)]

        def each(self, test, body):
            for piece, owner in enumerate(self.owners):
                same_a, same_e = owner["a"] == a, owner["e"] == e

                @pl.when(test(same_a, same_e))
                def _():
                    body(piece, owner)

        def local_or_remote(self, target, source, landing, send, recv, start):
            here = target["b"] == b
            for axis, mine in (("f", f), ("c", c)):
                here = here & (target[axis] == mine)
            away = remote(source, landing, send, recv, target)

            @pl.when(here)
            def _():
                if start:
                    pltpu.make_async_copy(source, landing, recv_sem.at[recv]).start()

            @pl.when(jnp.logical_not(here))
            def _():
                away.start() if start else away.wait_send()

        def out(self, start):
            first_row = rank(a, b, e, f, c) * R
            head = first_row // LANES
            piece = (head // 8) * (LANES // R) + lax.rem(first_row, LANES) // R
            target = {
                "b": lax.rem(head // 4, 2),
                "f": lax.rem(head, 2),
                "c": lax.rem(head // 2, 2),
            }
            landing = wd_ref.at[span(piece * R, R)]
            self.local_or_remote(target, dp_ref, landing, self.push, self.first + piece, start)

        def z(self, piece, s):
            rows_ = self.rows(piece)
            number = self.zs + piece * (E - 1) + s - 1
            return remote(rows_, rows_, number, self.first + piece, {"e": lax.rem(e + s, E)})

        def y(self, piece, t):
            rows_ = self.rows(piece)
            number = self.ys + piece * (A - 1) + t - 1
            return remote(rows_, rows_, number, self.first + piece, {"a": lax.rem(a + t, A)})

        def arrived(self, piece, _=None):
            wires.arrived(self.first + piece, self.rows(piece))

        def z_send(self):
            def body(piece, owner):
                self.arrived(piece)
                for s in range(1, E):
                    self.z(piece, s).start()

            self.each(lambda same_a, same_e: same_a & same_e, body)

        def y_send(self):
            self.each(lambda same_a, same_e: same_a & jnp.logical_not(same_e), self.arrived)

            def body(piece, owner):
                for t in range(1, A):
                    self.y(piece, t).start()

            self.each(lambda same_a, same_e: same_a, body)

        def y_arrive(self):
            self.each(lambda same_a, same_e: jnp.logical_not(same_a), self.arrived)

        def sent(self):
            self.out(False)

            def over_z(piece, owner):
                for s in range(1, E):
                    self.z(piece, s).wait_send()

            def over_y(piece, owner):
                for t in range(1, A):
                    self.y(piece, t).wait_send()

            self.each(lambda same_a, same_e: same_a & same_e, over_z)
            self.each(lambda same_a, same_e: same_a, over_y)

        def g_y(self, piece, t):
            to = lax.rem(a + t, A)
            number = self.gy + piece * (A - 1) + t - 1
            copy = remote(self.rows(piece), yd_ref.at[t - 1, piece], number, number, {"a": to})
            return to, copy

        def gy_send(self, start=True):
            for piece, owner in enumerate(self.owners):
                for t in range(1, A):
                    to, copy = self.g_y(piece, t)

                    @pl.when(owner["a"] == to)
                    def _():
                        copy.start() if start else copy.wait_send()

        def add(self, landing, piece):
            load = pltpu.make_async_copy(landing, td_ref, local_sem.at[SHARED])
            load.start()
            load.wait()

            @pl.loop(0, R // 16)
            def _(i):
                here, there = span(piece * R + i * 16, 16), span(i * 16, 16)
                wd_ref[here, :] = (
                    wd_ref[here, :].astype(F32) + td_ref[there, :].astype(F32)
                ).astype(BF16)

        def g_z(self, piece, s):
            to = lax.rem(e + s, E)
            number = self.gz + piece * (E - 1) + s - 1
            copy = remote(self.rows(piece), zd_ref.at[s - 1, piece], number, number, {"e": to})
            return to, copy

        def gz_send(self, start=True):
            for piece, owner in enumerate(self.owners):
                for s in range(1, E):
                    to, copy = self.g_z(piece, s)

                    @pl.when((owner["a"] == a) & (owner["e"] == to))
                    def _():
                        copy.start() if start else copy.wait_send()

        def gy_add(self):
            def body(piece, owner):
                for t in range(1, A):
                    landing = yd_ref.at[t - 1, piece]
                    wires.arrived(self.gy + piece * (A - 1) + t - 1, landing)
                    self.add(landing, piece)

            self.each(lambda same_a, same_e: same_a, body)
            self.gz_send()

        def home(self, piece, owner, start):
            target = {axis: owner[axis] for axis in ("b", "f", "c")}
            self.local_or_remote(
                target, self.rows(piece), od_ref, self.back_sends + piece, self.back, start
            )

        def gz_add(self):
            def body(piece, owner):
                for s in range(1, E):
                    landing = zd_ref.at[s - 1, piece]
                    wires.arrived(self.gz + piece * (E - 1) + s - 1, landing)
                    self.add(landing, piece)
                self.home(piece, owner, True)

            self.each(lambda same_a, same_e: same_a & same_e, body)

        def g_end(self):
            wires.arrived(self.back, od_ref)
            self.gy_send(False)
            self.gz_send(False)
            self.each(
                lambda same_a, same_e: same_a & same_e,
                lambda piece, owner: self.home(piece, owner, False),
            )

    dense = Dense()

    to_b, to_f, to_c = {"b": 1 - b}, {"f": 1 - f}, {"c": 1 - c}
    nb, nf, dg = slot(1 - b, f, c), slot(b, 1 - f, c), slot(1 - b, 1 - f, c)

    class Gather:
        def __init__(self, buf, lean):
            self.buf, self.first, self.copies, self.lean = buf, wires.take(10), [], lean

        def part(self, place, which):
            if which is None:
                return self.buf.at[span(place * rows, rows)]
            return self.buf.at[span(place * rows + which * (rows // 2), rows // 2)]

        def copy(self, number, place, which, device):
            here = self.part(place, which)
            self.copies.append(wires.send(self.first + number, here, here, device))

        def landed(self, number, place, which):
            wires.arrived(self.first + number, self.part(place, which))

        def start(self):
            self.copy(0, me, 0, to_b)
            self.copy(1, me, 1, to_f)
            self.copy(2, me, 1, to_b)
            self.copy(3, me, 0, to_f)
            self.copy(4, me, None, to_c)

        def relay(self):
            if self.lean:
                self.landed(1, nf, 1)
                self.copy(6, nf, 1, to_b)
                self.landed(3, nf, 0)
                self.copy(5, nf, 0, to_b)
                self.copy(8, nf, None, to_c)
                self.landed(0, nb, 0)
                self.landed(2, nb, 1)
                self.copy(7, nb, None, to_c)
                return
            self.landed(0, nb, 0)
            self.copy(5, nb, 0, to_f)
            self.landed(1, nf, 1)
            self.copy(6, nf, 1, to_b)
            self.landed(2, nb, 1)
            self.copy(7, nb, None, to_c)
            self.landed(3, nf, 0)
            self.copy(8, nf, None, to_c)

        def finish(self):
            self.landed(5, dg, 0)
            self.landed(6, dg, 1)
            self.copy(9, dg, None, to_c)
            other = 1 - c
            self.landed(4, slot(b, f, other), None)
            self.landed(7, slot(1 - b, f, other), None)
            self.landed(8, slot(b, 1 - f, other), None)
            self.landed(9, slot(1 - b, 1 - f, other), None)

    step = 16
    places = [(1 - b, 1 - f), (1 - b, f), (b, 1 - f), (b, f)]

    def accumulate(target, at, count, terms):
        @pl.loop(0, count // step)
        def _(i):
            window = pl.ds(pl.multiple_of(at + i * step, step), step)
            total = terms[0][window, :].astype(F32)
            for term in terms[1:]:
                total = total + term[window, :].astype(F32)
            target[window, :] = total.astype(target.dtype)

    def scatter(multiply, lean, early=None, late=None):
        first, copies = wires.take(10), []

        def send(*copy):
            copies.append(wires.send(*copy))

        multiply((1 - c) * half_rows, half_rows)
        for k, (bb, ff) in enumerate(places):
            send(
                first + k,
                pb_ref.at[span(slot(bb, ff, 1 - c) * rows, rows)],
                core_ref.at[pl.ds(k * rows, rows)],
                to_c,
            )
        multiply(c * half_rows, half_rows)
        own = [pb_ref.at[span(slot(bb, ff, c) * rows, rows)] for bb, ff in places]
        core = [core_ref.at[pl.ds(k * rows, rows)] for k in range(4)]
        mid = rows // 2
        low, high = pl.ds(0, mid), pl.ds(mid, mid)
        early, late = (hook or (lambda: None) for hook in (early, late))
        wires.arrived(first, core[0])
        accumulate(stage_ref.at[0], 0, rows, [own[0], core[0]])
        if lean:
            send(first + 4, stage_ref.at[0], relay_ref, to_b)
            wires.arrived(first + 1, core[1])
            accumulate(stage_ref.at[1], 0, rows, [own[1], core[1]])
            send(first + 6, stage_ref.at[1], land_ref.at[0], to_b)
            early()
            wires.arrived(first + 2, core[2])
            wires.arrived(first + 4, relay_ref)
            accumulate(stage_ref.at[2], 0, rows, [own[2], core[2], relay_ref])
            send(first + 7, stage_ref.at[2], land_ref.at[1], to_f)
            late()
            wires.arrived(first + 3, core[3])
            wires.arrived(first + 6, land_ref.at[0])
            wires.arrived(first + 7, land_ref.at[1])
        else:
            send(first + 4, stage_ref.at[0, low], relay_ref.at[low], to_b)
            send(first + 5, stage_ref.at[0, high], relay_ref.at[high], to_f)
            wires.arrived(first + 1, core[1])
            accumulate(stage_ref.at[1], 0, mid, [own[1], core[1]])
            send(first + 6, stage_ref.at[1, low], land_ref.at[0, low], to_b)
            wires.arrived(first + 2, core[2])
            accumulate(stage_ref.at[2], mid, mid, [own[2], core[2]])
            send(first + 7, stage_ref.at[2, high], land_ref.at[1, high], to_f)
            early()
            wires.arrived(first + 5, relay_ref.at[high])
            accumulate(stage_ref.at[1], mid, mid, [own[1], core[1], relay_ref])
            send(first + 8, stage_ref.at[1, high], land_ref.at[0, high], to_b)
            wires.arrived(first + 4, relay_ref.at[low])
            accumulate(stage_ref.at[2], 0, mid, [own[2], core[2], relay_ref])
            send(first + 9, stage_ref.at[2, low], land_ref.at[1, low], to_f)
            late()
            wires.arrived(first + 3, core[3])
            wires.arrived(first + 6, land_ref.at[0, low])
            wires.arrived(first + 7, land_ref.at[1, high])
            wires.arrived(first + 8, land_ref.at[0, high])
            wires.arrived(first + 9, land_ref.at[1, low])
        accumulate(sum_ref, 0, rows, [own[3], core[3], land_ref.at[0], land_ref.at[1]])
        sent(copies)

    def blocks(count_m, count_n, body):
        @pl.loop(0, count_m * count_n)
        def _(k):
            body(k // count_n, lax.rem(k, count_n))

    def onto_partial(*terms):
        def multiply(first, count):
            def body(m, n):
                here = pl.ds(pl.multiple_of(first, half_rows) + m * 512, 512)
                there = span(n * 512, 512)
                total = sum(dot(left[here, :], weight[there, :], NT) for left, weight in terms)
                pb_ref[here, there] = total.astype(BF16)

            blocks(count // 512, width // 512, body)

        return multiply

    loads[0].wait()
    cut_qkv()
    q_w.tp_send()
    columns = [bias_ref[...].astype(F32), gain_ref[...].astype(F32)]
    columns.append(jnp.zeros((R, LANES - sum(one.shape[1] for one in columns)), F32))
    turned = jnp.concatenate(columns, axis=1).T[0:16, :]
    if R < LANES:
        turned = jnp.concatenate([turned, jnp.zeros((16, LANES - R), F32)], axis=1)
    sp_ref[...] = turned.astype(BF16)
    s_w.tp_send()
    dense.out(True)
    own_x = pltpu.make_async_copy(
        x_ref.at[0], xg_ref.at[my_rows, pl.ds(0, width)], local_sem.at[5]
    )
    own_x.start()
    sg_ref[...] = jnp.zeros_like(sg_ref)

    @pl.when(me >= larger)
    def _():
        for weight in (g_w, u_w, o_w):
            weight.buf[:, tile:] = jnp.zeros((width, LANES), BF16)

    at = lax.broadcasted_iota(jnp.int32, (rows, LANES), 0)
    lane = lax.broadcasted_iota(jnp.int32, (rows, LANES), 1)
    docs = len_ref.shape[1]
    key, prefix_at, local_pos, valid, first = at + docs, at * 0, at * 0, at < 0, 0
    for k in range(docs):
        last = first + len_ref[0, k]
        member = (at >= first) & (at < last)
        key = jnp.where(member, k, key)
        prefix_at = jnp.where(member, pre_ref[0, k], prefix_at)
        local_pos = jnp.where(member, at - first, local_pos)
        valid = valid | member
        first = last
    info = jnp.where(lane == 0, key, jnp.where(lane == 1, prefix_at, local_pos))
    xg_ref[my_rows, width:] = info.astype(F32).astype(BF16)
    valid_ref[...] = jnp.where(valid, 1.0, 0.0)

    loads[1].wait()
    cut(fi_ref, 0, 0, 1)
    tokens = Gather(xg_ref, True)
    for db in range(2):
        q_w.tp_wait(db)
        q_w.z_send(db)
        q_w.y_send(db, 0)
    own_x.wait()
    tokens.start()
    g_w.tp_send()
    cut(fi_ref, hidden, 1, 0)
    loads[2].wait()
    cut(fo_ref, 0, 1, 1)
    for db in range(2):
        s_w.tp_wait(db)
        s_w.z_send(db)
        s_w.y_send(db, 0)
    dense.z_send()
    u_w.tp_send()
    q_w.z_arrive(0)
    tokens.relay()
    g_w.tp_wait(0)
    g_w.z_send(0)
    g_w.y_send(0, 0)
    q_w.z_arrive(1)
    s_w.z_arrive(0)
    s_w.z_arrive(1)
    dense.y_send()
    g_w.tp_wait(1)
    g_w.z_send(1)
    g_w.y_send(1, 0)
    tokens.finish()
    o_w.tp_send()
    s_w.y_arrive()
    q_w.y_arrive()

    lane = lane[0:16, :]

    @pl.loop(0, width // LANES)
    def _(k):
        line = jnp.zeros((16, LANES), F32)
        for j in range(LANES // R):
            part = ws_ref[span((k * (LANES // R) + j) * 16, 16), :].astype(F32)
            if j:
                part = pltpu.roll(part, j * R, axis=1)
            line = jnp.where(lane // R == j, part, line)
        bt_ref[:, span(k * LANES, LANES)] = line

    heads = [i * 8 + b * 4 + c * 2 + f for i in range(sw // LANES)]
    for t in range(3):
        for i, number in enumerate(heads):
            at = t * sw + i * LANES
            qb_ref[0:1, at : at + LANES] = bt_ref[t : t + 1, span(number * LANES, LANES)]

    def projection(m, n):
        here, cols = span(m * 512, 512), span(n * sw, sw)
        uf_ref[here, cols] = (
            dot(xg_ref[here, 0:width], wq_ref[:, cols]) + qb_ref[0:1, cols]
        )

    blocks(all_rows // 512, 3, projection)

    row_at = lax.broadcasted_iota(jnp.int32, (rows, rows), 0)
    col_at = lax.broadcasted_iota(jnp.int32, (rows, rows), 1)

    def sequence(s):
        here = span(s * rows, rows)
        info = xg_ref[here, width : width + LANES].astype(F32)
        turned = info.T
        allowed = (info[:, 0:1] == turned[0:1, :]) & (
            (turned[2:3, :] < info[:, 1:2]) | (col_at <= row_at)
        )
        picked = (info[:, 2:3] == col_at.astype(F32)).astype(BF16)
        parts = dot(picked, table_ref[...])
        cos_sin = parts[:, 0:LANES] + parts[:, LANES : 2 * LANES] + parts[:, 2 * LANES :]
        swapped = pltpu.roll(cos_sin, LANES // 2, axis=1)
        first = col_at < LANES // 2
        cosine = jnp.where(first, cos_sin, swapped)
        sine = jnp.where(first, -swapped, cos_sin)
        return here, allowed, cosine, sine

    def turn(value, cosine, sine):
        return value * cosine + pltpu.roll(value, LANES // 2, axis=1) * sine

    def softmax(q, k, allowed):
        scores = jnp.where(allowed, scale * dot(q, k, NT), MASKED_SCORE)
        power = jnp.exp(scores - jnp.max(scores, axis=1, keepdims=True))
        return power / jnp.sum(power, axis=1, keepdims=True)

    @pl.loop(0, GROUP)
    def _(s):
        here, allowed, cosine, sine = sequence(s)
        for i in range(sw // LANES):
            cols = [pl.ds(t * sw + i * LANES, LANES) for t in range(3)]
            q = turn(uf_ref[here, cols[0]], cosine, sine).astype(BF16)
            k = turn(uf_ref[here, cols[1]], cosine, sine).astype(BF16)
            v = uf_ref[here, cols[2]].astype(BF16)
            qk_ref[here, cols[0]] = q
            qk_ref[here, cols[1]] = k
            qk_ref[here, cols[2]] = v
            probs = softmax(q, k, allowed).astype(BF16)
            cx_ref[here, i * LANES : (i + 1) * LANES] = dot(probs, v).astype(BF16)

    u_w.tp_wait(0)
    u_w.tp_wait(1)
    u_w.z_send(0)
    g_w.z_arrive(0)
    dense.y_arrive()

    def dense_partial(first, count):
        def body(m, n):
            here = pl.ds(pl.multiple_of(first, half_rows) + m * 512, 512)
            cols = span(n * 512, 512)
            pb_ref[here, cols] = dot(cx_ref[here, :], wd_ref[:, cols]).astype(BF16)

        blocks(count // 512, width // 512, body)

    def more_units():
        u_w.z_send(1)
        u_w.y_send(0, 0)
        u_w.y_send(1, 0)

    scatter(dense_partial, True, lambda: g_w.z_arrive(1), more_units)

    def row_loop(body):
        @pl.loop(0, rows // 16)
        def _(i):
            body(span(i * 16, 16), span(me * rows + i * 16, 16))

    def normalize(value):
        centered = value - jnp.mean(value, axis=1, keepdims=True)
        rstd = lax.rsqrt(jnp.mean(centered * centered, axis=1, keepdims=True) + EPSILON)
        return centered * rstd, rstd

    def first_norm(here, there):
        value = (
            alpha * xg_ref[there, 0:width].astype(F32) + sum_ref[here, :] + bt_ref[3:4, :]
        )
        unit, rstd = normalize(value)
        xh_ref[here, :] = unit
        rstd_ref[here, :] = jnp.broadcast_to(rstd, (16, LANES))
        hg_ref[there, :] = (unit * bt_ref[7:8, :] + bt_ref[4:5, :]).astype(BF16)

    row_loop(first_norm)
    normed = Gather(hg_ref, True)
    normed.start()
    for db in range(2):
        o_w.tp_wait(db)
        o_w.z_send(db)
    u_w.z_arrive(0)
    o_w.y_send(0, 0)
    o_w.y_send(1, 0)
    normed.relay()
    u_w.z_arrive(1)
    normed.finish()
    g_w.y_arrive()
    u_w.y_arrive()

    def units(m, n):
        here = span(m * 512, 512)
        gate_cols = span(n * 256, 256)
        up_cols = span(uc + n * 256, 256)
        left = hg_ref[here, :]
        gate = dot(left, wg_ref[:, gate_cols])
        up = dot(left, wu_ref[:, gate_cols])
        cdf = 0.5 * (1.0 + lax.erf(gate * (0.5**0.5)))
        density = jnp.exp(-0.5 * gate * gate) * (1.0 / math.sqrt(2.0 * math.pi))
        act = gate * cdf
        mb_ref[here, gate_cols] = (act * up).astype(BF16)
        uf_ref[here, gate_cols] = (cdf + gate * density) * up
        uf_ref[here, up_cols] = act

    blocks(all_rows // 512, uc // 256, units)
    o_w.z_arrive(0)
    o_w.z_arrive(1)
    o_w.y_arrive()
    scatter(onto_partial((mb_ref, wo_ref)), False)

    def add_row(row, value):
        sg_ref[row : row + 1, :] += jnp.sum(value, axis=0, keepdims=True)

    def norm_back(grad, gain, unit, rstd):
        scaled = grad * gain
        return rstd * (
            scaled
            - jnp.mean(scaled, axis=1, keepdims=True)
            - unit * jnp.mean(scaled * unit, axis=1, keepdims=True)
        )

    def second_norm(here, there):
        normed_one = xh_ref[here, :] * bt_ref[7:8, :] + bt_ref[4:5, :]
        unit, rstd = normalize(alpha * normed_one + sum_ref[here, :] + bt_ref[5:6, :])
        out_ref[here, :] = (unit * bt_ref[8:9, :] + bt_ref[6:7, :]).astype(BF16)
        grad = cot_ref[0, here, :].astype(F32) * valid_ref[here, 0:1]
        back = norm_back(grad, bt_ref[8:9, :], unit, rstd)
        low = back.astype(BF16)
        dr_ref[here, :] = back
        dg_ref[there, :] = low
        add_row(5, low.astype(F32))
        add_row(6, grad)
        add_row(8, grad * unit)

    row_loop(second_norm)
    branch = Gather(dg_ref, False)
    branch.start()
    branch.relay()
    branch.finish()

    def units_back(m, n):
        here = span(m * 512, 512)
        gate_cols, up_cols = span(n * 256, 256), span(uc + n * 256, 256)
        grad = dot(dg_ref[here, :], wo_ref[:, gate_cols])
        du_ref[here, gate_cols] = (uf_ref[here, gate_cols] * grad).astype(BF16)
        du_ref[here, up_cols] = (uf_ref[here, up_cols] * grad).astype(BF16)

    def weight_grad(left, right, target, cols, bn):
        def body(m, n):
            here, there = span(m * 512, 512), span(n * bn, bn)
            target[here, there] = dot(left[:, here], right[:, there], TN).astype(BF16)

        blocks(width // 512, cols // bn, body)

    for flow in (normed, q_w, g_w, u_w, o_w):
        sent(flow.copies)
    weight_grad(dg_ref, mb_ref, go_ref, uc, uc)
    o_w.buf = go_ref
    o_w.gy_send()
    blocks(all_rows // 512, uc // 256, units_back)

    du_gate = du_ref.at[:, pl.ds(0, uc)]
    du_up = du_ref.at[:, pl.ds(uc, uc)]

    def in_grad():
        for weight, right in ((g_w, du_gate), (u_w, du_up)):
            weight_grad(hg_ref, right, weight.buf, uc, uc)
            weight.gy_send()
            if weight is g_w:
                o_w.gy_away(0)

    sent(branch.copies)
    scatter(
        onto_partial((du_gate, wg_ref), (du_up, wu_ref)), False, in_grad, lambda: o_w.gy_away(1)
    )

    def first_norm_back(here, there):
        grad = alpha * dr_ref[here, :] + sum_ref[here, :]
        unit = xh_ref[here, :]
        back = norm_back(grad, bt_ref[7:8, :], unit, rstd_ref[here, 0:1])
        low = back.astype(BF16)
        dr_ref[here, :] = back
        dg_ref[there, :] = low
        add_row(3, low.astype(F32))
        add_row(4, grad)
        add_row(7, grad * unit)

    row_loop(first_norm_back)
    attended = Gather(dg_ref, True)
    attended.start()
    g_w.gy_away(0)
    attended.relay()
    g_w.gy_away(1)
    attended.finish()

    def context_back(m, n):
        here = span(m * 512, 512)
        dc_ref[here, :] = dot(dg_ref[here, :], wd_ref[...], NT).astype(BF16)

    blocks(all_rows // 512, 1, context_back)

    def dense_grad(m, n):
        cols = span(n * 512, 512)
        wd_ref[:, cols] = dot(cx_ref[...], dg_ref[:, cols], TN).astype(BF16)

    dense.sent()
    blocks(1, width // 512, dense_grad)
    dense.gy_send()
    u_w.gy_away(0)
    o_w.home()

    @pl.loop(0, GROUP)
    def _(s):
        here, allowed, cosine, sine = sequence(s)
        for i, number in enumerate(heads):
            cols = [pl.ds(t * sw + i * LANES, LANES) for t in range(3)]
            q, k, v = (qk_ref[here, one] for one in cols)
            grad = dc_ref[here, i * LANES : (i + 1) * LANES]
            probs = softmax(q, k, allowed)
            d_probs = dot(grad, v, NT)
            d_value = dot(probs.astype(BF16), grad, TN)
            d_scores = probs * (d_probs - jnp.sum(probs * d_probs, axis=1, keepdims=True))
            low = jnp.where(allowed, d_scores, 0.0).astype(BF16)
            d_query = turn(scale * dot(low, k), cosine, -sine)
            d_key = turn(scale * dot(low, q, TN), cosine, -sine)
            for t, value in enumerate((d_query, d_key, d_value)):
                value = value.astype(BF16)
                mb_ref[here, cols[t]] = value
                lanes = span(number * LANES, LANES)
                sg_ref[t : t + 1, lanes] += jnp.sum(value.astype(F32), axis=0, keepdims=True)

    u_w.gy_away(1)

    def late_adds():
        q_w.gy_away(0)
        g_w.home()

    def qkv_grad():
        weight_grad(xg_ref, mb_ref, wq_ref, qc, qc)

        q_w.gy_send()
        sent(s_w.copies)

        @pl.loop(0, width // LANES)
        def _(k):
            line = sg_ref[:, span(k * LANES, LANES)]
            for j in range(LANES // R):
                part = line if j == 0 else pltpu.roll(line, LANES - j * R, axis=1)
                ws_ref[span((k * (LANES // R) + j) * 16, 16), :] = part.astype(BF16)

        s_w.gy_send()

    scatter(onto_partial((mb_ref, wq_ref)), True, qkv_grad, late_adds)

    def tokens_back(here, there):
        gx_ref[here, :] = alpha * dr_ref[here, :] + sum_ref[here, :]

    row_loop(tokens_back)

    q_w.gy_away(1)
    dense.gy_add()
    for db in range(2):
        s_w.gy_away(db)
    u_w.home()
    for db in range(2):
        q_w.gy_add(db, 0)
        s_w.gy_add(db, 0)
    for db in range(2):
        q_w.gz_add(db)
    for db in range(2):
        s_w.gz_add(db)
    dense.gz_add()
    o_w.g_end()
    join(fo_ref, [home_tiles(1, 1)])
    g_w.g_end()
    u_w.g_end()
    join(fi_ref, [home_tiles(0, 1), home_tiles(1, 0)])
    q_w.g_end()
    join_qkv()
    s_w.g_end()
    dense.g_end()
    for flow in (q_w, g_w, u_w, o_w, s_w, tokens, attended):
        sent(flow.copies)


def on_device(
    tokens,
    cotangent,
    lengths,
    prefix,
    qkv_weight,
    dense_weight,
    ffin_weight,
    ffout_weight,
    biases,
    norm_gains,
):
    _, rows, width = tokens.shape
    A, E = lax.axis_size("a"), lax.axis_size("e")
    R = qkv_weight.shape[0]
    head_dim = width // HEADS
    my_heads = HEADS // GROUP
    hidden = ffout_weight.shape[1]
    sw = my_heads * head_dim
    qc = 3 * sw

    inverse = np.float32(ROPE_BASE) ** (
        -np.arange(head_dim // 2, dtype=np.float32) * np.float32(2.0 / head_dim)
    )
    angles = np.arange(rows, dtype=np.float32)[:, None] * inverse.astype(np.float32)
    rest = np.concatenate([np.cos(angles), np.sin(angles)], axis=1).astype(np.float32)
    terms = []
    for _ in range(3):
        terms.append(rest.astype(BF16))
        rest = rest - terms[-1].astype(np.float32)
    table = jnp.asarray(np.concatenate(terms, axis=1))

    tiles = -(-hidden // LANES)
    larger = tiles % GROUP
    uc = (tiles // GROUP + 1) * LANES
    wires = 8 * (2 * GROUP + 4 * (E - 1) + 4 * E * (A - 1))
    wires += (sw // R) * 2 * (A + E) + 2 + 8 * 10
    group_rows = GROUP * rows
    sizes = (A, E, R, rows, width, sw, uc, larger, (2.0 * LAYERS) ** 0.5, head_dim ** (-0.5))
    shape = jax.ShapeDtypeStruct
    anywhere, vmem = pl.BlockSpec(memory_space=pl.ANY), pl.BlockSpec(memory_space=pltpu.VMEM)
    landings = [(64, LANES), (4 * R, qc), None] + [(4 * R, uc)] * 3
    dense_landing = (sw // R, R, width)
    results = pl.pallas_call(
        functools.partial(layer_kernel, sizes),
        out_shape=[
            shape((rows, width), BF16),
            shape((rows, width), F32),
            shape((R, 3 * width), BF16),
            shape((R, 2 * hidden), BF16),
            shape((R, hidden), BF16),
            shape((GROUP, 16, LANES), BF16),
            shape((R, width), BF16),
        ]
        + [
            shape((A - 1,) + ((2, E) + one if one else dense_landing), BF16)
            for one in landings
        ]
        + [
            shape((E - 1,) + ((2,) + one if one else dense_landing), BF16)
            for one in landings
        ],
        in_specs=[pl.BlockSpec(memory_space=pltpu.SMEM)] * 2 + [vmem] * 4 + [anywhere] * 5,
        out_specs=[vmem] * 5 + [anywhere] * 14,
        scratch_shapes=[
            pltpu.VMEM((16, LANES), BF16),
            pltpu.VMEM((width // R * 16, LANES), BF16),
            pltpu.VMEM((width, qc), BF16),
            pltpu.VMEM((sw, width), BF16),
            pltpu.VMEM((width, uc), BF16),
            pltpu.VMEM((width, uc), BF16),
            pltpu.VMEM((width, uc), BF16),
            pltpu.VMEM((width, uc), BF16),
            pltpu.VMEM((group_rows, width + LANES), BF16),
            pltpu.VMEM((group_rows, width), BF16),
            pltpu.VMEM((group_rows, width), BF16),
            pltpu.VMEM((group_rows, 2 * uc), F32),
            pltpu.VMEM((group_rows, uc), BF16),
            pltpu.VMEM((group_rows, 2 * uc), BF16),
            pltpu.VMEM((group_rows, qc), BF16),
            pltpu.VMEM((group_rows, sw), BF16),
            pltpu.VMEM((group_rows, sw), BF16),
            pltpu.VMEM((group_rows, width), BF16),
            pltpu.VMEM((4 * rows, width), BF16),
            pltpu.VMEM((3, rows, width), BF16),
            pltpu.VMEM((rows, width), BF16),
            pltpu.VMEM((2, rows, width), BF16),
            pltpu.VMEM((rows, width), F32),
            pltpu.VMEM((rows, width), F32),
            pltpu.VMEM((rows, width), F32),
            pltpu.VMEM((rows, LANES), F32),
            pltpu.VMEM((rows, LANES), F32),
            pltpu.VMEM((16, width), F32),
            pltpu.VMEM((16, width), F32),
            pltpu.VMEM((8, qc), F32),
            pltpu.VMEM((4 * R, max(uc, qc)), BF16),
            pltpu.VMEM((R, width), BF16),
            pltpu.SemaphoreType.DMA((SHARED + 5,)),
            pltpu.SemaphoreType.DMA((wires,)),
            pltpu.SemaphoreType.DMA((wires,)),
        ],
        compiler_params=pltpu.CompilerParams(
            collective_id=0, has_side_effects=True, vmem_limit_bytes=63 << 20
        ),
    )(
        lengths,
        prefix,
        cotangent,
        table,
        biases,
        norm_gains,
        tokens,
        qkv_weight,
        dense_weight,
        ffin_weight,
        ffout_weight,
    )
    result, d_tokens, qkv_grad, ffin_grad, ffout_grad, small_grads, dense_grad = results[:7]
    small_grads = jnp.sum(small_grads.astype(F32), axis=0)[:, :R].T
    return (
        result.reshape(tokens.shape),
        d_tokens.reshape(tokens.shape),
        qkv_grad.astype(F32),
        dense_grad.astype(F32),
        ffin_grad.astype(F32),
        ffout_grad.astype(F32),
        small_grads[:, :7],
        small_grads[:, 7:9],
    )


def solution(mesh):
    dp, fsdp = mesh.shape["dp"], mesh.shape["fsdp"]
    fine = Mesh(mesh.devices.reshape(dp // 2, 2, fsdp // 4, 2, 2), AXES)
    cube, flat = P(AXES, None, None), P(AXES, None)
    return jax.shard_map(
        on_device,
        mesh=fine,
        in_specs=(cube, cube) + (flat,) * 8,
        out_specs=(cube, cube) + (flat,) * 6,
        check_vma=False,
    )
```

```python
import functools
import math

import jax
import jax.numpy as jnp
import numpy as np
from jax import lax
from jax.experimental import pallas as pl
from jax.experimental.pallas import tpu as pltpu
from jax.sharding import Mesh
from jax.sharding import PartitionSpec as P

HEADS = 16
LAYERS = 24
MASKED_SCORE = -1e30
EPSILON = 1e-05
ROPE_BASE = 10000.0

AXES = ("a", "b", "e", "f", "c")
GROUP = 8
LANES = 128
SHARED = 6
DEVICE_MESH = pl.DeviceIdType.MESH
BF16 = jnp.bfloat16
F32 = jnp.float32
NT = (((1,), (1,)), ((), ()))
TN = (((0,), (0,)), ((), ()))


def dot(left, right, dims=(((1,), (0,)), ((), ()))):
    return lax.dot_general(left, right, dims, preferred_element_type=F32)


def span(start, size):
    return pl.ds(pl.multiple_of(start, size), size)


class Wires:
    def __init__(self, send_sem, recv_sem):
        self.send_sem, self.recv_sem, self.count = send_sem, recv_sem, 0

    def take(self, numbers=1):
        first = self.count
        self.count += numbers
        return first

    def send(self, number, source, target, device, condition=None):
        one = pltpu.make_async_remote_copy(
            src_ref=source,
            dst_ref=target,
            send_sem=self.send_sem.at[number],
            recv_sem=self.recv_sem.at[number],
            device_id=device,
            device_id_type=DEVICE_MESH,
        )
        when(condition, one.start)
        return condition, one

    def arrived(self, number, landing, condition=None):
        when(condition, pltpu.make_async_copy(landing, landing, self.recv_sem.at[number]).wait)


def when(condition, body):
    if condition is None:
        body()
    else:
        pl.when(condition)(body)


def sent(copies):
    for condition, one in copies:
        when(condition, one.wait_send)
    copies.clear()


def layer_kernel(
    sizes,
    len_ref,
    pre_ref,
    ct_ref,
    tb_ref,
    sp_ref,
    x_ref,
    rq_ref,
    dp_ref,
    ri_ref,
    ro_ref,
    small_ref,
    eo_ref,
    ex_ref,
    eq_ref,
    ei_ref,
    ef_ref,
    od_ref,
    ys_ref,
    yq_ref,
    yd_ref,
    yg_ref,
    yu_ref,
    yo_ref,
    zs_ref,
    zq_ref,
    zd_ref,
    zg_ref,
    zu_ref,
    zo_ref,
    out_ref,
    gx_ref,
    fq_ref,
    fi_ref,
    fo_ref,
    cot_ref,
    table_ref,
    os_ref,
    ws_ref,
    wq_ref,
    wd_ref,
    wg_ref,
    wu_ref,
    wo_ref,
    go_ref,
    xg_ref,
    hg_ref,
    dg_ref,
    uf_ref,
    mb_ref,
    du_ref,
    qk_ref,
    cx_ref,
    dc_ref,
    pb_ref,
    core_ref,
    stage_ref,
    relay_ref,
    land_ref,
    sum_ref,
    xh_ref,
    dr_ref,
    rstd_ref,
    valid_ref,
    bt_ref,
    sg_ref,
    qb_ref,
    tm_ref,
    td_ref,
    local_sem,
    send_sem,
    recv_sem,
):
    A, E, R, rows, width, sw, uc, larger, alpha, scale = sizes
    a, b, e, f, c = (lax.axis_index(axis) for axis in AXES)
    qc = 3 * sw
    all_rows = GROUP * rows
    half_rows = all_rows // 2
    slot = lambda bb, ff, cc: cc * 4 + bb * 2 + ff
    me = slot(b, f, c)
    my_rows = span(me * rows, rows)
    flip = lambda v, d: lax.rem(v + d, 2)
    rank = lambda aa, bb, ee, ff, cc: (((aa * 2 + bb) * E + ee) * 2 + ff) * 2 + cc
    wires = Wires(send_sem, recv_sem)
    peers = [(r // 4, r // 2 % 2, r % 2) for r in range(GROUP)]

    loads = [
        pltpu.make_async_copy(raw, final, local_sem.at[SHARED + 2 + k])
        for k, (raw, final) in enumerate(
            (
                (rq_ref, fq_ref),
                (ri_ref, fi_ref),
                (ro_ref, fo_ref),
                (tb_ref, table_ref),
                (ct_ref.at[0], cot_ref),
            )
        )
    ]
    results = [
        pltpu.make_async_copy(found, result, local_sem.at[SHARED + 7 + k])
        for k, (found, result) in enumerate(
            (
                (out_ref, eo_ref),
                (gx_ref, ex_ref),
                (fo_ref, ef_ref),
                (fi_ref, ei_ref),
                (fq_ref, eq_ref),
            )
        )
    ]
    for load in loads:
        load.start()

    barrier = pltpu.get_barrier_semaphore()
    others = 0
    for da in range(A):
        for de in range(E):
            for db, df, dc in peers:
                if da + de + db + df + dc:
                    pl.semaphore_signal(
                        barrier,
                        inc=1,
                        device_id={
                            "a": lax.rem(a + da, A),
                            "b": flip(b, db),
                            "e": lax.rem(e + de, E),
                            "f": flip(f, df),
                            "c": flip(c, dc),
                        },
                        device_id_type=DEVICE_MESH,
                    )
                    others += 1
    pl.semaphore_wait(barrier, others)

    class Weight:
        def __init__(self, index, R, parts, piece, buf, out, ylanding, zlanding):
            self.index, self.R, self.parts, self.buf = index, R, parts, buf
            self.piece, self.out = piece, out
            self.ylanding, self.zlanding = ylanding, zlanding
            self.copies = []
            take = lambda count: wires.take(count * len(parts))
            self.tp, self.z, self.y = take(GROUP), take(2 * (E - 1)), take(2 * E * (A - 1))
            self.gtp, self.gz, self.gy = take(GROUP), take(2 * (E - 1)), take(2 * E * (A - 1))

        def each(self, member, body):
            for k, (first, size, extra) in enumerate(self.parts):
                body(k, pl.ds(first, size), member < larger if extra else None)

        def send(self, first, number, source, target, device, member=me):
            def body(k, cols, condition):
                self.copies.append(
                    wires.send(
                        first + number * len(self.parts) + k,
                        source.at[:, cols],
                        target.at[:, cols],
                        device,
                        condition,
                    )
                )

            self.each(member, body)

        def arrived(self, first, number, landing, member=me):
            def body(k, cols, condition):
                wires.arrived(
                    first + number * len(self.parts) + k, landing.at[:, cols], condition
                )

            self.each(member, body)

        def line(self, aa, bb, ee, ff, cc):
            return span(rank(aa, bb, ee, ff, cc) * self.R, self.R)

        def block(self, aa, bb, ee):
            return span(((aa * 2 + bb) * E + ee) * 4 * self.R, 4 * self.R)

        def own(self):
            return pltpu.make_async_copy(
                self.piece(me), self.buf.at[self.line(a, b, e, f, c)], local_sem.at[self.index]
            )

        def tp_send(self):
            self.own().start()
            for r in range(1, GROUP):
                db, df, dc = peers[r]
                bb, ff, cc = flip(b, db), flip(f, df), flip(c, dc)
                place = slot(bb, ff, cc)
                self.send(
                    self.tp,
                    r,
                    self.piece(place),
                    self.buf.at[self.line(a, b, e, f, c)],
                    {"b": bb, "f": ff, "c": cc},
                    place,
                )

        def tp_wait(self, db):
            for r in range(4 * db, 4 * db + 4):
                if r == 0:
                    self.own().wait()
                else:
                    _, df, dc = peers[r]
                    rows_ = self.line(a, flip(b, db), e, flip(f, df), flip(c, dc))
                    self.arrived(self.tp, r, self.buf.at[rows_])

        def z_send(self, db):
            rows_ = self.buf.at[self.block(a, flip(b, db), e)]
            for s in range(1, E):
                self.send(self.z, db * (E - 1) + s - 1, rows_, rows_, {"e": lax.rem(e + s, E)})

        def y_send(self, db, s):
            rows_ = self.buf.at[self.block(a, flip(b, db), lax.rem(e + E - s, E))]
            for t in range(1, A):
                number = (db * E + s) * (A - 1) + t - 1
                self.send(self.y, number, rows_, rows_, {"a": lax.rem(a + t, A)})

        def z_arrive(self, db):
            for s in range(1, E):
                rows_ = self.block(a, flip(b, db), lax.rem(e + E - s, E))
                self.arrived(self.z, db * (E - 1) + s - 1, self.buf.at[rows_])
                self.y_send(db, s)

        def y_arrive(self):
            for db in range(2):
                for s in range(E):
                    for t in range(1, A):
                        rows_ = self.block(
                            lax.rem(a + A - t, A), flip(b, db), lax.rem(e + E - s, E)
                        )
                        self.arrived(
                            self.y, (db * E + s) * (A - 1) + t - 1, self.buf.at[rows_]
                        )

        def add(self, landing, base, count):
            def load(k, cols, condition):
                copy = pltpu.make_async_copy(
                    landing.at[:, cols],
                    tm_ref.at[pl.ds(0, count), cols],
                    local_sem.at[SHARED + k],
                )
                when(condition, copy.start)

                def total():
                    copy.wait()

                    @pl.loop(0, count // 16)
                    def _(i):
                        here = pl.ds(pl.multiple_of(base + i * 16, 16), 16)
                        there = span(i * 16, 16)
                        self.buf[here, cols] = (
                            self.buf[here, cols].astype(F32) + tm_ref[there, cols].astype(F32)
                        ).astype(BF16)

                return lambda: when(condition, total)

            totals = []
            self.each(me, lambda *part: totals.append(load(*part)))
            for total in totals:
                total()

        def gy_send(self):
            for s in (*range(1, E), 0):
                for db in range(2):
                    for t in range(1, A):
                        to = lax.rem(a + t, A)
                        self.send(
                            self.gy,
                            (db * E + s) * (A - 1) + t - 1,
                            self.buf.at[self.block(to, flip(b, db), lax.rem(e + s, E))],
                            self.ylanding.at[t - 1, db, s],
                            {"a": to},
                        )

        def gy_add(self, db, s):
            bb, to = flip(b, db), lax.rem(e + s, E)
            for t in range(1, A):
                landing = self.ylanding.at[t - 1, db, s]
                self.arrived(self.gy, (db * E + s) * (A - 1) + t - 1, landing)
                self.add(landing, ((a * 2 + bb) * E + to) * 4 * self.R, 4 * self.R)
            if s:
                self.send(
                    self.gz,
                    db * (E - 1) + s - 1,
                    self.buf.at[self.block(a, bb, to)],
                    self.zlanding.at[s - 1, db],
                    {"e": to},
                )

        def gy_away(self, db):
            for s in range(1, E):
                self.gy_add(db, s)

        def home(self):
            for db in range(2):
                self.gy_add(db, 0)
            for db in range(2):
                self.gz_add(db)

        def gz_add(self, db):
            bb = flip(b, db)
            for s in range(1, E):
                landing = self.zlanding.at[s - 1, db]
                self.arrived(self.gz, db * (E - 1) + s - 1, landing)
                self.add(landing, ((a * 2 + bb) * E + e) * 4 * self.R, 4 * self.R)
            for r in range(4 * db, 4 * db + 4):
                _, df, dc = peers[r]
                ff, cc = flip(f, df), flip(c, dc)
                rows_ = self.buf.at[self.line(a, bb, e, ff, cc)]
                if r == 0:
                    pltpu.make_async_copy(rows_, self.out(me), local_sem.at[self.index]).start()
                else:
                    self.send(self.gtp, r, rows_, self.out(me), {"b": bb, "f": ff, "c": cc})

        def g_end(self):
            for r in range(GROUP):
                db, df, dc = peers[r]
                if r == 0:
                    pltpu.make_async_copy(
                        self.buf.at[self.line(a, b, e, f, c)],
                        self.out(me),
                        local_sem.at[self.index],
                    ).wait()
                else:
                    place = slot(flip(b, db), flip(f, df), flip(c, dc))
                    self.arrived(self.gtp, r, self.out(place), place)

    tile = uc - LANES
    shares = [(0, tile, False), (tile, LANES, True)]

    def quarter(ref, down, right):
        return lambda place: ref.at[
            span((down * GROUP + place) * R, R), pl.ds(right * uc, uc)
        ]

    def weight(index, parts, down, right, *rest):
        buf, ylanding, zlanding = rest
        piece, out = quarter(du_ref, down, right), quarter(hg_ref, down, right)
        return Weight(index, R, parts, piece, buf, out, ylanding, zlanding)

    s_w = Weight(
        0,
        16,
        [(0, LANES, False)],
        lambda place: sp_ref,
        ws_ref,
        lambda place: os_ref.at[place],
        ys_ref,
        zs_ref,
    )
    q_w = weight(1, [(0, qc, False)], 0, 0, wq_ref, yq_ref, zq_ref)
    g_w = weight(2, shares, 0, 1, wg_ref, yg_ref, zg_ref)
    u_w = weight(3, shares, 1, 0, wu_ref, yu_ref, zu_ref)
    o_w = weight(4, shares, 1, 1, wo_ref, yo_ref, zo_ref)

    hidden = fo_ref.shape[1]
    tiles = -(-hidden // LANES)
    tile_lane = lax.broadcasted_iota(jnp.int32, (R, LANES), 1)

    def lanes_of(ref, start, valid=LANES):
        def aligned(m):
            width_ = min(LANES, ref.shape[1] - m * LANES)
            part = ref[:, m * LANES : m * LANES + max(width_, 0)].astype(F32) if width_ > 0 else None
            if width_ >= LANES:
                return part
            if part is None:
                return jnp.zeros((R, LANES), F32)
            return jnp.concatenate([part, jnp.zeros((R, LANES - width_), F32)], axis=1)

        base, off = divmod(start, LANES)
        value = aligned(base)
        if off:
            back = LANES - off
            value = jnp.where(
                tile_lane < back,
                pltpu.roll(value, back, axis=1),
                pltpu.roll(aligned(base + 1), back, axis=1),
            )
        return jnp.where(tile_lane < valid, value, 0.0) if valid < LANES else value

    def member_tiles():
        for place in range(GROUP):
            first = place * (uc // LANES - 1) + min(place, larger)
            for k in range(uc // LANES - (place >= larger)):
                yield place, k, first + k

    def cut(ref, start, down, right):
        for place, k, number in member_tiles():
            at = (down * GROUP + place) * R, right * uc + k * LANES
            du_ref[at[0] : at[0] + R, at[1] : at[1] + LANES] = lanes_of(
                ref, start + number * LANES, min(LANES, hidden - number * LANES)
            ).astype(BF16)
        for place in range(larger, GROUP):
            at = (down * GROUP + place) * R, (right + 1) * uc - LANES
            du_ref[at[0] : at[0] + R, at[1] : at[1] + LANES] = jnp.zeros((R, LANES), BF16)

    def home_tiles(down, right):
        found = {}
        for place, k, number in member_tiles():
            at = (down * GROUP + place) * R, right * uc + k * LANES
            found[number] = at
        return lambda number: hg_ref[
            found[number][0] : found[number][0] + R, found[number][1] : found[number][1] + LANES
        ].astype(F32)

    def join(ref, groups):
        total = hidden * len(groups)
        for number in range(-(-total // LANES)):
            value = None
            for k, tile_of in enumerate(groups):
                shift = k * hidden % LANES
                first = number - k * hidden // LANES
                for piece in (first, first - 1) if shift else (first,):
                    if not 0 <= piece < tiles:
                        continue
                    start = k * hidden + piece * LANES - number * LANES
                    end = min(start + LANES, (k + 1) * hidden - number * LANES)
                    if start >= LANES or end <= 0:
                        continue
                    part = tile_of(piece)
                    if shift:
                        part = pltpu.roll(part, shift, axis=1)
                    if value is None:
                        value = part
                    else:
                        value = jnp.where((tile_lane >= start) & (tile_lane < end), part, value)
            size = min(LANES, total - number * LANES)
            ref[:, number * LANES : number * LANES + size] = value[:, :size].astype(BF16)

    def qkv_places():
        for place in range(GROUP):
            cc, bb, ff = place // 4, place // 2 % 2, place % 2
            for t in range(3):
                for i in range(sw // LANES):
                    number = i * 8 + bb * 4 + cc * 2 + ff
                    yield place * R, t * sw + i * LANES, t * width + number * LANES

    def cut_qkv():
        for row, col, start in qkv_places():
            du_ref[row : row + R, col : col + LANES] = fq_ref[:, start : start + LANES]

    def join_qkv():
        for row, col, start in qkv_places():
            fq_ref[:, start : start + LANES] = hg_ref[row : row + R, col : col + LANES]

    def remote(source, landing, send, recv, target):
        return pltpu.make_async_remote_copy(
            src_ref=source,
            dst_ref=landing,
            send_sem=send_sem.at[send],
            recv_sem=recv_sem.at[recv],
            device_id=target,
            device_id_type=DEVICE_MESH,
        )

    class Dense:
        def __init__(self):
            self.pieces = wd_ref.shape[0] // R
            self.first = wires.take(self.pieces)
            self.push = wires.take(1)
            self.zs = wires.take(self.pieces * (E - 1))
            self.ys = wires.take(self.pieces * (A - 1))
            self.gy = wires.take(self.pieces * (A - 1))
            self.gz = wires.take(self.pieces * (E - 1))
            self.back = wires.take(1)
            self.back_sends = wires.take(self.pieces)
            self.owners = []
            for piece in range(self.pieces):
                i, offset = piece * R // LANES, piece * R % LANES
                owner = ((i * 8 + b * 4 + c * 2 + f) * LANES + offset) // R
                self.owners.append(
                    {
                        "a": owner // (8 * E),
                        "b": lax.rem(owner // (4 * E), 2),
                        "e": lax.rem(owner // 4, E),
                        "f": lax.rem(owner // 2, 2),
                        "c": lax.rem(owner, 2),
                    }
                )

        def rows(self, piece):
            return wd_ref.at[pl.ds(piece * R, R)]

        def each(self, test, body):
            for piece, owner in enumerate(self.owners):
                same_a, same_e = owner["a"] == a, owner["e"] == e

                @pl.when(test(same_a, same_e))
                def _():
                    body(piece, owner)

        def local_or_remote(self, target, source, landing, send, recv, start):
            here = target["b"] == b
            for axis, mine in (("f", f), ("c", c)):
                here = here & (target[axis] == mine)
            away = remote(source, landing, send, recv, target)

            @pl.when(here)
            def _():
                if start:
                    pltpu.make_async_copy(source, landing, recv_sem.at[recv]).start()

            @pl.when(jnp.logical_not(here))
            def _():
                away.start() if start else away.wait_send()

        def out(self, start):
            first_row = rank(a, b, e, f, c) * R
            head = first_row // LANES
            piece = (head // 8) * (LANES // R) + lax.rem(first_row, LANES) // R
            target = {
                "b": lax.rem(head // 4, 2),
                "f": lax.rem(head, 2),
                "c": lax.rem(head // 2, 2),
            }
            landing = wd_ref.at[span(piece * R, R)]
            self.local_or_remote(target, dp_ref, landing, self.push, self.first + piece, start)

        def z(self, piece, s):
            rows_ = self.rows(piece)
            number = self.zs + piece * (E - 1) + s - 1
            return remote(rows_, rows_, number, self.first + piece, {"e": lax.rem(e + s, E)})

        def y(self, piece, t):
            rows_ = self.rows(piece)
            number = self.ys + piece * (A - 1) + t - 1
            return remote(rows_, rows_, number, self.first + piece, {"a": lax.rem(a + t, A)})

        def arrived(self, piece, _=None):
            wires.arrived(self.first + piece, self.rows(piece))

        def z_send(self):
            def body(piece, owner):
                self.arrived(piece)
                for s in range(1, E):
                    self.z(piece, s).start()

            self.each(lambda same_a, same_e: same_a & same_e, body)

        def y_send(self):
            self.each(lambda same_a, same_e: same_a & jnp.logical_not(same_e), self.arrived)

            def body(piece, owner):
                for t in range(1, A):
                    self.y(piece, t).start()

            self.each(lambda same_a, same_e: same_a, body)

        def y_arrive(self):
            self.each(lambda same_a, same_e: jnp.logical_not(same_a), self.arrived)

        def sent(self):
            self.out(False)

            def over_z(piece, owner):
                for s in range(1, E):
                    self.z(piece, s).wait_send()

            def over_y(piece, owner):
                for t in range(1, A):
                    self.y(piece, t).wait_send()

            self.each(lambda same_a, same_e: same_a & same_e, over_z)
            self.each(lambda same_a, same_e: same_a, over_y)

        def g_y(self, piece, t):
            to = lax.rem(a + t, A)
            number = self.gy + piece * (A - 1) + t - 1
            copy = remote(self.rows(piece), yd_ref.at[t - 1, piece], number, number, {"a": to})
            return to, copy

        def gy_send(self, start=True):
            for piece, owner in enumerate(self.owners):
                for t in range(1, A):
                    to, copy = self.g_y(piece, t)

                    @pl.when(owner["a"] == to)
                    def _():
                        copy.start() if start else copy.wait_send()

        def add(self, landing, piece):
            load = pltpu.make_async_copy(landing, td_ref, local_sem.at[SHARED])
            load.start()
            load.wait()

            @pl.loop(0, R // 16)
            def _(i):
                here, there = span(piece * R + i * 16, 16), span(i * 16, 16)
                wd_ref[here, :] = (
                    wd_ref[here, :].astype(F32) + td_ref[there, :].astype(F32)
                ).astype(BF16)

        def g_z(self, piece, s):
            to = lax.rem(e + s, E)
            number = self.gz + piece * (E - 1) + s - 1
            copy = remote(self.rows(piece), zd_ref.at[s - 1, piece], number, number, {"e": to})
            return to, copy

        def gz_send(self, start=True):
            for piece, owner in enumerate(self.owners):
                for s in range(1, E):
                    to, copy = self.g_z(piece, s)

                    @pl.when((owner["a"] == a) & (owner["e"] == to))
                    def _():
                        copy.start() if start else copy.wait_send()

        def gy_add(self):
            def body(piece, owner):
                for t in range(1, A):
                    landing = yd_ref.at[t - 1, piece]
                    wires.arrived(self.gy + piece * (A - 1) + t - 1, landing)
                    self.add(landing, piece)

            self.each(lambda same_a, same_e: same_a, body)
            self.gz_send()

        def home(self, piece, owner, start):
            target = {axis: owner[axis] for axis in ("b", "f", "c")}
            self.local_or_remote(
                target, self.rows(piece), od_ref, self.back_sends + piece, self.back, start
            )

        def gz_add(self):
            def body(piece, owner):
                for s in range(1, E):
                    landing = zd_ref.at[s - 1, piece]
                    wires.arrived(self.gz + piece * (E - 1) + s - 1, landing)
                    self.add(landing, piece)
                self.home(piece, owner, True)

            self.each(lambda same_a, same_e: same_a & same_e, body)

        def g_end(self):
            wires.arrived(self.back, od_ref)
            self.gy_send(False)
            self.gz_send(False)
            self.each(
                lambda same_a, same_e: same_a & same_e,
                lambda piece, owner: self.home(piece, owner, False),
            )

    dense = Dense()

    chain = wires.take(10), wires.take(10)
    to_b, to_f, to_c = {"b": 1 - b}, {"f": 1 - f}, {"c": 1 - c}
    nb, nf, dg = slot(1 - b, f, c), slot(b, 1 - f, c), slot(1 - b, 1 - f, c)

    class Gather:
        def __init__(self, buf, lean):
            self.buf, self.first, self.copies, self.lean = buf, chain[0], [], lean

        def part(self, place, which):
            if which is None:
                return self.buf.at[span(place * rows, rows)]
            return self.buf.at[span(place * rows + which * (rows // 2), rows // 2)]

        def copy(self, number, place, which, device):
            here = self.part(place, which)
            self.copies.append(wires.send(self.first + number, here, here, device))

        def landed(self, number, place, which):
            wires.arrived(self.first + number, self.part(place, which))

        def start(self):
            self.copy(0, me, 0, to_b)
            self.copy(1, me, 1, to_f)
            self.copy(2, me, 1, to_b)
            self.copy(3, me, 0, to_f)
            self.copy(4, me, None, to_c)

        def relay(self):
            if self.lean:
                self.landed(1, nf, 1)
                self.copy(6, nf, 1, to_b)
                self.landed(3, nf, 0)
                self.copy(5, nf, 0, to_b)
                self.copy(8, nf, None, to_c)
                self.landed(0, nb, 0)
                self.landed(2, nb, 1)
                self.copy(7, nb, None, to_c)
                return
            self.landed(0, nb, 0)
            self.copy(5, nb, 0, to_f)
            self.landed(1, nf, 1)
            self.copy(6, nf, 1, to_b)
            self.landed(2, nb, 1)
            self.copy(7, nb, None, to_c)
            self.landed(3, nf, 0)
            self.copy(8, nf, None, to_c)

        def finish(self):
            self.landed(5, dg, 0)
            self.landed(6, dg, 1)
            self.copy(9, dg, None, to_c)
            other = 1 - c
            self.landed(4, slot(b, f, other), None)
            self.landed(7, slot(1 - b, f, other), None)
            self.landed(8, slot(b, 1 - f, other), None)
            self.landed(9, slot(1 - b, 1 - f, other), None)

    step = 16
    places = [(1 - b, 1 - f), (1 - b, f), (b, 1 - f), (b, f)]

    def accumulate(target, at, count, terms):
        @pl.loop(0, count // step)
        def _(i):
            window = pl.ds(pl.multiple_of(at + i * step, step), step)
            total = terms[0][window, :].astype(F32)
            for term in terms[1:]:
                total = total + term[window, :].astype(F32)
            target[window, :] = total.astype(target.dtype)

    def scatter(multiply, lean, early=None, late=None):
        first, copies = chain[1], []

        def send(*copy):
            copies.append(wires.send(*copy))

        multiply((1 - c) * half_rows, half_rows)
        for k, (bb, ff) in enumerate(places):
            send(
                first + k,
                pb_ref.at[span(slot(bb, ff, 1 - c) * rows, rows)],
                core_ref.at[pl.ds(k * rows, rows)],
                to_c,
            )
        multiply(c * half_rows, half_rows)
        own = [pb_ref.at[span(slot(bb, ff, c) * rows, rows)] for bb, ff in places]
        core = [core_ref.at[pl.ds(k * rows, rows)] for k in range(4)]
        mid = rows // 2
        low, high = pl.ds(0, mid), pl.ds(mid, mid)
        early, late = (hook or (lambda: None) for hook in (early, late))
        wires.arrived(first, core[0])
        accumulate(stage_ref.at[0], 0, rows, [own[0], core[0]])
        if lean:
            send(first + 4, stage_ref.at[0], relay_ref, to_b)
            wires.arrived(first + 1, core[1])
            accumulate(stage_ref.at[1], 0, rows, [own[1], core[1]])
            send(first + 6, stage_ref.at[1], land_ref.at[0], to_b)
            early()
            wires.arrived(first + 2, core[2])
            wires.arrived(first + 4, relay_ref)
            accumulate(stage_ref.at[2], 0, rows, [own[2], core[2], relay_ref])
            send(first + 7, stage_ref.at[2], land_ref.at[1], to_f)
            late()
            wires.arrived(first + 3, core[3])
            wires.arrived(first + 6, land_ref.at[0])
            wires.arrived(first + 7, land_ref.at[1])
        else:
            send(first + 4, stage_ref.at[0, low], relay_ref.at[low], to_b)
            send(first + 5, stage_ref.at[0, high], relay_ref.at[high], to_f)
            wires.arrived(first + 1, core[1])
            accumulate(stage_ref.at[1], 0, mid, [own[1], core[1]])
            send(first + 6, stage_ref.at[1, low], land_ref.at[0, low], to_b)
            wires.arrived(first + 2, core[2])
            accumulate(stage_ref.at[2], mid, mid, [own[2], core[2]])
            send(first + 7, stage_ref.at[2, high], land_ref.at[1, high], to_f)
            early()
            wires.arrived(first + 5, relay_ref.at[high])
            accumulate(stage_ref.at[1], mid, mid, [own[1], core[1], relay_ref])
            send(first + 8, stage_ref.at[1, high], land_ref.at[0, high], to_b)
            wires.arrived(first + 4, relay_ref.at[low])
            accumulate(stage_ref.at[2], 0, mid, [own[2], core[2], relay_ref])
            send(first + 9, stage_ref.at[2, low], land_ref.at[1, low], to_f)
            late()
            wires.arrived(first + 3, core[3])
            wires.arrived(first + 6, land_ref.at[0, low])
            wires.arrived(first + 7, land_ref.at[1, high])
            wires.arrived(first + 8, land_ref.at[0, high])
            wires.arrived(first + 9, land_ref.at[1, low])
        accumulate(sum_ref, 0, rows, [own[3], core[3], land_ref.at[0], land_ref.at[1]])
        sent(copies)

    def blocks(count_m, count_n, body):
        @pl.loop(0, count_m * count_n)
        def _(k):
            body(k // count_n, lax.rem(k, count_n))

    def onto_partial(*terms):
        def multiply(first, count):
            def body(m, n):
                here = pl.ds(pl.multiple_of(first, half_rows) + m * 512, 512)
                there = span(n * 512, 512)
                total = sum(dot(left[here, :], weight[there, :], NT) for left, weight in terms)
                pb_ref[here, there] = total.astype(BF16)

            blocks(count // 512, width // 512, body)

        return multiply

    loads[0].wait()
    cut_qkv()
    q_w.tp_send()
    s_w.tp_send()
    dense.out(True)
    own_x = pltpu.make_async_copy(
        x_ref.at[0], xg_ref.at[my_rows, pl.ds(0, width)], local_sem.at[5]
    )
    own_x.start()
    sg_ref[...] = jnp.zeros_like(sg_ref)

    @pl.when(me >= larger)
    def _():
        for weight in (g_w, u_w, o_w):
            weight.buf[:, tile:] = jnp.zeros((width, LANES), BF16)

    at = lax.broadcasted_iota(jnp.int32, (rows, LANES), 0)
    lane = lax.broadcasted_iota(jnp.int32, (rows, LANES), 1)
    docs = len_ref.shape[1]
    key, prefix_at, local_pos, valid, first = at + docs, at * 0, at * 0, at < 0, 0
    for k in range(docs):
        last = first + len_ref[0, k]
        member = (at >= first) & (at < last)
        key = jnp.where(member, k, key)
        prefix_at = jnp.where(member, pre_ref[0, k], prefix_at)
        local_pos = jnp.where(member, at - first, local_pos)
        valid = valid | member
        first = last
    info = jnp.where(lane == 0, key, jnp.where(lane == 1, prefix_at, local_pos))
    xg_ref[my_rows, width:] = info.astype(F32).astype(BF16)
    valid_ref[...] = jnp.where(valid, 1.0, 0.0)

    loads[1].wait()
    cut(fi_ref, 0, 0, 1)
    tokens = Gather(xg_ref, True)
    for db in range(2):
        q_w.tp_wait(db)
        q_w.z_send(db)
        q_w.y_send(db, 0)
    own_x.wait()
    tokens.start()
    g_w.tp_send()
    cut(fi_ref, hidden, 1, 0)
    loads[2].wait()
    cut(fo_ref, 0, 1, 1)
    for db in range(2):
        s_w.tp_wait(db)
        s_w.z_send(db)
        s_w.y_send(db, 0)
    dense.z_send()
    u_w.tp_send()
    q_w.z_arrive(0)
    tokens.relay()
    g_w.tp_wait(0)
    g_w.z_send(0)
    g_w.y_send(0, 0)
    q_w.z_arrive(1)
    s_w.z_arrive(0)
    s_w.z_arrive(1)
    dense.y_send()
    g_w.tp_wait(1)
    g_w.z_send(1)
    g_w.y_send(1, 0)
    tokens.finish()
    o_w.tp_send()
    for db in range(2):
        u_w.tp_wait(db)
        u_w.y_send(db, 0)
    s_w.y_arrive()
    q_w.y_arrive()

    lane = lane[0:16, :]

    @pl.loop(0, width // LANES)
    def _(k):
        line = jnp.zeros((16, LANES), F32)
        for j in range(LANES // R):
            part = ws_ref[span((k * (LANES // R) + j) * 16, 16), :].astype(F32)
            if j:
                part = pltpu.roll(part, j * R, axis=1)
            line = jnp.where(lane // R == j, part, line)
        bt_ref[:, span(k * LANES, LANES)] = line

    heads = [i * 8 + b * 4 + c * 2 + f for i in range(sw // LANES)]
    for t in range(3):
        for i, number in enumerate(heads):
            at = t * sw + i * LANES
            qb_ref[0:1, at : at + LANES] = bt_ref[t : t + 1, span(number * LANES, LANES)]

    def projection(m, n):
        here, cols = span(m * 512, 512), span(n * sw, sw)
        uf_ref[here, cols] = (
            dot(xg_ref[here, 0:width], wq_ref[:, cols]) + qb_ref[0:1, cols]
        )

    blocks(all_rows // 512, 3, projection)

    loads[3].wait()
    row_at = lax.broadcasted_iota(jnp.int32, (rows, rows), 0)
    col_at = lax.broadcasted_iota(jnp.int32, (rows, rows), 1)

    def sequence(s):
        here = span(s * rows, rows)
        info = xg_ref[here, width : width + LANES].astype(F32)
        turned = info.T
        allowed = (info[:, 0:1] == turned[0:1, :]) & (
            (turned[2:3, :] < info[:, 1:2]) | (col_at <= row_at)
        )
        picked = (info[:, 2:3] == col_at.astype(F32)).astype(BF16)
        parts = dot(picked, table_ref[...])
        cos_sin = parts[:, 0:LANES] + parts[:, LANES : 2 * LANES] + parts[:, 2 * LANES :]
        swapped = pltpu.roll(cos_sin, LANES // 2, axis=1)
        first = col_at < LANES // 2
        cosine = jnp.where(first, cos_sin, swapped)
        sine = jnp.where(first, -swapped, cos_sin)
        return here, allowed, cosine, sine

    def turn(value, cosine, sine):
        return value * cosine + pltpu.roll(value, LANES // 2, axis=1) * sine

    def softmax(q, k, allowed):
        scores = jnp.where(allowed, scale * dot(q, k, NT), MASKED_SCORE)
        power = jnp.exp(scores - jnp.max(scores, axis=1, keepdims=True))
        return power / jnp.sum(power, axis=1, keepdims=True)

    @pl.loop(0, GROUP)
    def _(s):
        here, allowed, cosine, sine = sequence(s)
        for i in range(sw // LANES):
            cols = [pl.ds(t * sw + i * LANES, LANES) for t in range(3)]
            q = turn(uf_ref[here, cols[0]], cosine, sine).astype(BF16)
            k = turn(uf_ref[here, cols[1]], cosine, sine).astype(BF16)
            v = uf_ref[here, cols[2]].astype(BF16)
            qk_ref[here, cols[0]] = q
            qk_ref[here, cols[1]] = k
            qk_ref[here, cols[2]] = v
            probs = softmax(q, k, allowed).astype(BF16)
            cx_ref[here, i * LANES : (i + 1) * LANES] = dot(probs, v).astype(BF16)

    u_w.z_send(0)
    g_w.z_arrive(0)
    dense.y_arrive()

    def dense_partial(first, count):
        def body(m, n):
            here = pl.ds(pl.multiple_of(first, half_rows) + m * 512, 512)
            cols = span(n * 512, 512)
            pb_ref[here, cols] = dot(cx_ref[here, :], wd_ref[:, cols]).astype(BF16)

        blocks(count // 512, width // 512, body)

    def more_units():
        u_w.z_send(1)
        for db in range(2):
            o_w.tp_wait(db)
            o_w.y_send(db, 0)

    scatter(dense_partial, True, lambda: g_w.z_arrive(1), more_units)

    def row_loop(body):
        @pl.loop(0, rows // 16)
        def _(i):
            body(span(i * 16, 16), span(me * rows + i * 16, 16))

    def normalize(value):
        centered = value - jnp.mean(value, axis=1, keepdims=True)
        rstd = lax.rsqrt(jnp.mean(centered * centered, axis=1, keepdims=True) + EPSILON)
        return centered * rstd, rstd

    def first_norm(here, there):
        value = (
            alpha * xg_ref[there, 0:width].astype(F32) + sum_ref[here, :] + bt_ref[3:4, :]
        )
        unit, rstd = normalize(value)
        xh_ref[here, :] = unit
        rstd_ref[here, :] = jnp.broadcast_to(rstd, (16, LANES))
        hg_ref[there, :] = (unit * bt_ref[7:8, :] + bt_ref[4:5, :]).astype(BF16)

    row_loop(first_norm)
    normed = Gather(hg_ref, True)
    sent(tokens.copies)
    normed.start()
    for db in range(2):
        o_w.z_send(db)
    u_w.z_arrive(0)
    normed.relay()
    u_w.z_arrive(1)
    normed.finish()
    o_w.z_arrive(0)
    g_w.y_arrive()
    u_w.y_arrive()

    def units(m, n):
        here = pl.ds(m * 512, 512)
        gate_cols = span(n * 256, 256)
        up_cols = span(uc + n * 256, 256)
        left = hg_ref[here, :]
        gate = dot(left, wg_ref[:, gate_cols])
        up = dot(left, wu_ref[:, gate_cols])
        cdf = 0.5 * (1.0 + lax.erf(gate * (0.5**0.5)))
        density = jnp.exp(-0.5 * gate * gate) * (1.0 / math.sqrt(2.0 * math.pi))
        act = gate * cdf
        mb_ref[here, gate_cols] = (act * up).astype(BF16)
        uf_ref[here, gate_cols] = (cdf + gate * density) * up
        uf_ref[here, up_cols] = act

    for m in range(all_rows // 512):
        blocks(1, uc // 256, lambda _, n: units(m, n))
        if m == 0:
            o_w.z_arrive(1)
    o_w.y_arrive()
    scatter(onto_partial((mb_ref, wo_ref)), False)

    def add_row(row, value):
        sg_ref[row : row + 1, :] += jnp.sum(value, axis=0, keepdims=True)

    def norm_back(grad, gain, unit, rstd):
        scaled = grad * gain
        return rstd * (
            scaled
            - jnp.mean(scaled, axis=1, keepdims=True)
            - unit * jnp.mean(scaled * unit, axis=1, keepdims=True)
        )

    def second_norm(here, there):
        normed_one = xh_ref[here, :] * bt_ref[7:8, :] + bt_ref[4:5, :]
        unit, rstd = normalize(alpha * normed_one + sum_ref[here, :] + bt_ref[5:6, :])
        out_ref[here, :] = (unit * bt_ref[8:9, :] + bt_ref[6:7, :]).astype(BF16)
        grad = cot_ref[here, :].astype(F32) * valid_ref[here, 0:1]
        back = norm_back(grad, bt_ref[8:9, :], unit, rstd)
        low = back.astype(BF16)
        dr_ref[here, :] = back
        dg_ref[there, :] = low
        add_row(5, low.astype(F32))
        add_row(6, grad)
        add_row(8, grad * unit)

    loads[4].wait()
    row_loop(second_norm)
    results[0].start()
    branch = Gather(dg_ref, False)
    sent(normed.copies)
    branch.start()
    branch.relay()
    branch.finish()

    def units_back(m, n):
        here = span(m * 512, 512)
        gate_cols, up_cols = span(n * 256, 256), span(uc + n * 256, 256)
        grad = dot(dg_ref[here, :], wo_ref[:, gate_cols])
        du_ref[here, gate_cols] = (uf_ref[here, gate_cols] * grad).astype(BF16)
        du_ref[here, up_cols] = (uf_ref[here, up_cols] * grad).astype(BF16)

    def weight_grad(left, right, target, cols, bn):
        def body(m, n):
            here, there = span(m * 512, 512), span(n * bn, bn)
            target[here, there] = dot(left[:, here], right[:, there], TN).astype(BF16)

        blocks(width // 512, cols // bn, body)

    for flow in (normed, q_w, g_w, u_w, o_w):
        sent(flow.copies)
    weight_grad(dg_ref, mb_ref, go_ref, uc, uc)
    o_w.buf = go_ref
    o_w.gy_send()
    blocks(all_rows // 512, uc // 256, units_back)

    du_gate = du_ref.at[:, pl.ds(0, uc)]
    du_up = du_ref.at[:, pl.ds(uc, uc)]

    def in_grad():
        for weight, right in ((g_w, du_gate), (u_w, du_up)):
            weight_grad(hg_ref, right, weight.buf, uc, uc)
            weight.gy_send()
            if weight is g_w:
                o_w.gy_away(0)

    sent(branch.copies)
    scatter(
        onto_partial((du_gate, wg_ref), (du_up, wu_ref)), False, in_grad, lambda: o_w.gy_away(1)
    )

    def first_norm_back(here, there):
        grad = alpha * dr_ref[here, :] + sum_ref[here, :]
        unit = xh_ref[here, :]
        back = norm_back(grad, bt_ref[7:8, :], unit, rstd_ref[here, 0:1])
        low = back.astype(BF16)
        dr_ref[here, :] = back
        dg_ref[there, :] = low
        add_row(3, low.astype(F32))
        add_row(4, grad)
        add_row(7, grad * unit)

    row_loop(first_norm_back)
    attended = Gather(dg_ref, False)
    attended.start()
    g_w.gy_away(0)
    attended.relay()
    g_w.gy_away(1)
    attended.finish()

    def context_back(m, n):
        here = span(m * 512, 512)
        dc_ref[here, :] = dot(dg_ref[here, :], wd_ref[...], NT).astype(BF16)

    blocks(all_rows // 512, 1, context_back)

    def dense_grad(m, n):
        cols = span(n * 512, 512)
        wd_ref[:, cols] = dot(cx_ref[...], dg_ref[:, cols], TN).astype(BF16)

    dense.sent()
    blocks(1, width // 512, dense_grad)
    dense.gy_send()
    u_w.gy_away(0)
    o_w.home()

    @pl.loop(0, GROUP)
    def _(s):
        here, allowed, cosine, sine = sequence(s)
        for i, number in enumerate(heads):
            cols = [pl.ds(t * sw + i * LANES, LANES) for t in range(3)]
            q, k, v = (qk_ref[here, one] for one in cols)
            grad = dc_ref[here, i * LANES : (i + 1) * LANES]
            probs = softmax(q, k, allowed)
            d_probs = dot(grad, v, NT)
            d_value = dot(probs.astype(BF16), grad, TN)
            d_scores = probs * (d_probs - jnp.sum(probs * d_probs, axis=1, keepdims=True))
            low = jnp.where(allowed, d_scores, 0.0).astype(BF16)
            d_query = turn(scale * dot(low, k), cosine, -sine)
            d_key = turn(scale * dot(low, q, TN), cosine, -sine)
            for t, value in enumerate((d_query, d_key, d_value)):
                value = value.astype(BF16)
                mb_ref[here, cols[t]] = value
                lanes = span(number * LANES, LANES)
                sg_ref[t : t + 1, lanes] += jnp.sum(value.astype(F32), axis=0, keepdims=True)

    u_w.gy_away(1)

    def late_adds():
        q_w.gy_away(0)
        q_w.gy_away(1)
        g_w.home()

    def qkv_grad():
        weight_grad(xg_ref, mb_ref, wq_ref, qc, qc)

        q_w.gy_send()
        sent(s_w.copies)

        @pl.loop(0, width // LANES)
        def _(k):
            line = sg_ref[:, span(k * LANES, LANES)]
            for j in range(LANES // R):
                part = line if j == 0 else pltpu.roll(line, LANES - j * R, axis=1)
                ws_ref[span((k * (LANES // R) + j) * 16, 16), :] = part.astype(BF16)

        s_w.gy_send()
        dense.gy_add()

    scatter(onto_partial((mb_ref, wq_ref)), True, qkv_grad, late_adds)

    def tokens_back(here, there):
        gx_ref[here, :] = alpha * dr_ref[here, :] + sum_ref[here, :]

    row_loop(tokens_back)
    results[1].start()

    for db in range(2):
        s_w.gy_away(db)
    u_w.home()
    for db in range(2):
        q_w.gy_add(db, 0)
        s_w.gy_add(db, 0)
    for db in range(2):
        q_w.gz_add(db)
    for db in range(2):
        s_w.gz_add(db)
    dense.gz_add()
    o_w.g_end()
    join(fo_ref, [home_tiles(1, 1)])
    results[2].start()
    g_w.g_end()
    u_w.g_end()
    join(fi_ref, [home_tiles(0, 1), home_tiles(1, 0)])
    results[3].start()
    q_w.g_end()
    join_qkv()
    results[4].start()
    s_w.g_end()
    small_ref[...] = sum(os_ref[place].astype(F32) for place in range(GROUP))
    dense.g_end()
    for result in results:
        result.wait()
    for flow in (q_w, g_w, u_w, o_w, s_w, tokens, attended):
        sent(flow.copies)


def final_kernel(count, plain, *refs):
    small_ref, bias_ref, gain_ref = refs[0], refs[1 + count], refs[2 + count]
    refs = refs[1 : 1 + count] + refs[3 + count :]
    sources, targets, held = (refs[k * count : (k + 1) * count] for k in range(3))
    wide = refs[3 * count : -2]
    load_sem, store_sem = refs[-2:]
    loads = [
        pltpu.make_async_copy(source, one, load_sem.at[k])
        for k, (source, one) in enumerate(zip(sources, held))
    ]
    for one in loads:
        one.start()
    cut, own = bias_ref.shape
    bias_ref[...] = small_ref[0:cut, 0:own]
    gain_ref[...] = small_ref[cut : cut + gain_ref.shape[0], 0:own]
    stores = []
    for k, load in enumerate(loads):
        load.wait()
        found = held[k]
        if k >= plain:
            found = wide[k - plain]
            found[...] = held[k][...].astype(F32)
        stores.append(pltpu.make_async_copy(found, targets[k], store_sem.at[k]))
        stores[-1].start()
    for one in stores:
        one.wait()


def finish(small, cuts, plain, narrow):
    shape, anywhere = jax.ShapeDtypeStruct, pl.BlockSpec(memory_space=pl.ANY)
    vmem = pl.BlockSpec(memory_space=pltpu.VMEM)
    arrays = [*plain, *narrow]
    count = len(arrays)
    return pl.pallas_call(
        functools.partial(final_kernel, count, len(plain)),
        out_shape=[shape(cut, F32) for cut in cuts]
        + [shape(one.shape, one.dtype) for one in plain]
        + [shape(one.shape, F32) for one in narrow],
        in_specs=[vmem] + [anywhere] * count,
        out_specs=[vmem] * 2 + [anywhere] * count,
        scratch_shapes=[pltpu.VMEM(one.shape, one.dtype) for one in arrays]
        + [pltpu.VMEM(one.shape, F32) for one in narrow]
        + [pltpu.SemaphoreType.DMA((count,)), pltpu.SemaphoreType.DMA((count,))],
        compiler_params=pltpu.CompilerParams(vmem_limit_bytes=63 << 20),
    )(small, *arrays)


def on_device(
    tokens,
    cotangent,
    lengths,
    prefix,
    qkv_weight,
    dense_weight,
    ffin_weight,
    ffout_weight,
    biases,
    norm_gains,
):
    _, rows, width = tokens.shape
    A, E = lax.axis_size("a"), lax.axis_size("e")
    R = qkv_weight.shape[0]
    head_dim = width // HEADS
    my_heads = HEADS // GROUP
    hidden = ffout_weight.shape[1]
    sw = my_heads * head_dim
    qc = 3 * sw

    inverse = np.float32(ROPE_BASE) ** (
        -np.arange(head_dim // 2, dtype=np.float32) * np.float32(2.0 / head_dim)
    )
    angles = np.arange(rows, dtype=np.float32)[:, None] * inverse.astype(np.float32)
    rest = np.concatenate([np.cos(angles), np.sin(angles)], axis=1).astype(np.float32)
    terms = []
    for _ in range(3):
        terms.append(rest.astype(BF16))
        rest = rest - terms[-1].astype(np.float32)
    table = jnp.asarray(np.concatenate(terms, axis=1))

    small = jnp.concatenate([biases, norm_gains], axis=1).T
    small = jnp.pad(small, ((0, 16 - small.shape[0]), (0, LANES - R)))

    tiles = -(-hidden // LANES)
    larger = tiles % GROUP
    uc = (tiles // GROUP + 1) * LANES
    wires = 8 * (2 * GROUP + 4 * (E - 1) + 4 * E * (A - 1))
    wires += (sw // R) * 2 * (A + E) + 2 + 2 * 10
    group_rows = GROUP * rows
    sizes = (A, E, R, rows, width, sw, uc, larger, (2.0 * LAYERS) ** 0.5, head_dim ** (-0.5))
    shape = jax.ShapeDtypeStruct
    anywhere, vmem = pl.BlockSpec(memory_space=pl.ANY), pl.BlockSpec(memory_space=pltpu.VMEM)
    landings = [(64, LANES), (4 * R, qc), None] + [(4 * R, uc)] * 3
    dense_landing = (sw // R, R, width)
    results = pl.pallas_call(
        functools.partial(layer_kernel, sizes),
        out_shape=[
            shape((16, LANES), F32),
            shape((rows, width), BF16),
            shape((rows, width), F32),
            shape((R, 3 * width), BF16),
            shape((R, 2 * hidden), BF16),
            shape((R, hidden), BF16),
            shape((R, width), BF16),
        ]
        + [
            shape((A - 1,) + ((2, E) + one if one else dense_landing), BF16)
            for one in landings
        ]
        + [
            shape((E - 1,) + ((2,) + one if one else dense_landing), BF16)
            for one in landings
        ],
        in_specs=[pl.BlockSpec(memory_space=pltpu.SMEM)] * 2 + [anywhere] * 8,
        out_specs=[vmem] + [anywhere] * 18,
        scratch_shapes=[
            pltpu.VMEM((rows, width), BF16),
            pltpu.VMEM((rows, width), F32),
            pltpu.VMEM((R, 3 * width), BF16),
            pltpu.VMEM((R, 2 * hidden), BF16),
            pltpu.VMEM((R, hidden), BF16),
            pltpu.VMEM((rows, width), BF16),
            pltpu.VMEM((rows, 3 * LANES), BF16),
            pltpu.VMEM((GROUP, 16, LANES), BF16),
            pltpu.VMEM((width // R * 16, LANES), BF16),
            pltpu.VMEM((width, qc), BF16),
            pltpu.VMEM((sw, width), BF16),
            pltpu.VMEM((width, uc), BF16),
            pltpu.VMEM((width, uc), BF16),
            pltpu.VMEM((width, uc), BF16),
            pltpu.VMEM((width, uc), BF16),
            pltpu.VMEM((group_rows, width + LANES), BF16),
            pltpu.VMEM((group_rows, width), BF16),
            pltpu.VMEM((group_rows, width), BF16),
            pltpu.VMEM((group_rows, 2 * uc), F32),
            pltpu.VMEM((group_rows, uc), BF16),
            pltpu.VMEM((group_rows, 2 * uc), BF16),
            pltpu.VMEM((group_rows, qc), BF16),
            pltpu.VMEM((group_rows, sw), BF16),
            pltpu.VMEM((group_rows, sw), BF16),
            pltpu.VMEM((group_rows, width), BF16),
            pltpu.VMEM((4 * rows, width), BF16),
            pltpu.VMEM((3, rows, width), BF16),
            pltpu.VMEM((rows, width), BF16),
            pltpu.VMEM((2, rows, width), BF16),
            pltpu.VMEM((rows, width), F32),
            pltpu.VMEM((rows, width), F32),
            pltpu.VMEM((rows, width), F32),
            pltpu.VMEM((rows, LANES), F32),
            pltpu.VMEM((rows, LANES), F32),
            pltpu.VMEM((16, width), F32),
            pltpu.VMEM((16, width), F32),
            pltpu.VMEM((8, qc), F32),
            pltpu.VMEM((4 * R, max(uc, qc)), BF16),
            pltpu.VMEM((R, width), BF16),
            pltpu.SemaphoreType.DMA((SHARED + 12,)),
            pltpu.SemaphoreType.DMA((wires,)),
            pltpu.SemaphoreType.DMA((wires,)),
        ],
        compiler_params=pltpu.CompilerParams(
            collective_id=0, has_side_effects=True, vmem_limit_bytes=63 << 20
        ),
    )(
        lengths,
        prefix,
        cotangent,
        table,
        small,
        tokens,
        qkv_weight,
        dense_weight,
        ffin_weight,
        ffout_weight,
    )
    small_grads, result, d_tokens, qkv_grad, ffin_grad, ffout_grad, dense_grad = results[:7]
    bias_grad, gain_grad, result, d_tokens, ffin_grad, qkv_grad, ffout_grad, dense_grad = finish(
        small_grads,
        (biases.shape[::-1], norm_gains.shape[::-1]),
        [result, d_tokens],
        [ffin_grad, qkv_grad, ffout_grad, dense_grad],
    )
    return (
        result.reshape(tokens.shape),
        d_tokens.reshape(tokens.shape),
        qkv_grad,
        dense_grad,
        ffin_grad,
        ffout_grad,
        bias_grad.T,
        gain_grad.T,
    )


def solution(mesh):
    dp, fsdp = mesh.shape["dp"], mesh.shape["fsdp"]
    fine = Mesh(mesh.devices.reshape(dp // 2, 2, fsdp // 4, 2, 2), AXES)
    cube, flat = P(AXES, None, None), P(AXES, None)
    return jax.shard_map(
        on_device,
        mesh=fine,
        in_specs=(cube, cube) + (flat,) * 8,
        out_specs=(cube, cube) + (flat,) * 6,
        check_vma=False,
    )
```

```python
import functools
import math

import jax
import jax.numpy as jnp
import numpy as np
from jax import lax
from jax.experimental import pallas as pl
from jax.experimental.pallas import tpu as pltpu
from jax.sharding import Mesh
from jax.sharding import PartitionSpec as P

HEADS = 16
LAYERS = 24
MASKED_SCORE = -1e30
EPSILON = 1e-05
ROPE_BASE = 10000.0

AXES = ("a", "b", "e", "f", "c")
GROUP = 8
LANES = 128
SHARED = 6
DEVICE_MESH = pl.DeviceIdType.MESH
BF16 = jnp.bfloat16
F32 = jnp.float32
NT = (((1,), (1,)), ((), ()))
TN = (((0,), (0,)), ((), ()))


def dot(left, right, dims=(((1,), (0,)), ((), ()))):
    return lax.dot_general(left, right, dims, preferred_element_type=F32)


def span(start, size):
    return pl.ds(pl.multiple_of(start, size), size)


class Wires:
    def __init__(self, send_sem, recv_sem):
        self.send_sem, self.recv_sem, self.count, self.outs = send_sem, recv_sem, 0, 0

    def take(self, numbers=1):
        first = self.count
        self.count += numbers
        return first

    def out(self, numbers=1):
        first = self.outs
        self.outs += numbers
        return first

    def send(self, out, number, source, target, device, condition=None):
        one = pltpu.make_async_remote_copy(
            src_ref=source,
            dst_ref=target,
            send_sem=self.send_sem.at[out],
            recv_sem=self.recv_sem.at[number],
            device_id=device,
            device_id_type=DEVICE_MESH,
        )
        when(condition, one.start)
        return condition, one

    def arrived(self, number, landing, condition=None):
        when(condition, pltpu.make_async_copy(landing, landing, self.recv_sem.at[number]).wait)


def when(condition, body):
    if condition is None:
        body()
    else:
        pl.when(condition)(body)


def sent(copies):
    for condition, one in copies:
        when(condition, one.wait_send)
    copies.clear()


def layer_kernel(
    sizes,
    len_ref,
    pre_ref,
    ct_ref,
    tb_ref,
    sp_ref,
    x_ref,
    rq_ref,
    dp_ref,
    ri_ref,
    ro_ref,
    small_ref,
    eo_ref,
    ex_ref,
    eq_ref,
    ei_ref,
    ef_ref,
    od_ref,
    ys_ref,
    yq_ref,
    yd_ref,
    yg_ref,
    yu_ref,
    yo_ref,
    zs_ref,
    zq_ref,
    zd_ref,
    zg_ref,
    zu_ref,
    zo_ref,
    out_ref,
    gx_ref,
    fq_ref,
    fi_ref,
    fo_ref,
    cot_ref,
    table_ref,
    os_ref,
    ws_ref,
    wq_ref,
    wd_ref,
    wg_ref,
    wu_ref,
    wo_ref,
    go_ref,
    xg_ref,
    hg_ref,
    dg_ref,
    uf_ref,
    mb_ref,
    du_ref,
    qk_ref,
    cx_ref,
    dc_ref,
    pb_ref,
    core_ref,
    stage_ref,
    relay_ref,
    land_ref,
    sum_ref,
    xh_ref,
    dr_ref,
    rstd_ref,
    valid_ref,
    bt_ref,
    sg_ref,
    qb_ref,
    tm_ref,
    td_ref,
    local_sem,
    send_sem,
    recv_sem,
):
    A, E, R, rows, width, sw, uc, larger, alpha, scale = sizes
    a, b, e, f, c = (lax.axis_index(axis) for axis in AXES)
    qc = 3 * sw
    all_rows = GROUP * rows
    half_rows = all_rows // 2
    slot = lambda bb, ff, cc: cc * 4 + bb * 2 + ff
    me = slot(b, f, c)
    my_rows = span(me * rows, rows)
    flip = lambda v, d: lax.rem(v + d, 2)
    rank = lambda aa, bb, ee, ff, cc: (((aa * 2 + bb) * E + ee) * 2 + ff) * 2 + cc
    wires = Wires(send_sem, recv_sem)
    peers = [(r // 4, r // 2 % 2, r % 2) for r in range(GROUP)]

    loads = [
        pltpu.make_async_copy(raw, final, local_sem.at[SHARED + 2 + k])
        for k, (raw, final) in enumerate(
            (
                (rq_ref, fq_ref),
                (ri_ref, fi_ref),
                (ro_ref, fo_ref),
                (tb_ref, table_ref),
                (ct_ref.at[0], cot_ref),
            )
        )
    ]
    results = [
        pltpu.make_async_copy(found, result, local_sem.at[SHARED + 7 + k])
        for k, (found, result) in enumerate(
            (
                (out_ref, eo_ref),
                (gx_ref, ex_ref),
                (fo_ref, ef_ref),
                (fi_ref, ei_ref),
                (fq_ref, eq_ref),
            )
        )
    ]
    for load in loads:
        load.start()

    barrier = pltpu.get_barrier_semaphore()
    others = 0
    for da in range(A):
        for de in range(E):
            for db, df, dc in peers:
                if da + de + db + df + dc:
                    pl.semaphore_signal(
                        barrier,
                        inc=1,
                        device_id={
                            "a": lax.rem(a + da, A),
                            "b": flip(b, db),
                            "e": lax.rem(e + de, E),
                            "f": flip(f, df),
                            "c": flip(c, dc),
                        },
                        device_id_type=DEVICE_MESH,
                    )
                    others += 1
    pl.semaphore_wait(barrier, others)

    class Weight:
        def __init__(self, index, R, parts, piece, buf, out, ylanding, zlanding):
            self.index, self.R, self.parts, self.buf = index, R, parts, buf
            self.piece, self.out = piece, out
            self.ylanding, self.zlanding = ylanding, zlanding
            self.copies, self.shared, self.way = [], wires.out(2), 0
            take = lambda count: wires.take(count * len(parts))
            self.tp, self.z, self.y = take(GROUP), take(2 * (E - 1)), take(2 * E * (A - 1))
            self.gtp, self.gz, self.gy = take(GROUP), take(2 * (E - 1)), take(2 * E * (A - 1))

        def each(self, member, body):
            for k, (first, size, extra) in enumerate(self.parts):
                body(k, pl.ds(first, size), member < larger if extra else None)

        def send(self, first, number, source, target, device, member=me):
            def body(k, cols, condition):
                if condition is None:
                    out, copies = self.shared + self.way, []
                else:
                    out, copies = wires.out(), self.copies
                copies.append(
                    wires.send(
                        out,
                        first + number * len(self.parts) + k,
                        source.at[:, cols],
                        target.at[:, cols],
                        device,
                        condition,
                    )
                )

            self.each(member, body)

        def arrived(self, first, number, landing, member=me):
            def body(k, cols, condition):
                wires.arrived(
                    first + number * len(self.parts) + k, landing.at[:, cols], condition
                )

            self.each(member, body)

        def sent(self):
            first, size, _ = self.parts[0]
            rows_ = self.buf.at[pl.ds(0, (A * E * GROUP - 1) * self.R), pl.ds(first, size)]
            pltpu.make_async_copy(rows_, rows_, send_sem.at[self.shared + self.way]).wait()
            sent(self.copies)
            self.way = 1

        def line(self, aa, bb, ee, ff, cc):
            return span(rank(aa, bb, ee, ff, cc) * self.R, self.R)

        def block(self, aa, bb, ee):
            return span(((aa * 2 + bb) * E + ee) * 4 * self.R, 4 * self.R)

        def own(self):
            return pltpu.make_async_copy(
                self.piece(me), self.buf.at[self.line(a, b, e, f, c)], local_sem.at[self.index]
            )

        def tp_send(self):
            self.own().start()
            for r in range(1, GROUP):
                db, df, dc = peers[r]
                bb, ff, cc = flip(b, db), flip(f, df), flip(c, dc)
                place = slot(bb, ff, cc)
                self.send(
                    self.tp,
                    r,
                    self.piece(place),
                    self.buf.at[self.line(a, b, e, f, c)],
                    {"b": bb, "f": ff, "c": cc},
                    place,
                )

        def tp_wait(self, db):
            for r in range(4 * db, 4 * db + 4):
                if r == 0:
                    self.own().wait()
                else:
                    _, df, dc = peers[r]
                    rows_ = self.line(a, flip(b, db), e, flip(f, df), flip(c, dc))
                    self.arrived(self.tp, r, self.buf.at[rows_])

        def z_send(self, db):
            rows_ = self.buf.at[self.block(a, flip(b, db), e)]
            for s in range(1, E):
                self.send(self.z, db * (E - 1) + s - 1, rows_, rows_, {"e": lax.rem(e + s, E)})

        def y_send(self, db, s):
            rows_ = self.buf.at[self.block(a, flip(b, db), lax.rem(e + E - s, E))]
            for t in range(1, A):
                number = (db * E + s) * (A - 1) + t - 1
                self.send(self.y, number, rows_, rows_, {"a": lax.rem(a + t, A)})

        def z_arrive(self, db):
            for s in range(1, E):
                rows_ = self.block(a, flip(b, db), lax.rem(e + E - s, E))
                self.arrived(self.z, db * (E - 1) + s - 1, self.buf.at[rows_])
                self.y_send(db, s)

        def y_arrive(self):
            for db in range(2):
                for s in range(E):
                    for t in range(1, A):
                        rows_ = self.block(
                            lax.rem(a + A - t, A), flip(b, db), lax.rem(e + E - s, E)
                        )
                        self.arrived(
                            self.y, (db * E + s) * (A - 1) + t - 1, self.buf.at[rows_]
                        )

        def add(self, landing, base, count):
            def load(k, cols, condition):
                copy = pltpu.make_async_copy(
                    landing.at[:, cols],
                    tm_ref.at[pl.ds(0, count), cols],
                    local_sem.at[SHARED + k],
                )
                when(condition, copy.start)

                def total():
                    copy.wait()

                    @pl.loop(0, count // 16)
                    def _(i):
                        here = pl.ds(pl.multiple_of(base + i * 16, 16), 16)
                        there = span(i * 16, 16)
                        self.buf[here, cols] = (
                            self.buf[here, cols].astype(F32) + tm_ref[there, cols].astype(F32)
                        ).astype(BF16)

                return lambda: when(condition, total)

            totals = []
            self.each(me, lambda *part: totals.append(load(*part)))
            for total in totals:
                total()

        def gy_send(self):
            for s in (*range(1, E), 0):
                for db in range(2):
                    for t in range(1, A):
                        to = lax.rem(a + t, A)
                        self.send(
                            self.gy,
                            (db * E + s) * (A - 1) + t - 1,
                            self.buf.at[self.block(to, flip(b, db), lax.rem(e + s, E))],
                            self.ylanding.at[t - 1, db, s],
                            {"a": to},
                        )

        def gy_add(self, db, s):
            bb, to = flip(b, db), lax.rem(e + s, E)
            for t in range(1, A):
                landing = self.ylanding.at[t - 1, db, s]
                self.arrived(self.gy, (db * E + s) * (A - 1) + t - 1, landing)
                self.add(landing, ((a * 2 + bb) * E + to) * 4 * self.R, 4 * self.R)
            if s:
                self.send(
                    self.gz,
                    db * (E - 1) + s - 1,
                    self.buf.at[self.block(a, bb, to)],
                    self.zlanding.at[s - 1, db],
                    {"e": to},
                )

        def gy_away(self, db):
            for s in range(1, E):
                self.gy_add(db, s)

        def home(self):
            for db in range(2):
                self.gy_add(db, 0)
            for db in range(2):
                self.gz_add(db)

        def gz_add(self, db):
            bb = flip(b, db)
            for s in range(1, E):
                landing = self.zlanding.at[s - 1, db]
                self.arrived(self.gz, db * (E - 1) + s - 1, landing)
                self.add(landing, ((a * 2 + bb) * E + e) * 4 * self.R, 4 * self.R)
            for r in range(4 * db, 4 * db + 4):
                _, df, dc = peers[r]
                ff, cc = flip(f, df), flip(c, dc)
                rows_ = self.buf.at[self.line(a, bb, e, ff, cc)]
                if r == 0:
                    pltpu.make_async_copy(rows_, self.out(me), local_sem.at[self.index]).start()
                else:
                    self.send(self.gtp, r, rows_, self.out(me), {"b": bb, "f": ff, "c": cc})

        def g_end(self):
            for r in range(GROUP):
                db, df, dc = peers[r]
                if r == 0:
                    pltpu.make_async_copy(
                        self.buf.at[self.line(a, b, e, f, c)],
                        self.out(me),
                        local_sem.at[self.index],
                    ).wait()
                else:
                    place = slot(flip(b, db), flip(f, df), flip(c, dc))
                    self.arrived(self.gtp, r, self.out(place), place)

    tile = uc - LANES
    shares = [(0, tile, False), (tile, LANES, True)]

    def quarter(ref, down, right):
        return lambda place: ref.at[
            span((down * GROUP + place) * R, R), pl.ds(right * uc, uc)
        ]

    def weight(index, parts, down, right, *rest):
        buf, ylanding, zlanding = rest
        piece, out = quarter(du_ref, down, right), quarter(hg_ref, down, right)
        return Weight(index, R, parts, piece, buf, out, ylanding, zlanding)

    s_w = Weight(
        0,
        16,
        [(0, LANES, False)],
        lambda place: sp_ref,
        ws_ref,
        lambda place: os_ref.at[place],
        ys_ref,
        zs_ref,
    )
    q_w = weight(1, [(0, qc, False)], 0, 0, wq_ref, yq_ref, zq_ref)
    g_w = weight(2, shares, 0, 1, wg_ref, yg_ref, zg_ref)
    u_w = weight(3, shares, 1, 0, wu_ref, yu_ref, zu_ref)
    o_w = weight(4, shares, 1, 1, wo_ref, yo_ref, zo_ref)

    hidden = fo_ref.shape[1]
    tiles = -(-hidden // LANES)
    tile_lane = lax.broadcasted_iota(jnp.int32, (R, LANES), 1)

    def lanes_of(ref, start, valid=LANES):
        def aligned(m):
            width_ = min(LANES, ref.shape[1] - m * LANES)
            part = ref[:, m * LANES : m * LANES + max(width_, 0)].astype(F32) if width_ > 0 else None
            if width_ >= LANES:
                return part
            if part is None:
                return jnp.zeros((R, LANES), F32)
            return jnp.concatenate([part, jnp.zeros((R, LANES - width_), F32)], axis=1)

        base, off = divmod(start, LANES)
        value = aligned(base)
        if off:
            back = LANES - off
            value = jnp.where(
                tile_lane < back,
                pltpu.roll(value, back, axis=1),
                pltpu.roll(aligned(base + 1), back, axis=1),
            )
        return jnp.where(tile_lane < valid, value, 0.0) if valid < LANES else value

    def member_tiles():
        for place in range(GROUP):
            first = place * (uc // LANES - 1) + min(place, larger)
            for k in range(uc // LANES - (place >= larger)):
                yield place, k, first + k

    def cut(ref, start, down, right):
        for place, k, number in member_tiles():
            at = (down * GROUP + place) * R, right * uc + k * LANES
            du_ref[at[0] : at[0] + R, at[1] : at[1] + LANES] = lanes_of(
                ref, start + number * LANES, min(LANES, hidden - number * LANES)
            ).astype(BF16)
        for place in range(larger, GROUP):
            at = (down * GROUP + place) * R, (right + 1) * uc - LANES
            du_ref[at[0] : at[0] + R, at[1] : at[1] + LANES] = jnp.zeros((R, LANES), BF16)

    def home_tiles(down, right):
        found = {}
        for place, k, number in member_tiles():
            at = (down * GROUP + place) * R, right * uc + k * LANES
            found[number] = at
        return lambda number: hg_ref[
            found[number][0] : found[number][0] + R, found[number][1] : found[number][1] + LANES
        ].astype(F32)

    def join(ref, groups):
        total = hidden * len(groups)
        for number in range(-(-total // LANES)):
            value = None
            for k, tile_of in enumerate(groups):
                shift = k * hidden % LANES
                first = number - k * hidden // LANES
                for piece in (first, first - 1) if shift else (first,):
                    if not 0 <= piece < tiles:
                        continue
                    start = k * hidden + piece * LANES - number * LANES
                    end = min(start + LANES, (k + 1) * hidden - number * LANES)
                    if start >= LANES or end <= 0:
                        continue
                    part = tile_of(piece)
                    if shift:
                        part = pltpu.roll(part, shift, axis=1)
                    if value is None:
                        value = part
                    else:
                        value = jnp.where((tile_lane >= start) & (tile_lane < end), part, value)
            size = min(LANES, total - number * LANES)
            ref[:, number * LANES : number * LANES + size] = value[:, :size].astype(BF16)

    def qkv_places():
        for place in range(GROUP):
            cc, bb, ff = place // 4, place // 2 % 2, place % 2
            for t in range(3):
                for i in range(sw // LANES):
                    number = i * 8 + bb * 4 + cc * 2 + ff
                    yield place * R, t * sw + i * LANES, t * width + number * LANES

    def cut_qkv():
        for row, col, start in qkv_places():
            du_ref[row : row + R, col : col + LANES] = fq_ref[:, start : start + LANES]

    def join_qkv():
        for row, col, start in qkv_places():
            fq_ref[:, start : start + LANES] = hg_ref[row : row + R, col : col + LANES]

    def remote(source, landing, send, recv, target):
        return pltpu.make_async_remote_copy(
            src_ref=source,
            dst_ref=landing,
            send_sem=send_sem.at[send],
            recv_sem=recv_sem.at[recv],
            device_id=target,
            device_id_type=DEVICE_MESH,
        )

    class Dense:
        def __init__(self):
            self.pieces = wd_ref.shape[0] // R
            self.first = wires.take(self.pieces)
            self.push = wires.out()
            self.zs = wires.out(self.pieces * (E - 1))
            self.ys = wires.out(self.pieces * (A - 1))
            self.gy = wires.take(self.pieces * (A - 1))
            self.gz = wires.take(self.pieces * (E - 1))
            self.back = wires.take(1)
            self.back_sends = wires.out(self.pieces)
            self.gys, self.gzs = wires.out(self.pieces * (A - 1)), wires.out(self.pieces * (E - 1))
            self.owners = []
            for piece in range(self.pieces):
                i, offset = piece * R // LANES, piece * R % LANES
                owner = ((i * 8 + b * 4 + c * 2 + f) * LANES + offset) // R
                self.owners.append(
                    {
                        "a": owner // (8 * E),
                        "b": lax.rem(owner // (4 * E), 2),
                        "e": lax.rem(owner // 4, E),
                        "f": lax.rem(owner // 2, 2),
                        "c": lax.rem(owner, 2),
                    }
                )

        def rows(self, piece):
            return wd_ref.at[pl.ds(piece * R, R)]

        def each(self, test, body):
            for piece, owner in enumerate(self.owners):
                same_a, same_e = owner["a"] == a, owner["e"] == e

                @pl.when(test(same_a, same_e))
                def _():
                    body(piece, owner)

        def local_or_remote(self, target, source, landing, send, recv, start):
            here = target["b"] == b
            for axis, mine in (("f", f), ("c", c)):
                here = here & (target[axis] == mine)
            away = remote(source, landing, send, recv, target)

            @pl.when(here)
            def _():
                if start:
                    pltpu.make_async_copy(source, landing, recv_sem.at[recv]).start()

            @pl.when(jnp.logical_not(here))
            def _():
                away.start() if start else away.wait_send()

        def out(self, start):
            first_row = rank(a, b, e, f, c) * R
            head = first_row // LANES
            piece = (head // 8) * (LANES // R) + lax.rem(first_row, LANES) // R
            target = {
                "b": lax.rem(head // 4, 2),
                "f": lax.rem(head, 2),
                "c": lax.rem(head // 2, 2),
            }
            landing = wd_ref.at[span(piece * R, R)]
            self.local_or_remote(target, dp_ref, landing, self.push, self.first + piece, start)

        def z(self, piece, s):
            rows_ = self.rows(piece)
            number = self.zs + piece * (E - 1) + s - 1
            return remote(rows_, rows_, number, self.first + piece, {"e": lax.rem(e + s, E)})

        def y(self, piece, t):
            rows_ = self.rows(piece)
            number = self.ys + piece * (A - 1) + t - 1
            return remote(rows_, rows_, number, self.first + piece, {"a": lax.rem(a + t, A)})

        def arrived(self, piece, _=None):
            wires.arrived(self.first + piece, self.rows(piece))

        def z_send(self):
            def body(piece, owner):
                self.arrived(piece)
                for s in range(1, E):
                    self.z(piece, s).start()

            self.each(lambda same_a, same_e: same_a & same_e, body)

        def y_send(self):
            self.each(lambda same_a, same_e: same_a & jnp.logical_not(same_e), self.arrived)

            def body(piece, owner):
                for t in range(1, A):
                    self.y(piece, t).start()

            self.each(lambda same_a, same_e: same_a, body)

        def y_arrive(self):
            self.each(lambda same_a, same_e: jnp.logical_not(same_a), self.arrived)

        def sent(self):
            self.out(False)

            def over_z(piece, owner):
                for s in range(1, E):
                    self.z(piece, s).wait_send()

            def over_y(piece, owner):
                for t in range(1, A):
                    self.y(piece, t).wait_send()

            self.each(lambda same_a, same_e: same_a & same_e, over_z)
            self.each(lambda same_a, same_e: same_a, over_y)

        def g_y(self, piece, t):
            to = lax.rem(a + t, A)
            number = piece * (A - 1) + t - 1
            landing = yd_ref.at[t - 1, piece]
            copy = remote(
                self.rows(piece), landing, self.gys + number, self.gy + number, {"a": to}
            )
            return to, copy

        def gy_send(self, start=True):
            for piece, owner in enumerate(self.owners):
                for t in range(1, A):
                    to, copy = self.g_y(piece, t)

                    @pl.when(owner["a"] == to)
                    def _():
                        copy.start() if start else copy.wait_send()

        def add(self, landing, piece):
            load = pltpu.make_async_copy(landing, td_ref, local_sem.at[SHARED])
            load.start()
            load.wait()

            @pl.loop(0, R // 16)
            def _(i):
                here, there = span(piece * R + i * 16, 16), span(i * 16, 16)
                wd_ref[here, :] = (
                    wd_ref[here, :].astype(F32) + td_ref[there, :].astype(F32)
                ).astype(BF16)

        def g_z(self, piece, s):
            to = lax.rem(e + s, E)
            number = piece * (E - 1) + s - 1
            landing = zd_ref.at[s - 1, piece]
            copy = remote(
                self.rows(piece), landing, self.gzs + number, self.gz + number, {"e": to}
            )
            return to, copy

        def gz_send(self, start=True):
            for piece, owner in enumerate(self.owners):
                for s in range(1, E):
                    to, copy = self.g_z(piece, s)

                    @pl.when((owner["a"] == a) & (owner["e"] == to))
                    def _():
                        copy.start() if start else copy.wait_send()

        def gy_add(self):
            def body(piece, owner):
                for t in range(1, A):
                    landing = yd_ref.at[t - 1, piece]
                    wires.arrived(self.gy + piece * (A - 1) + t - 1, landing)
                    self.add(landing, piece)

            self.each(lambda same_a, same_e: same_a, body)
            self.gz_send()

        def home(self, piece, owner, start):
            target = {axis: owner[axis] for axis in ("b", "f", "c")}
            self.local_or_remote(
                target, self.rows(piece), od_ref, self.back_sends + piece, self.back, start
            )

        def gz_add(self):
            def body(piece, owner):
                for s in range(1, E):
                    landing = zd_ref.at[s - 1, piece]
                    wires.arrived(self.gz + piece * (E - 1) + s - 1, landing)
                    self.add(landing, piece)
                self.home(piece, owner, True)

            self.each(lambda same_a, same_e: same_a & same_e, body)

        def g_end(self):
            wires.arrived(self.back, od_ref)
            self.gy_send(False)
            self.gz_send(False)
            self.each(
                lambda same_a, same_e: same_a & same_e,
                lambda piece, owner: self.home(piece, owner, False),
            )

    dense = Dense()

    chain, chain_out = (wires.take(10), wires.take(10)), (wires.out(10), wires.out(10))
    to_b, to_f, to_c = {"b": 1 - b}, {"f": 1 - f}, {"c": 1 - c}
    nb, nf, dg = slot(1 - b, f, c), slot(b, 1 - f, c), slot(1 - b, 1 - f, c)

    class Gather:
        def __init__(self, buf, lean):
            self.buf, self.first, self.copies, self.lean = buf, chain[0], [], lean

        def part(self, place, which):
            if which is None:
                return self.buf.at[span(place * rows, rows)]
            return self.buf.at[span(place * rows + which * (rows // 2), rows // 2)]

        def copy(self, number, place, which, device):
            here = self.part(place, which)
            self.copies.append(
                wires.send(chain_out[0] + number, self.first + number, here, here, device)
            )

        def landed(self, number, place, which):
            wires.arrived(self.first + number, self.part(place, which))

        def start(self):
            self.copy(0, me, 0, to_b)
            self.copy(1, me, 1, to_f)
            self.copy(2, me, 1, to_b)
            self.copy(3, me, 0, to_f)
            self.copy(4, me, None, to_c)

        def relay(self):
            if self.lean:
                self.landed(1, nf, 1)
                self.copy(6, nf, 1, to_b)
                self.landed(3, nf, 0)
                self.copy(5, nf, 0, to_b)
                self.copy(8, nf, None, to_c)
                self.landed(0, nb, 0)
                self.landed(2, nb, 1)
                self.copy(7, nb, None, to_c)
                return
            self.landed(0, nb, 0)
            self.copy(5, nb, 0, to_f)
            self.landed(1, nf, 1)
            self.copy(6, nf, 1, to_b)
            self.landed(2, nb, 1)
            self.copy(7, nb, None, to_c)
            self.landed(3, nf, 0)
            self.copy(8, nf, None, to_c)

        def finish(self):
            self.landed(5, dg, 0)
            self.landed(6, dg, 1)
            self.copy(9, dg, None, to_c)
            other = 1 - c
            self.landed(4, slot(b, f, other), None)
            self.landed(7, slot(1 - b, f, other), None)
            self.landed(8, slot(b, 1 - f, other), None)
            self.landed(9, slot(1 - b, 1 - f, other), None)

    step = 16
    places = [(1 - b, 1 - f), (1 - b, f), (b, 1 - f), (b, f)]

    def accumulate(target, at, count, terms):
        @pl.loop(0, count // step)
        def _(i):
            window = pl.ds(pl.multiple_of(at + i * step, step), step)
            total = terms[0][window, :].astype(F32)
            for term in terms[1:]:
                total = total + term[window, :].astype(F32)
            target[window, :] = total.astype(target.dtype)

    def scatter(multiply, lean, early=None, late=None):
        first, copies = chain[1], []

        def send(number, *copy):
            copies.append(wires.send(chain_out[1] + number - first, number, *copy))

        multiply((1 - c) * half_rows, half_rows)
        for k, (bb, ff) in enumerate(places):
            send(
                first + k,
                pb_ref.at[span(slot(bb, ff, 1 - c) * rows, rows)],
                core_ref.at[pl.ds(k * rows, rows)],
                to_c,
            )
        multiply(c * half_rows, half_rows)
        own = [pb_ref.at[span(slot(bb, ff, c) * rows, rows)] for bb, ff in places]
        core = [core_ref.at[pl.ds(k * rows, rows)] for k in range(4)]
        mid = rows // 2
        low, high = pl.ds(0, mid), pl.ds(mid, mid)
        early, late = (hook or (lambda: None) for hook in (early, late))
        wires.arrived(first, core[0])
        accumulate(stage_ref.at[0], 0, rows, [own[0], core[0]])
        if lean:
            send(first + 4, stage_ref.at[0], relay_ref, to_b)
            wires.arrived(first + 1, core[1])
            accumulate(stage_ref.at[1], 0, rows, [own[1], core[1]])
            send(first + 6, stage_ref.at[1], land_ref.at[0], to_b)
            early()
            wires.arrived(first + 2, core[2])
            wires.arrived(first + 4, relay_ref)
            accumulate(stage_ref.at[2], 0, rows, [own[2], core[2], relay_ref])
            send(first + 7, stage_ref.at[2], land_ref.at[1], to_f)
            late()
            wires.arrived(first + 3, core[3])
            wires.arrived(first + 6, land_ref.at[0])
            wires.arrived(first + 7, land_ref.at[1])
        else:
            send(first + 4, stage_ref.at[0, low], relay_ref.at[low], to_b)
            send(first + 5, stage_ref.at[0, high], relay_ref.at[high], to_f)
            wires.arrived(first + 1, core[1])
            accumulate(stage_ref.at[1], 0, mid, [own[1], core[1]])
            send(first + 6, stage_ref.at[1, low], land_ref.at[0, low], to_b)
            wires.arrived(first + 2, core[2])
            accumulate(stage_ref.at[2], mid, mid, [own[2], core[2]])
            send(first + 7, stage_ref.at[2, high], land_ref.at[1, high], to_f)
            early()
            wires.arrived(first + 5, relay_ref.at[high])
            accumulate(stage_ref.at[1], mid, mid, [own[1], core[1], relay_ref])
            send(first + 8, stage_ref.at[1, high], land_ref.at[0, high], to_b)
            wires.arrived(first + 4, relay_ref.at[low])
            accumulate(stage_ref.at[2], 0, mid, [own[2], core[2], relay_ref])
            send(first + 9, stage_ref.at[2, low], land_ref.at[1, low], to_f)
            late()
            wires.arrived(first + 3, core[3])
            wires.arrived(first + 6, land_ref.at[0, low])
            wires.arrived(first + 7, land_ref.at[1, high])
            wires.arrived(first + 8, land_ref.at[0, high])
            wires.arrived(first + 9, land_ref.at[1, low])
        accumulate(sum_ref, 0, rows, [own[3], core[3], land_ref.at[0], land_ref.at[1]])
        sent(copies)

    def blocks(count_m, count_n, body):
        @pl.loop(0, count_m * count_n)
        def _(k):
            body(k // count_n, lax.rem(k, count_n))

    def onto_partial(*terms):
        def multiply(first, count):
            def body(m, n):
                here = pl.ds(pl.multiple_of(first, half_rows) + m * 512, 512)
                there = span(n * 512, 512)
                total = sum(dot(left[here, :], weight[there, :], NT) for left, weight in terms)
                pb_ref[here, there] = total.astype(BF16)

            blocks(count // 512, width // 512, body)

        return multiply

    loads[0].wait()
    cut_qkv()
    q_w.tp_send()
    s_w.tp_send()
    dense.out(True)
    own_x = pltpu.make_async_copy(
        x_ref.at[0], xg_ref.at[my_rows, pl.ds(0, width)], local_sem.at[5]
    )
    own_x.start()
    sg_ref[...] = jnp.zeros_like(sg_ref)

    @pl.when(me >= larger)
    def _():
        for weight in (g_w, u_w, o_w):
            weight.buf[:, tile:] = jnp.zeros((width, LANES), BF16)

    at = lax.broadcasted_iota(jnp.int32, (rows, LANES), 0)
    lane = lax.broadcasted_iota(jnp.int32, (rows, LANES), 1)
    docs = len_ref.shape[1]
    key, prefix_at, local_pos, valid, first = at + docs, at * 0, at * 0, at < 0, 0
    for k in range(docs):
        last = first + len_ref[0, k]
        member = (at >= first) & (at < last)
        key = jnp.where(member, k, key)
        prefix_at = jnp.where(member, pre_ref[0, k], prefix_at)
        local_pos = jnp.where(member, at - first, local_pos)
        valid = valid | member
        first = last
    info = jnp.where(lane == 0, key, jnp.where(lane == 1, prefix_at, local_pos))
    xg_ref[my_rows, width:] = info.astype(F32).astype(BF16)
    valid_ref[...] = jnp.where(valid, 1.0, 0.0)

    loads[1].wait()
    cut(fi_ref, 0, 0, 1)
    tokens = Gather(xg_ref, True)
    for db in range(2):
        q_w.tp_wait(db)
        q_w.z_send(db)
        q_w.y_send(db, 0)
    own_x.wait()
    tokens.start()
    g_w.tp_send()
    cut(fi_ref, hidden, 1, 0)
    loads[2].wait()
    cut(fo_ref, 0, 1, 1)
    for db in range(2):
        s_w.tp_wait(db)
        s_w.z_send(db)
        s_w.y_send(db, 0)
    dense.z_send()
    u_w.tp_send()
    q_w.z_arrive(0)
    tokens.relay()
    g_w.tp_wait(0)
    g_w.z_send(0)
    g_w.y_send(0, 0)
    q_w.z_arrive(1)
    s_w.z_arrive(0)
    s_w.z_arrive(1)
    dense.y_send()
    g_w.tp_wait(1)
    g_w.z_send(1)
    g_w.y_send(1, 0)
    tokens.finish()
    o_w.tp_send()
    for db in range(2):
        u_w.tp_wait(db)
        u_w.y_send(db, 0)
    s_w.y_arrive()
    q_w.y_arrive()

    lane = lane[0:16, :]

    @pl.loop(0, width // LANES)
    def _(k):
        line = jnp.zeros((16, LANES), F32)
        for j in range(LANES // R):
            part = ws_ref[span((k * (LANES // R) + j) * 16, 16), :].astype(F32)
            if j:
                part = pltpu.roll(part, j * R, axis=1)
            line = jnp.where(lane // R == j, part, line)
        bt_ref[:, span(k * LANES, LANES)] = line

    heads = [i * 8 + b * 4 + c * 2 + f for i in range(sw // LANES)]
    for t in range(3):
        for i, number in enumerate(heads):
            at = t * sw + i * LANES
            qb_ref[0:1, at : at + LANES] = bt_ref[t : t + 1, span(number * LANES, LANES)]

    def projection(m, n):
        here, cols = span(m * 512, 512), span(n * sw, sw)
        uf_ref[here, cols] = (
            dot(xg_ref[here, 0:width], wq_ref[:, cols]) + qb_ref[0:1, cols]
        )

    blocks(all_rows // 512, 3, projection)

    loads[3].wait()
    row_at = lax.broadcasted_iota(jnp.int32, (rows, rows), 0)
    col_at = lax.broadcasted_iota(jnp.int32, (rows, rows), 1)

    def sequence(s):
        here = span(s * rows, rows)
        info = xg_ref[here, width : width + LANES].astype(F32)
        turned = info.T
        allowed = (info[:, 0:1] == turned[0:1, :]) & (
            (turned[2:3, :] < info[:, 1:2]) | (col_at <= row_at)
        )
        picked = (info[:, 2:3] == col_at.astype(F32)).astype(BF16)
        parts = dot(picked, table_ref[...])
        cos_sin = parts[:, 0:LANES] + parts[:, LANES : 2 * LANES] + parts[:, 2 * LANES :]
        swapped = pltpu.roll(cos_sin, LANES // 2, axis=1)
        first = col_at < LANES // 2
        cosine = jnp.where(first, cos_sin, swapped)
        sine = jnp.where(first, -swapped, cos_sin)
        return here, allowed, cosine, sine

    def turn(value, cosine, sine):
        return value * cosine + pltpu.roll(value, LANES // 2, axis=1) * sine

    def softmax(q, k, allowed):
        scores = jnp.where(allowed, scale * dot(q, k, NT), MASKED_SCORE)
        power = jnp.exp(scores - jnp.max(scores, axis=1, keepdims=True))
        return power / jnp.sum(power, axis=1, keepdims=True)

    @pl.loop(0, GROUP)
    def _(s):
        here, allowed, cosine, sine = sequence(s)
        for i in range(sw // LANES):
            cols = [pl.ds(t * sw + i * LANES, LANES) for t in range(3)]
            q = turn(uf_ref[here, cols[0]], cosine, sine).astype(BF16)
            k = turn(uf_ref[here, cols[1]], cosine, sine).astype(BF16)
            v = uf_ref[here, cols[2]].astype(BF16)
            qk_ref[here, cols[0]] = q
            qk_ref[here, cols[1]] = k
            qk_ref[here, cols[2]] = v
            probs = softmax(q, k, allowed).astype(BF16)
            cx_ref[here, i * LANES : (i + 1) * LANES] = dot(probs, v).astype(BF16)

    u_w.z_send(0)
    g_w.z_arrive(0)
    dense.y_arrive()

    def dense_partial(first, count):
        def body(m, n):
            here = pl.ds(pl.multiple_of(first, half_rows) + m * 512, 512)
            cols = span(n * 512, 512)
            pb_ref[here, cols] = dot(cx_ref[here, :], wd_ref[:, cols]).astype(BF16)

        blocks(count // 512, width // 512, body)

    def more_units():
        u_w.z_send(1)
        for db in range(2):
            o_w.tp_wait(db)
            o_w.y_send(db, 0)

    scatter(dense_partial, True, lambda: g_w.z_arrive(1), more_units)

    def row_loop(body):
        @pl.loop(0, rows // 16)
        def _(i):
            body(span(i * 16, 16), span(me * rows + i * 16, 16))

    def normalize(value):
        centered = value - jnp.mean(value, axis=1, keepdims=True)
        rstd = lax.rsqrt(jnp.mean(centered * centered, axis=1, keepdims=True) + EPSILON)
        return centered * rstd, rstd

    def first_norm(here, there):
        value = (
            alpha * xg_ref[there, 0:width].astype(F32) + sum_ref[here, :] + bt_ref[3:4, :]
        )
        unit, rstd = normalize(value)
        xh_ref[here, :] = unit
        rstd_ref[here, :] = jnp.broadcast_to(rstd, (16, LANES))
        hg_ref[there, :] = (unit * bt_ref[7:8, :] + bt_ref[4:5, :]).astype(BF16)

    row_loop(first_norm)
    normed = Gather(hg_ref, True)
    sent(tokens.copies)
    o_w.z_send(0)
    normed.start()
    o_w.z_send(1)
    u_w.z_arrive(0)
    normed.relay()
    u_w.z_arrive(1)
    normed.finish()
    o_w.z_arrive(0)
    g_w.y_arrive()
    u_w.y_arrive()

    def units(m, n):
        here = pl.ds(m * 512, 512)
        gate_cols = span(n * 256, 256)
        up_cols = span(uc + n * 256, 256)
        left = hg_ref[here, :]
        gate = dot(left, wg_ref[:, gate_cols])
        up = dot(left, wu_ref[:, gate_cols])
        cdf = 0.5 * (1.0 + lax.erf(gate * (0.5**0.5)))
        density = jnp.exp(-0.5 * gate * gate) * (1.0 / math.sqrt(2.0 * math.pi))
        act = gate * cdf
        mb_ref[here, gate_cols] = (act * up).astype(BF16)
        uf_ref[here, gate_cols] = (cdf + gate * density) * up
        uf_ref[here, up_cols] = act

    for m in range(all_rows // 512):
        blocks(1, uc // 256, lambda _, n: units(m, n))
        if m == 0:
            o_w.z_arrive(1)
    o_w.y_arrive()
    scatter(onto_partial((mb_ref, wo_ref)), False)

    def add_row(row, value):
        sg_ref[row : row + 1, :] += jnp.sum(value, axis=0, keepdims=True)

    def norm_back(grad, gain, unit, rstd):
        scaled = grad * gain
        return rstd * (
            scaled
            - jnp.mean(scaled, axis=1, keepdims=True)
            - unit * jnp.mean(scaled * unit, axis=1, keepdims=True)
        )

    def second_norm(here, there):
        normed_one = xh_ref[here, :] * bt_ref[7:8, :] + bt_ref[4:5, :]
        unit, rstd = normalize(alpha * normed_one + sum_ref[here, :] + bt_ref[5:6, :])
        out_ref[here, :] = (unit * bt_ref[8:9, :] + bt_ref[6:7, :]).astype(BF16)
        grad = cot_ref[here, :].astype(F32) * valid_ref[here, 0:1]
        back = norm_back(grad, bt_ref[8:9, :], unit, rstd)
        low = back.astype(BF16)
        dr_ref[here, :] = back
        dg_ref[there, :] = low
        add_row(5, low.astype(F32))
        add_row(6, grad)
        add_row(8, grad * unit)

    loads[4].wait()
    row_loop(second_norm)
    results[0].start()
    branch = Gather(dg_ref, False)
    sent(normed.copies)
    branch.start()
    branch.relay()
    branch.finish()

    def units_back(m, n):
        here = span(m * 512, 512)
        gate_cols, up_cols = span(n * 256, 256), span(uc + n * 256, 256)
        grad = dot(dg_ref[here, :], wo_ref[:, gate_cols])
        du_ref[here, gate_cols] = (uf_ref[here, gate_cols] * grad).astype(BF16)
        du_ref[here, up_cols] = (uf_ref[here, up_cols] * grad).astype(BF16)

    def weight_grad(left, right, target, cols, bn):
        def body(m, n):
            here, there = span(m * 512, 512), span(n * bn, bn)
            target[here, there] = dot(left[:, here], right[:, there], TN).astype(BF16)

        blocks(width // 512, cols // bn, body)

    for flow in (q_w, g_w, u_w, o_w):
        flow.sent()
    weight_grad(dg_ref, mb_ref, go_ref, uc, uc)
    o_w.buf = go_ref
    o_w.gy_send()
    blocks(all_rows // 512, uc // 256, units_back)

    du_gate = du_ref.at[:, pl.ds(0, uc)]
    du_up = du_ref.at[:, pl.ds(uc, uc)]

    def in_grad():
        for weight, right in ((g_w, du_gate), (u_w, du_up)):
            weight_grad(hg_ref, right, weight.buf, uc, uc)
            weight.gy_send()
            if weight is g_w:
                o_w.gy_away(0)

    sent(branch.copies)
    scatter(
        onto_partial((du_gate, wg_ref), (du_up, wu_ref)), False, in_grad, lambda: o_w.gy_away(1)
    )

    def first_norm_back(here, there):
        grad = alpha * dr_ref[here, :] + sum_ref[here, :]
        unit = xh_ref[here, :]
        back = norm_back(grad, bt_ref[7:8, :], unit, rstd_ref[here, 0:1])
        low = back.astype(BF16)
        dr_ref[here, :] = back
        dg_ref[there, :] = low
        add_row(3, low.astype(F32))
        add_row(4, grad)
        add_row(7, grad * unit)

    row_loop(first_norm_back)
    attended = Gather(dg_ref, False)
    attended.start()
    g_w.gy_away(0)
    attended.relay()
    g_w.gy_away(1)
    attended.finish()

    def context_back(m, n):
        here = span(m * 512, 512)
        dc_ref[here, :] = dot(dg_ref[here, :], wd_ref[...], NT).astype(BF16)

    blocks(all_rows // 512, 1, context_back)

    def dense_grad(m, n):
        cols = span(n * 512, 512)
        wd_ref[:, cols] = dot(cx_ref[...], dg_ref[:, cols], TN).astype(BF16)

    dense.sent()
    blocks(1, width // 512, dense_grad)
    dense.gy_send()
    u_w.gy_away(0)
    o_w.home()

    @pl.loop(0, GROUP)
    def _(s):
        here, allowed, cosine, sine = sequence(s)
        for i, number in enumerate(heads):
            cols = [pl.ds(t * sw + i * LANES, LANES) for t in range(3)]
            q, k, v = (qk_ref[here, one] for one in cols)
            grad = dc_ref[here, i * LANES : (i + 1) * LANES]
            probs = softmax(q, k, allowed)
            d_probs = dot(grad, v, NT)
            d_value = dot(probs.astype(BF16), grad, TN)
            d_scores = probs * (d_probs - jnp.sum(probs * d_probs, axis=1, keepdims=True))
            low = jnp.where(allowed, d_scores, 0.0).astype(BF16)
            d_query = turn(scale * dot(low, k), cosine, -sine)
            d_key = turn(scale * dot(low, q, TN), cosine, -sine)
            for t, value in enumerate((d_query, d_key, d_value)):
                value = value.astype(BF16)
                mb_ref[here, cols[t]] = value
                lanes = span(number * LANES, LANES)
                sg_ref[t : t + 1, lanes] += jnp.sum(value.astype(F32), axis=0, keepdims=True)

    u_w.gy_away(1)

    def late_adds():
        q_w.gy_away(0)
        q_w.gy_away(1)
        g_w.home()

    def qkv_grad():
        weight_grad(xg_ref, mb_ref, wq_ref, qc, qc)

        s_w.sent()

        @pl.loop(0, width // LANES)
        def _(k):
            line = sg_ref[:, span(k * LANES, LANES)]
            for j in range(LANES // R):
                part = line if j == 0 else pltpu.roll(line, LANES - j * R, axis=1)
                ws_ref[span((k * (LANES // R) + j) * 16, 16), :] = part.astype(BF16)

        s_w.gy_send()
        q_w.gy_send()
        dense.gy_add()

    scatter(onto_partial((mb_ref, wq_ref)), True, qkv_grad, late_adds)

    def tokens_back(here, there):
        gx_ref[here, :] = alpha * dr_ref[here, :] + sum_ref[here, :]

    row_loop(tokens_back)
    results[1].start()

    for db in range(2):
        s_w.gy_away(db)
    u_w.home()
    for db in range(2):
        q_w.gy_add(db, 0)
        s_w.gy_add(db, 0)
    for db in range(2):
        q_w.gz_add(db)
    for db in range(2):
        s_w.gz_add(db)
    dense.gz_add()
    o_w.g_end()
    join(fo_ref, [home_tiles(1, 1)])
    results[2].start()
    g_w.g_end()
    u_w.g_end()
    join(fi_ref, [home_tiles(0, 1), home_tiles(1, 0)])
    results[3].start()
    q_w.g_end()
    join_qkv()
    results[4].start()
    s_w.g_end()
    small_ref[...] = sum(os_ref[place].astype(F32) for place in range(GROUP))
    dense.g_end()
    for result in results:
        result.wait()
    for flow in (q_w, g_w, u_w, o_w, s_w):
        flow.sent()
    sent(attended.copies)


def final_kernel(count, plain, *refs):
    small_ref, bias_ref, gain_ref = refs[0], refs[1 + count], refs[2 + count]
    refs = refs[1 : 1 + count] + refs[3 + count :]
    sources, targets, held = (refs[k * count : (k + 1) * count] for k in range(3))
    wide = refs[3 * count : -2]
    load_sem, store_sem = refs[-2:]
    loads = [
        pltpu.make_async_copy(source, one, load_sem.at[k])
        for k, (source, one) in enumerate(zip(sources, held))
    ]
    for one in loads:
        one.start()
    cut, own = bias_ref.shape
    bias_ref[...] = small_ref[0:cut, 0:own]
    gain_ref[...] = small_ref[cut : cut + gain_ref.shape[0], 0:own]
    stores = []
    for k, load in enumerate(loads):
        load.wait()
        found = held[k]
        if k >= plain:
            found = wide[k - plain]
            found[...] = held[k][...].astype(F32)
        stores.append(pltpu.make_async_copy(found, targets[k], store_sem.at[k]))
        stores[-1].start()
    for one in stores:
        one.wait()


def finish(small, cuts, plain, narrow):
    shape, anywhere = jax.ShapeDtypeStruct, pl.BlockSpec(memory_space=pl.ANY)
    vmem = pl.BlockSpec(memory_space=pltpu.VMEM)
    arrays = [*plain, *narrow]
    count = len(arrays)
    return pl.pallas_call(
        functools.partial(final_kernel, count, len(plain)),
        out_shape=[shape(cut, F32) for cut in cuts]
        + [shape(one.shape, one.dtype) for one in plain]
        + [shape(one.shape, F32) for one in narrow],
        in_specs=[vmem] + [anywhere] * count,
        out_specs=[vmem] * 2 + [anywhere] * count,
        scratch_shapes=[pltpu.VMEM(one.shape, one.dtype) for one in arrays]
        + [pltpu.VMEM(one.shape, F32) for one in narrow]
        + [pltpu.SemaphoreType.DMA((count,)), pltpu.SemaphoreType.DMA((count,))],
        compiler_params=pltpu.CompilerParams(vmem_limit_bytes=63 << 20),
    )(small, *arrays)


def on_device(
    tokens,
    cotangent,
    lengths,
    prefix,
    qkv_weight,
    dense_weight,
    ffin_weight,
    ffout_weight,
    biases,
    norm_gains,
):
    _, rows, width = tokens.shape
    A, E = lax.axis_size("a"), lax.axis_size("e")
    R = qkv_weight.shape[0]
    head_dim = width // HEADS
    my_heads = HEADS // GROUP
    hidden = ffout_weight.shape[1]
    sw = my_heads * head_dim
    qc = 3 * sw

    inverse = np.float32(ROPE_BASE) ** (
        -np.arange(head_dim // 2, dtype=np.float32) * np.float32(2.0 / head_dim)
    )
    angles = np.arange(rows, dtype=np.float32)[:, None] * inverse.astype(np.float32)
    rest = np.concatenate([np.cos(angles), np.sin(angles)], axis=1).astype(np.float32)
    terms = []
    for _ in range(3):
        terms.append(rest.astype(BF16))
        rest = rest - terms[-1].astype(np.float32)
    table = jnp.asarray(np.concatenate(terms, axis=1))

    small = jnp.concatenate([biases, norm_gains], axis=1).T
    small = jnp.pad(small, ((0, 16 - small.shape[0]), (0, LANES - R)))

    tiles = -(-hidden // LANES)
    larger = tiles % GROUP
    uc = (tiles // GROUP + 1) * LANES
    wires = 8 * (2 * GROUP + 4 * (E - 1) + 4 * E * (A - 1))
    outs = 3 * (2 * GROUP + 4 * (E - 1) + 4 * E * (A - 1)) + 10
    outs += (sw // R) * 2 * (A + E) + 2 + 2 * 10
    wires += (sw // R) * 2 * (A + E) + 2 + 2 * 10
    group_rows = GROUP * rows
    sizes = (A, E, R, rows, width, sw, uc, larger, (2.0 * LAYERS) ** 0.5, head_dim ** (-0.5))
    shape = jax.ShapeDtypeStruct
    anywhere, vmem = pl.BlockSpec(memory_space=pl.ANY), pl.BlockSpec(memory_space=pltpu.VMEM)
    landings = [(64, LANES), (4 * R, qc), None] + [(4 * R, uc)] * 3
    dense_landing = (sw // R, R, width)
    results = pl.pallas_call(
        functools.partial(layer_kernel, sizes),
        out_shape=[
            shape((16, LANES), F32),
            shape((rows, width), BF16),
            shape((rows, width), F32),
            shape((R, 3 * width), BF16),
            shape((R, 2 * hidden), BF16),
            shape((R, hidden), BF16),
            shape((R, width), BF16),
        ]
        + [
            shape((A - 1,) + ((2, E) + one if one else dense_landing), BF16)
            for one in landings
        ]
        + [
            shape((E - 1,) + ((2,) + one if one else dense_landing), BF16)
            for one in landings
        ],
        in_specs=[pl.BlockSpec(memory_space=pltpu.SMEM)] * 2 + [anywhere] * 8,
        out_specs=[vmem] + [anywhere] * 18,
        scratch_shapes=[
            pltpu.VMEM((rows, width), BF16),
            pltpu.VMEM((rows, width), F32),
            pltpu.VMEM((R, 3 * width), BF16),
            pltpu.VMEM((R, 2 * hidden), BF16),
            pltpu.VMEM((R, hidden), BF16),
            pltpu.VMEM((rows, width), BF16),
            pltpu.VMEM((rows, 3 * LANES), BF16),
            pltpu.VMEM((GROUP, 16, LANES), BF16),
            pltpu.VMEM((width // R * 16, LANES), BF16),
            pltpu.VMEM((width, qc), BF16),
            pltpu.VMEM((sw, width), BF16),
            pltpu.VMEM((width, uc), BF16),
            pltpu.VMEM((width, uc), BF16),
            pltpu.VMEM((width, uc), BF16),
            pltpu.VMEM((width, uc), BF16),
            pltpu.VMEM((group_rows, width + LANES), BF16),
            pltpu.VMEM((group_rows, width), BF16),
            pltpu.VMEM((group_rows, width), BF16),
            pltpu.VMEM((group_rows, 2 * uc), F32),
            pltpu.VMEM((group_rows, uc), BF16),
            pltpu.VMEM((group_rows, 2 * uc), BF16),
            pltpu.VMEM((group_rows, qc), BF16),
            pltpu.VMEM((group_rows, sw), BF16),
            pltpu.VMEM((group_rows, sw), BF16),
            pltpu.VMEM((group_rows, width), BF16),
            pltpu.VMEM((4 * rows, width), BF16),
            pltpu.VMEM((3, rows, width), BF16),
            pltpu.VMEM((rows, width), BF16),
            pltpu.VMEM((2, rows, width), BF16),
            pltpu.VMEM((rows, width), F32),
            pltpu.VMEM((rows, width), F32),
            pltpu.VMEM((rows, width), F32),
            pltpu.VMEM((rows, LANES), F32),
            pltpu.VMEM((rows, LANES), F32),
            pltpu.VMEM((16, width), F32),
            pltpu.VMEM((16, width), F32),
            pltpu.VMEM((8, qc), F32),
            pltpu.VMEM((4 * R, max(uc, qc)), BF16),
            pltpu.VMEM((R, width), BF16),
            pltpu.SemaphoreType.DMA((SHARED + 12,)),
            pltpu.SemaphoreType.DMA((outs,)),
            pltpu.SemaphoreType.DMA((wires,)),
        ],
        compiler_params=pltpu.CompilerParams(
            collective_id=0, has_side_effects=True, vmem_limit_bytes=63 << 20
        ),
    )(
        lengths,
        prefix,
        cotangent,
        table,
        small,
        tokens,
        qkv_weight,
        dense_weight,
        ffin_weight,
        ffout_weight,
    )
    small_grads, result, d_tokens, qkv_grad, ffin_grad, ffout_grad, dense_grad = results[:7]
    bias_grad, gain_grad, result, d_tokens, ffin_grad, qkv_grad, ffout_grad, dense_grad = finish(
        small_grads,
        (biases.shape[::-1], norm_gains.shape[::-1]),
        [result, d_tokens],
        [ffin_grad, qkv_grad, ffout_grad, dense_grad],
    )
    return (
        result.reshape(tokens.shape),
        d_tokens.reshape(tokens.shape),
        qkv_grad,
        dense_grad,
        ffin_grad,
        ffout_grad,
        bias_grad.T,
        gain_grad.T,
    )


def solution(mesh):
    dp, fsdp = mesh.shape["dp"], mesh.shape["fsdp"]
    fine = Mesh(mesh.devices.reshape(dp // 2, 2, fsdp // 4, 2, 2), AXES)
    cube, flat = P(AXES, None, None), P(AXES, None)
    return jax.shard_map(
        on_device,
        mesh=fine,
        in_specs=(cube, cube) + (flat,) * 8,
        out_specs=(cube, cube) + (flat,) * 6,
        check_vma=False,
    )
```
